32 devices in a mesh: expert: 8 (over z, x), tensor: 4 (over y, core).
Axes of the slice: x: 2, y: 2, z: 4, core: 2. Of those that a mesh axis runs over, the one named last changes fastest.
Arguments:
- tokens: bfloat16 [4096, 768], P('expert'), may hold values from -6 to 6
- cotangent: bfloat16 [4096, 768], P('expert', 'tensor'), may hold values from -6 to 6
- norm1_gain: float32 [768], replicated, may hold values from 0.5 to 1.5
- w_query: bfloat16 [768, 768], P(None, 'tensor'), may hold values from -0.21875 to 0.21875
- w_key: bfloat16 [768, 768], P(None, 'tensor'), may hold values from -0.21875 to 0.21875
- w_value: bfloat16 [768, 768], P(None, 'tensor'), may hold values from -0.21875 to 0.21875
- w_attn_out: bfloat16 [768, 768], P('tensor'), may hold values from -2.5 to 2.5
- bias_table: float32 [32, 12], P(None, 'tensor'), may hold values from -3 to 3
- norm2_gain: float32 [768], P('tensor'), may hold values from 0.5 to 1.5
- w_router: bfloat16 [768, 8], P('tensor'), may hold values from -0.15625 to 0.15625
- expert_in: bfloat16 [8, 768, 3072], P('expert', None, 'tensor'), may hold values from -0.21875 to 0.21875
- expert_out: bfloat16 [8, 3072, 768], P('expert', 'tensor'), may hold values from -1.25 to 1.25
- route: int32 [4096], P('expert'), may hold values from 0 to 7, as said below
- slot: int32 [4096], P('expert'), may hold values from 0 to 127, as said below
- segment: int32 [4096], P('expert'), may hold values from 0 to 15, never falling along the last dimension, each value on 1 to 512 neighbouring positions
- rel_bucket: int32 [1023], replicated, may hold values from 0 to 31, as said below
Outputs:
- block_out: bfloat16 [4096, 768], P('expert', 'tensor')
- input_grad: float32 [4096, 768], P('expert', 'tensor')
- norm1_gain_grad: float32 [768], replicated
- query_grad: float32 [768, 768], P(None, 'tensor')
- key_grad: float32 [768, 768], P(None, 'tensor')
- value_grad: float32 [768, 768], P(None, 'tensor')
- attn_out_grad: float32 [768, 768], P('tensor')
- table_grad: float32 [32, 12], P(None, 'tensor')
- norm2_gain_grad: float32 [768], P('tensor')
- router_grad: float32 [768, 8], P('tensor')
- expert_in_grad: float32 [8, 768, 3072], P('expert', None, 'tensor')
- expert_out_grad: float32 [8, 3072, 768], P('expert', 'tensor')
The draws below stay inside these ranges and needn't reach their ends.
Inputs may be any that keep to these rules, and one draw needn't show every extreme that they name: `route`: in each aligned block of 512 rows no expert is named more than 128 times, and one expert, the same in every block, is named exactly 128 times in every block. Within each aligned block of 512 rows no two tokens share both route and slot. `segment`: never falls along the tokens; a document holds 1 to 512 tokens. `rel_bucket`: entry 511 + r belongs to a key r positions after its query; it grows with the distance on each side, offsets after the query take buckets above 16 and offset 0 takes bucket 0.
All inputs are finite; a program needn't handle non-finite values.
Results may differ from the reference program's by a relative error of at most 0.015.
Values may be sent and summed in bfloat16 or wider, within the bound.
No kernel may reach another device: no remote copies, remote signals or barrier semaphores. Data moves between devices by JAX's collectives and lax.ppermute only.
A program may use at most 128 MiB of HBM per device.

```python
import math
import jax
import jax.numpy as jnp
import numpy as np
from jax import lax

D = 768
HEADS = 12
HDIM = 64
FF = 3072
BUCKETS = 32
SEQ = 512
TOK_DEV = 512
EXPERTS = 8
TOKENS = 4096
CAP = 128


def route_cells(key):
    blocks = TOKENS // TOK_DEV
    favored = jax.random.randint(jax.random.fold_in(key, 11), (), 0, EXPERTS)
    expert_ids = jnp.arange(EXPERTS, dtype=jnp.int32)[:, None]
    lanes = jnp.arange(CAP, dtype=jnp.int32)[None, :]
    labels = jnp.arange(EXPERTS * CAP, dtype=jnp.int32).reshape(EXPERTS, CAP)

    def one_block(block_key):
        costs = jax.random.randint(jax.random.fold_in(block_key, 1), (EXPERTS, 1), 1, 9)
        jitter = jax.random.randint(jax.random.fold_in(block_key, 2), (EXPERTS, CAP), 0, 4)
        scores = (CAP - lanes) * costs * 4 + jitter
        scores = jnp.where(expert_ids == favored, 64 * CAP, scores)
        unique = scores * (EXPERTS * CAP) + labels
        _, picked = lax.top_k(unique.reshape(-1), TOK_DEV)
        order = jax.random.permutation(jax.random.fold_in(block_key, 3), TOK_DEV)
        return jnp.zeros((TOK_DEV,), jnp.int32).at[order].set(picked.astype(jnp.int32))
    block_keys = jax.random.split(key, blocks)
    return jax.vmap(one_block)(block_keys).reshape(-1)


def draw_route(key, part):
    cells = route_cells(key)
    return (cells // CAP).astype(jnp.int32)


def draw_slot(key, part):
    cells = route_cells(key)
    return (cells % CAP).astype(jnp.int32)


def draw_rel_bucket(key, part):
    key = jax.random.fold_in(key, 5)
    half_count = BUCKETS // 2
    exact_count = half_count // 2
    spread = jax.random.permutation(key, SEQ - exact_count)[:half_count - exact_count] + exact_count
    bounds = jnp.concatenate([jnp.arange(1, exact_count, dtype=jnp.int32), spread.astype(jnp.int32)])
    shifts = jnp.arange(2 * SEQ - 1, dtype=jnp.int32) - (SEQ - 1)
    distance = jnp.abs(shifts)
    levels = jnp.sum((distance[:, None] >= bounds[None, :]).astype(jnp.int32), axis=1)
    return (levels + half_count * (shifts > 0).astype(jnp.int32)).astype(jnp.int32)


def steps_of(rng, shape, cuts, low, high):
    def one(dim, shards_of):
        draws = jax.random.uniform(jax.random.fold_in(jax.random.fold_in(rng, 6), dim), (shards_of,), jnp.float32, low / len(cuts), high / len(cuts))
        return jnp.repeat(jnp.exp(draws), shape[dim] // shards_of).reshape((-1,) + (1,) * (len(shape) - dim - 1))

    level = one(*cuts[0])
    for cut in cuts[1:]:
        level = level * one(*cut)
    return level


def profile(count, total, most, lean):
    portions = [(1 << 20) // math.isqrt(standing ** lean) + 1 for standing in range(2, count + 1)]
    rest, given = total - most - (count - 1), [1] * (count - 1)
    while rest > 0:
        candidates = [i for i in range(count - 1) if given[i] < most]
        whole, left = sum([portions[i] for i in candidates]), rest
        for i in candidates:
            more = min(most - given[i], max(1, left * portions[i] // whole), rest)
            given[i] = given[i] + more
            rest = rest - more
    return np.array([most] + given)


def uneven_parts(rng, amount, total, limit, skew):
    if amount == 2:
        one = jax.random.randint(rng, (), max(1, total - limit), min(limit, total - 1) + 1)
        return jnp.stack([one, total - one])
    tallies = jnp.asarray(profile(amount, total, limit, skew), jnp.int32)
    twos = (amount - 1) // 2
    donor, taker = tallies[1:1 + 2 * twos:2], tallies[2:2 + 2 * twos:2]
    margin = jnp.minimum(donor - 1, limit - taker)
    passed = jax.random.randint(jax.random.fold_in(rng, 1), (twos,), 0, 1 << 20) % (margin + 1)
    tallies = tallies.at[1:1 + 2 * twos:2].set(donor - passed).at[2:2 + 2 * twos:2].set(taker + passed)
    return tallies[jax.random.permutation(jax.random.fold_in(rng, 2), amount)]


def normal_values(stream_key, extent, deviation, reach, cuts=(), held_as=jnp.bfloat16):
    values = deviation * jax.random.normal(stream_key, extent, jnp.float32)
    if cuts:
        values = values * steps_of(stream_key, extent, cuts, -0.22, 0.18)
    return jnp.clip(values, -reach, reach).astype(held_as)


def setup_inputs(seed: int = 0) -> dict:
    streams_of = jax.random.split(jax.random.key(seed), 17)
    return {
        "tokens": normal_values(streams_of[0], (TOKENS, D), 1.0, 6.0, ((0, 8),)),
        "cotangent": normal_values(streams_of[1], (TOKENS, D), 1.0, 6.0, ((0, 8), (1, 4))),
        "norm1_gain": jnp.clip(1.0 + 0.1 * jax.random.normal(streams_of[2], (D,), jnp.float32), 0.5, 1.5),
        "w_query": normal_values(streams_of[3], (D, HEADS * HDIM), D ** -0.5, 0.21875, ((1, 4),)),
        "w_key": normal_values(streams_of[4], (D, HEADS * HDIM), D ** -0.5, 0.21875, ((1, 4),)),
        "w_value": normal_values(streams_of[5], (D, HEADS * HDIM), D ** -0.5, 0.21875, ((1, 4),)),
        "w_attn_out": normal_values(streams_of[6], (HEADS * HDIM, D), (max(1, 4 * D // SEQ)) ** -0.5, 2.5, ((0, 4),)),
        "bias_table": normal_values(streams_of[7], (BUCKETS, HEADS), 1.0, 3.0, ((1, 4),), jnp.float32),
        "norm2_gain": jnp.clip(1.0 + 0.1 * jax.random.normal(streams_of[8], (D,), jnp.float32), 0.5, 1.5),
        "w_router": normal_values(streams_of[9], (D, EXPERTS), (2 * D) ** -0.5, 0.15625, ((0, 4),)),
        "expert_in": normal_values(streams_of[10], (EXPERTS, D, FF), D ** -0.5, 0.21875, ((0, 8), (2, 4))),
        "expert_out": normal_values(streams_of[11], (EXPERTS, FF, D), (0.027 * EXPERTS), 1.25, ((0, 8), (1, 4))),
        "route": draw_route(jax.random.fold_in(streams_of[16], 71), 0),
        "slot": draw_slot(jax.random.fold_in(streams_of[16], 71), 0),
        "segment": jnp.searchsorted(jnp.cumsum(uneven_parts(streams_of[14], 2 * TOKENS // SEQ, TOKENS, SEQ, 0)), jnp.arange(TOKENS), side="right").astype(jnp.int32),
        "rel_bucket": draw_rel_bucket(jax.random.fold_in(streams_of[16], 71), 0),
    }


EPSILON = 1e-06
MASKED_SCORE = -1e+30
SCORE_SCALE = 0.125

@jax.custom_vjp
def low(v):
    return lax.optimization_barrier(v.astype(jnp.bfloat16)).astype(jnp.float32)

@jax.custom_vjp
def low_back(v):
    return v

def low_keep(v):
    return (low(v), None)

def low_pass(kept, grad):
    return (grad,)

def back_keep(v):
    return (v, None)

def back_low(kept, grad):
    return (low(grad),)
low.defvjp(low_keep, low_pass)
low_back.defvjp(back_keep, back_low)

def product(left, right):
    return jnp.dot(left, right, precision=lax.Precision.HIGHEST, preferred_element_type=jnp.float32)

def expert_pass(inputs):
    rows_in, weight_in, weight_out = inputs
    hidden = low_back(product(rows_in, weight_in))
    activated = low(jax.nn.gelu(hidden))
    return low_back(low(product(activated, weight_out)))

def reference(tokens, cotangent, norm1_gain, w_query, w_key, w_value, w_attn_out, bias_table, norm2_gain, w_router, expert_in, expert_out, route, slot, segment, rel_bucket):
    groups = TOKENS // TOK_DEV
    seq_count = TOKENS // SEQ
    owner_group = (jnp.arange(TOKENS, dtype=jnp.int32) // TOK_DEV).astype(jnp.int32)
    place_index = (jnp.arange(SEQ, dtype=jnp.int32)[None, :] - jnp.arange(SEQ, dtype=jnp.int32)[:, None] + (SEQ - 1)).astype(jnp.int32)
    buckets = rel_bucket[place_index]
    route_marks = (route[:, None] == jnp.arange(EXPERTS, dtype=jnp.int32)[None, :]).astype(jnp.float32)
    seg_rows = segment.reshape(seq_count, SEQ)

    def forward(source, gain_one, query_w, key_w, value_w, attn_w, table_w, gain_two, router_w, in_w, out_w):
        scale_one = lax.rsqrt(lax.optimization_barrier(jnp.mean(source * source, axis=1, keepdims=True)) + EPSILON)
        normed_one = low(source * scale_one * gain_one)
        queries = low(low_back(product(normed_one, query_w)))
        keys_all = low(low_back(product(normed_one, key_w)))
        values = low(low_back(product(normed_one, value_w)))
        bias_grid = jnp.transpose(table_w[buckets], (2, 0, 1))

        def attend(inputs):
            query_seq, key_seq, value_seq, seg_ids = inputs
            heads_q = query_seq.reshape(SEQ, HEADS, HDIM)
            heads_k = key_seq.reshape(SEQ, HEADS, HDIM)
            heads_v = value_seq.reshape(SEQ, HEADS, HDIM)
            raw_scores = low_back(SCORE_SCALE * jnp.einsum('qhd,khd->hqk', heads_q, heads_k, precision=lax.Precision.HIGHEST))
            same_doc = (seg_ids[:, None] == seg_ids[None, :])[None]
            scores = jnp.where(same_doc, raw_scores + bias_grid, MASKED_SCORE)
            weights = jnp.exp(scores - lax.optimization_barrier(jnp.max(scores, axis=2, keepdims=True)))
            weights_low = low(weights / lax.optimization_barrier(jnp.sum(weights, axis=2, keepdims=True)))
            mixed_seq = jnp.einsum('hqk,khd->qhd', weights_low, heads_v, precision=lax.Precision.HIGHEST)
            return low(low_back(mixed_seq.reshape(SEQ, HEADS * HDIM)))
        mixed = lax.map(jax.checkpoint(attend), (queries.reshape(seq_count, SEQ, -1), keys_all.reshape(seq_count, SEQ, -1), values.reshape(seq_count, SEQ, -1), seg_rows))
        mixed = mixed.reshape(TOKENS, HEADS * HDIM)
        residual = source + low_back(product(mixed, attn_w))
        scale_two = lax.rsqrt(lax.optimization_barrier(jnp.mean(residual * residual, axis=1, keepdims=True)) + EPSILON)
        normed_two = residual * scale_two * gain_two
        router_probs = jax.nn.softmax(product(normed_two, router_w), axis=1)
        gate_value = lax.optimization_barrier(jnp.sum(router_probs * route_marks, axis=1, keepdims=True))
        buffer = jnp.zeros((EXPERTS, groups, CAP, D), jnp.float32).at[route, owner_group, slot].set(low(normed_two))
        routed = low_back(buffer).reshape(EXPERTS, groups * CAP, D)
        returned = lax.map(jax.checkpoint(expert_pass), (routed, in_w, out_w))
        picked = returned.reshape(EXPERTS, groups, CAP, D)[route, owner_group, slot]
        return residual + gate_value * picked
    floats = (tokens.astype(jnp.float32), norm1_gain.astype(jnp.float32), w_query.astype(jnp.float32), w_key.astype(jnp.float32), w_value.astype(jnp.float32), w_attn_out.astype(jnp.float32), bias_table.astype(jnp.float32), norm2_gain.astype(jnp.float32), w_router.astype(jnp.float32), expert_in.astype(jnp.float32), expert_out.astype(jnp.float32))
    block_out, pull_back = jax.vjp(forward, *floats)
    grads = pull_back(cotangent.astype(jnp.float32))
    return (block_out.astype(jnp.bfloat16), grads[0], grads[1], grads[2], grads[3], grads[4], grads[5], grads[6], grads[7], grads[8], grads[9], grads[10])
```

```python
import functools

import jax
import jax.numpy as jnp
from jax import lax
from jax.experimental import pallas as pl
from jax.experimental.pallas import tpu as pltpu
from jax.sharding import PartitionSpec as P

HDIM = 64
EPSILON = 1e-06
MASKED_SCORE = -1e30
SCORE_SCALE = 0.125
PRECISE = lax.Precision.HIGHEST
F32 = jnp.float32
BF16 = jnp.bfloat16
GELU_C = 0.7978845608028654
GELU_A = 0.044715
CHUNK = 128


def dot_nn(a, b, precision=None):
    return lax.dot_general(
        a, b, (((1,), (0,)), ((), ())), precision=precision, preferred_element_type=F32
    )


def dot_nt(a, b, precision=None):
    return lax.dot_general(
        a, b, (((1,), (1,)), ((), ())), precision=precision, preferred_element_type=F32
    )


def dot_tn(a, b, precision=None):
    return lax.dot_general(
        a, b, (((0,), (0,)), ((), ())), precision=precision, preferred_element_type=F32
    )


def row_scale(rows):
    return lax.rsqrt(jnp.mean(rows * rows, axis=1, keepdims=True) + EPSILON)


def bucket_marks(bucket_ref, count):
    width = bucket_ref.shape[1]
    return lax.broadcasted_iota(jnp.int32, (count, width), 0) == bucket_ref[...]


def in_order(blocks, place):
    stack = place
    for j, (block, where) in enumerate(blocks):
        stack[where] = block[...]
    return jnp.concatenate([stack[r] for r in range(len(blocks))], axis=1)


def attend_kernel(
    tokens, gain, w_query, w_key, w_value, seg_col, seg_row, bucket, table,
    normed_out, query_out, key_out, value_out, probs_out, mixed_out, band,
):
    length = tokens.shape[0]
    width = 2 * length
    heads = query_out.shape[1] // HDIM
    rows = tokens[...].astype(F32)
    normed = (rows * row_scale(rows) * gain[...]).astype(BF16)
    normed_out[...] = normed
    query = dot_nn(normed, w_query[...]).astype(BF16)
    key = dot_nn(normed, w_key[...]).astype(BF16)
    value = dot_nn(normed, w_value[...]).astype(BF16)
    query_out[...] = query
    key_out[...] = key
    value_out[...] = value
    marks = bucket_marks(bucket, table.shape[0])
    for h in range(heads):
        cols = slice(h * HDIM, (h + 1) * HDIM)
        offsets = jnp.sum(
            jnp.where(marks, table[:, h : h + 1], 0.0), axis=0, keepdims=True
        )
        base = jnp.concatenate(
            [offsets] + [pltpu.roll(offsets, r, 1) for r in range(1, 8)], axis=0
        )
        for b in range(length // 8):
            turned = pltpu.roll(base, (length + 1 + 8 * b) % width, 1)
            band[8 * b : 8 * b + 8, :] = turned[:, :length]
        for c in range(0, length, CHUNK):
            span = slice(c, c + CHUNK)
            scores = dot_nt(query[span, cols], key[:, cols]) * SCORE_SCALE + band[span, :]
            scores = jnp.where(seg_col[span, :] == seg_row[...], scores, MASKED_SCORE)
            weights = jnp.exp(scores - jnp.max(scores, axis=1, keepdims=True))
            probs = weights / jnp.sum(weights, axis=1, keepdims=True)
            probs_out[h, span, :] = probs
            mixed_out[span, cols] = dot_nn(probs.astype(BF16), value[:, cols]).astype(BF16)


def cotangent_kernel(meta, code, c0, c1, c2, c3, *rest):
    outs, place = rest[:-1], rest[-1]
    rank = meta[0]
    full = in_order([(c, rank ^ j) for j, c in enumerate((c0, c1, c2, c3))], place)
    outs[0][...] = full
    dispatch(code, full, outs[1:])


def dispatch(code, rows, outs):
    share = outs[0].shape[0]
    for k, out in enumerate(outs):
        ids = lax.broadcasted_iota(jnp.int32, (share, code.shape[1]), 0) + k * share
        marks = jnp.where(ids == code[...], 1.0, 0.0).astype(BF16)
        out[...] = dot_nn(marks, rows).astype(BF16)


def residual_kernel(
    meta, code, route_col, m0, m1, m2, m3, w0, w1, w2, w3, p0, p1, p2, p3, tokens,
    residual_out, gate_out, probs_out, params_out, *rest,
):
    outs, place = rest[:-1], rest[-1]
    rank = meta[0]
    experts = probs_out.shape[1]
    params = in_order([(p, rank ^ j) for j, p in enumerate((p0, p1, p2, p3))], place)
    params_out[...] = params
    router = params[:experts]
    gain = params[experts : experts + 1]
    residual = tokens[...].astype(F32)
    for m, w in ((m0, w0), (m1, w1), (m2, w2), (m3, w3)):
        residual = residual + dot_nn(m[...], w[...])
    residual_out[...] = residual
    normed = residual * row_scale(residual) * gain
    logits = dot_nt(normed, router, PRECISE)
    shifted = jnp.exp(logits - jnp.max(logits, axis=1, keepdims=True))
    probs = shifted / jnp.sum(shifted, axis=1, keepdims=True)
    probs_out[...] = probs
    lanes = lax.broadcasted_iota(jnp.int32, probs.shape, 1)
    gate_out[...] = jnp.sum(jnp.where(lanes == route_col[...], probs, 0.0), axis=1, keepdims=True)
    dispatch(code, normed.astype(BF16), outs)


def expert_kernel(
    meta, x0, x1, x2, x3, c0, c1, c2, c3, w_in, w_out, router,
    rows_out, act_out, cots_out, d_hidden_out, keep_out, send_out,
    x_all, c_all, part_all, *, direct,
):
    rank, expert = meta[0], meta[1]
    ranks = 4
    total = rows_out.shape[0]
    feats = rows_out.shape[1]
    cols = feats // ranks
    if direct:
        sources, _, share, _ = x_all.shape
        for j, (x, c) in enumerate(((x0, c0), (x1, c1), (x2, c2), (x3, c3))):
            for s in range(sources):
                x_all[s, rank ^ j] = x[s * share : (s + 1) * share, :]
                c_all[s, rank ^ j] = c[s * share : (s + 1) * share, :]
        step = 256 // (ranks * share)
    else:
        step = 0

    def chunk(i, carry):
        span = pl.ds(pl.multiple_of(i * 256, 256), 256)
        if direct:
            rows = x_all[pl.ds(i * step, step)].reshape(256, feats)
            cots = c_all[pl.ds(i * step, step)].reshape(256, feats)
        else:
            rows = x0[span, :]
            cots = c0[span, :]
        rows_out[span, :] = rows
        logits = dot_nt(rows, router[...].astype(BF16))
        shifted = jnp.exp(logits - jnp.max(logits, axis=1, keepdims=True))
        lanes = lax.broadcasted_iota(jnp.int32, logits.shape, 1)
        gate = jnp.sum(jnp.where(lanes == expert, shifted, 0.0), axis=1, keepdims=True) / jnp.sum(
            shifted, axis=1, keepdims=True
        )
        cots = (gate * cots.astype(F32)).astype(BF16)
        cots_out[span, :] = cots
        hidden = dot_nn(rows, w_in[...])
        bent = jnp.tanh(GELU_C * (hidden + GELU_A * hidden * hidden * hidden))
        act = (0.5 * hidden * (1.0 + bent)).astype(BF16)
        act_out[span, :] = act
        slope = 0.5 * (1.0 + bent) + 0.5 * hidden * (1.0 - bent * bent) * (
            GELU_C * (1.0 + 3.0 * GELU_A * hidden * hidden)
        )
        d_hidden = (dot_nt(cots, w_out[...]) * slope).astype(BF16)
        d_hidden_out[span, :] = d_hidden
        part = dot_nn(act, w_out[...]).astype(BF16)
        d_part = dot_nt(d_hidden, w_in[...]).astype(BF16)
        for r in range(ranks):
            j = rank ^ r
            place = (j % 2) * 2 + j // 2
            own = slice(r * cols, (r + 1) * cols)
            part_all[place] = jnp.concatenate([part[:, own], d_part[:, own]], axis=1)
        keep_out[:, span, :] = part_all[0:2]
        send_out[:, span, :] = part_all[2:4]
        return carry

    lax.fori_loop(0, total // 256, chunk, 0)


def combine_kernel(meta, code_col, residual, gate, cotangent, *rest):
    *blocks, block_out, packed_out, came, place = rest
    rank = meta[0]
    cap = blocks[0].shape[0]
    cols = cotangent.shape[1]
    for k, block in enumerate(blocks):
        came[k * cap : (k + 1) * cap, :] = block[...]
    ids = lax.broadcasted_iota(jnp.int32, (code_col.shape[0], came.shape[0]), 1)
    marks = jnp.where(ids == code_col[...], 1.0, 0.0).astype(BF16)
    both = dot_nn(marks, came[...])
    returned = both[:, :cols]
    for r in range(4):
        place[r] = residual[:, r * cols : (r + 1) * cols]
    block_out[...] = (place[rank] + gate[...] * returned).astype(BF16)
    total = jnp.sum(cotangent[...].astype(F32) * returned, axis=1, keepdims=True)
    high = total.astype(BF16).astype(F32)
    low = total - high
    tail = packed_out.shape[1] - cols
    lanes = lax.broadcasted_iota(jnp.int32, (total.shape[0], tail), 1)
    extra = jnp.where(lanes == 0, high, jnp.where(lanes == 1, low, 0.0))
    packed_out[...] = jnp.concatenate([both[:, cols:], extra], axis=1).astype(BF16)


def residual_back_kernel(
    meta, r0, r1, r2, r3, residual, gate, probs, route_col, params, cotangent, mixed, w_attn_out,
    d_attn_cols_out, attn_grad_out, d_mixed_out, router_grad_out, gain_grad_out,
    place, place_f32,
):
    rank = meta[0]
    experts = probs.shape[1]
    feats = residual.shape[1]
    cols = feats // 4
    router = params[:experts, :]
    gain = params[experts : experts + 1, :]
    d_gate = 0.0
    for j, r in enumerate((r0, r1, r2, r3)):
        place[rank ^ j] = r[:, :cols]
        d_gate = d_gate + r[:, cols : cols + 1].astype(F32) + r[:, cols + 1 : cols + 2].astype(F32)
    d_routed = jnp.concatenate([place[r] for r in range(4)], axis=1).astype(F32)
    res = residual[...]
    scale = row_scale(res)
    lanes = lax.broadcasted_iota(jnp.int32, probs.shape, 1)
    onehot = jnp.where(lanes == route_col[...], 1.0, 0.0)
    d_logits = d_gate * probs[...] * (onehot - gate[...])
    d_normed = d_routed + dot_nn(d_logits, router, PRECISE)
    normed = res * scale * gain
    router_grad = dot_tn(d_logits, normed, PRECISE)
    gain_grad = jnp.sum(d_normed * res * scale, axis=0, keepdims=True)
    cross = jnp.sum(gain * res * d_normed, axis=1, keepdims=True)
    d_residual = (
        cotangent[...].astype(F32)
        + scale * gain * d_normed
        - res * (scale * scale * scale * cross * (1.0 / feats))
    )
    for r in range(4):
        own = slice(r * cols, (r + 1) * cols)
        place_f32[r] = d_residual[:, own]

        @pl.when(rank == r)
        def _():
            router_grad_out[...] = router_grad[:, own]
            gain_grad_out[...] = gain_grad[:, own]

    d_attn_cols_out[...] = place_f32[rank]
    d_attn = d_residual.astype(BF16)
    attn_grad_out[...] = dot_tn(mixed[...], d_attn).astype(BF16)
    d_mixed_out[...] = dot_nt(d_attn, w_attn_out[...]).astype(BF16)


def attend_back_kernel(
    meta, tokens, gain, normed, query, key, value, probs, d_mixed, bucket,
    w_query, w_key, w_value,
    query_grad_out, key_grad_out, value_grad_out, table_grad_out, gain_grad_out,
    keep_out, send_out, d_query, d_key, d_value, place,
    *, buckets,
):
    rank = meta[0]
    length = tokens.shape[0]
    width = 2 * length
    heads = query.shape[1] // HDIM
    marks = bucket_marks(bucket, buckets)
    zeros = jnp.zeros((8, width - length), F32)
    table_cols = []
    for h in range(heads):
        cols = slice(h * HDIM, (h + 1) * HDIM)
        dk = jnp.zeros((length, HDIM), F32)
        dv = jnp.zeros((length, HDIM), F32)
        diagonals = jnp.zeros((8, width), F32)
        for c in range(0, length, CHUNK):
            span = slice(c, c + CHUNK)
            weights = probs[h, span, :]
            d_probs = dot_nt(d_mixed[span, cols], value[:, cols])
            inner = jnp.sum(d_probs * weights, axis=1, keepdims=True)
            d_scores = weights * (d_probs - inner)
            for b in range(CHUNK // 8):
                piece = jnp.concatenate([d_scores[8 * b : 8 * b + 8, :], zeros], axis=1)
                diagonals = diagonals + pltpu.roll(piece, (length - 1 - c - 8 * b) % width, 1)
            low = d_scores.astype(BF16)
            d_query[span, cols] = (dot_nn(low, key[:, cols]) * SCORE_SCALE).astype(BF16)
            dk = dk + dot_tn(low, query[span, cols])
            dv = dv + dot_tn(weights.astype(BF16), d_mixed[span, cols])
        d_key[:, cols] = (dk * SCORE_SCALE).astype(BF16)
        d_value[:, cols] = dv.astype(BF16)
        line = diagonals[0:1]
        for r in range(1, 8):
            line = line + pltpu.roll(diagonals[r : r + 1], width - r, 1)
        table_cols.append(jnp.sum(jnp.where(marks, line, 0.0), axis=1, keepdims=True))
    table_grad_out[...] = jnp.concatenate(table_cols, axis=1)
    normed_rows = normed[...]
    query_grad_out[...] = dot_tn(normed_rows, d_query[...]).astype(BF16)
    key_grad_out[...] = dot_tn(normed_rows, d_key[...]).astype(BF16)
    value_grad_out[...] = dot_tn(normed_rows, d_value[...]).astype(BF16)
    d_normed = (
        dot_nt(d_query[...], w_query[...])
        + dot_nt(d_key[...], w_key[...])
        + dot_nt(d_value[...], w_value[...])
    )
    rows = tokens[...].astype(F32)
    scale = row_scale(rows)
    product = d_normed * rows
    gain_grad_out[...] = jnp.sum(product * scale, axis=0, keepdims=True)
    cross = jnp.sum(product * gain[...], axis=1, keepdims=True)
    high = cross.astype(BF16).astype(F32)
    low = cross - high
    cols = rows.shape[1] // 4
    tail = place.shape[2] - cols
    lanes = lax.broadcasted_iota(jnp.int32, (length, tail), 1)
    extra = jnp.where(lanes == 0, high, jnp.where(lanes == 1, low, 0.0)).astype(BF16)
    for r in range(4):
        j = rank ^ r
        own = d_normed[:, r * cols : (r + 1) * cols].astype(BF16)
        place[(j % 2) * 2 + j // 2] = jnp.concatenate([own, extra], axis=1)
    keep_out[...] = place[0:2]
    send_out[...] = place[2:4]


def input_kernel(meta, tokens, gain, d_attn_cols, first, second, out, place, gain_place):
    rank = meta[0]
    feats = tokens.shape[1]
    cols = feats // 4
    rows = tokens[...].astype(F32)
    scale = row_scale(rows)
    both = first[...].astype(F32) + second[...].astype(F32)
    cross = both[:, cols : cols + 1] + both[:, cols + 1 : cols + 2]
    for r in range(4):
        place[r] = rows[:, r * cols : (r + 1) * cols]
        gain_place[r] = gain[:, r * cols : (r + 1) * cols]
    out[...] = (
        d_attn_cols[...]
        + scale * gain_place[rank] * both[:, :cols]
        - place[rank] * (scale * scale * scale * cross * (1.0 / feats))
    )


def call(kernel, outs, scratch, *operands, flops=0, moved=0, smem=1):
    specs = [
        pl.BlockSpec(memory_space=pltpu.SMEM if i < smem else pltpu.VMEM)
        for i in range(len(operands))
    ]
    return pl.pallas_call(
        kernel,
        out_shape=[jax.ShapeDtypeStruct(shape, kind) for shape, kind in outs],
        in_specs=specs,
        out_specs=[pl.BlockSpec(memory_space=pltpu.VMEM)] * len(outs),
        scratch_shapes=[pltpu.VMEM(shape, kind) for shape, kind in scratch],
        compiler_params=pltpu.CompilerParams(vmem_limit_bytes=48 * 1024 * 1024),
        cost_estimate=pl.CostEstimate(flops=flops, bytes_accessed=moved, transcendentals=0),
    )(*operands)


def swap(array, axis, bit):
    size = lax.axis_size(axis)
    return lax.ppermute(array, axis, [(i, i ^ bit) for i in range(size)])


def gather_four(array):
    across = swap(array, "tensor", 2)
    beside = swap(array, "tensor", 1)
    return [array, beside, across, swap(across, "tensor", 1)]


def exchange(blocks):
    return [blocks[0]] + [swap(b, "expert", k) for k, b in enumerate(blocks) if k]


def on_device(
    tokens, cotangent, norm1_gain, w_query, w_key, w_value, w_attn_out, bias_table, norm2_gain,
    w_router, expert_in, expert_out, route, slot, segment, rel_bucket,
):
    length, feats = tokens.shape
    cols = cotangent.shape[1]
    heads = cols // HDIM
    experts = lax.axis_size("expert")
    cap = 2 * length // experts
    share = cap // 4
    rank = lax.axis_index("tensor").astype(jnp.int32)
    expert = lax.axis_index("expert").astype(jnp.int32)
    meta = jnp.stack([rank, expert])
    total = experts * cap
    direct = share % 16 == 0

    relative = route ^ expert
    code_col = (relative * cap + slot)[:, None]
    part_slot = slot - rank * share
    inside = (part_slot >= 0) & (part_slot < share)
    code_row = jnp.where(inside, relative * share + part_slot, -1)[None, :]
    route_col = route[:, None]

    cot_parts = gather_four(cotangent)
    cot_outs = call(
        cotangent_kernel,
        [((length, feats), BF16)] + [((share, feats), BF16)] * experts,
        [((4, length, cols), BF16)],
        meta, code_row, *cot_parts,
        flops=2 * total // 4 * length * feats, moved=4 * length * feats,
    )
    cot_full = cot_outs[0]
    cot_rows = gather_four(jnp.concatenate(exchange(cot_outs[1:]), axis=0))

    attn_weights = gather_four(w_attn_out)
    pad_rows = -(experts + 1) % 8
    packed_params = jnp.concatenate(
        [w_router.astype(F32).T, norm2_gain[None, :], jnp.zeros((pad_rows, cols), F32)], axis=0
    )
    param_rows = packed_params.shape[0]
    params_parts = gather_four(packed_params)

    gain_row = norm1_gain[None, :]
    bucket_row = jnp.concatenate([rel_bucket, jnp.full((1,), -1, jnp.int32)])[None, :]
    normed, query, key, value, probs, mixed = call(
        attend_kernel,
        [((length, feats), BF16)]
        + [((length, cols), BF16)] * 3
        + [((heads, length, length), F32), ((length, cols), BF16)],
        [((length, length), F32)],
        tokens, gain_row, w_query, w_key, w_value, segment[:, None], segment[None, :],
        bucket_row, bias_table,
        flops=8 * length * feats * cols, moved=8 * length * feats, smem=0,
    )

    mixed_parts = gather_four(mixed)
    res_outs = call(
        residual_kernel,
        [
            ((length, feats), F32),
            ((length, 1), F32),
            ((length, experts), F32),
            ((param_rows, feats), F32),
        ]
        + [((share, feats), BF16)] * experts,
        [((4, param_rows, cols), F32)],
        meta, code_row, route_col, *mixed_parts, *attn_weights, *params_parts, tokens,
        flops=4 * length * feats * feats, moved=8 * length * feats,
    )
    residual, gate, router_probs, params = res_outs[:4]
    rows = gather_four(jnp.concatenate(exchange(res_outs[4:]), axis=0))

    if not direct:
        def assemble(parts):
            stacked = jnp.stack(parts).reshape(4, experts, share, feats)
            stacked = stacked[rank ^ jnp.arange(4, dtype=jnp.int32)]
            return [jnp.transpose(stacked, (1, 0, 2, 3)).reshape(total, feats)]

        one = jnp.zeros((16, 128), BF16)
        rows = assemble(rows) + [one] * 3
        cot_rows = assemble(cot_rows) + [one] * 3
    w_in, w_out = expert_in[0], expert_out[0]
    hidden_count = w_in.shape[1]
    all_shape = (experts, 4, share, feats) if direct else (1, 1, 16, 128)
    rows_all, act, cots, d_hidden, keep, send = call(
        functools.partial(expert_kernel, direct=direct),
        [((total, feats), BF16), ((total, hidden_count), BF16), ((total, feats), BF16),
         ((total, hidden_count), BF16), ((2, total, 2 * cols), BF16), ((2, total, 2 * cols), BF16)],
        [(all_shape, BF16), (all_shape, BF16), ((4, 256, 2 * cols), BF16)],
        meta, *rows, *cot_rows, w_in, w_out, params[:experts],
        flops=8 * total * feats * hidden_count, moved=20 * total * feats,
    )
    expert_out_grad = dot_tn(act, cots)[None]
    expert_in_grad = dot_tn(rows_all, d_hidden)[None]

    met = (keep.astype(F32) + swap(send, "tensor", 1).astype(F32)).astype(BF16)
    whole = (met[0].astype(F32) + swap(met[1], "tensor", 2).astype(F32)).astype(BF16)
    came = exchange([whole[k * cap : (k + 1) * cap] for k in range(experts)])

    packed_width = -(-(cols + 2) // 128) * 128
    block_out, packed = call(
        combine_kernel,
        [((length, cols), BF16), ((length, packed_width), BF16)],
        [((total, 2 * cols), BF16), ((4, length, cols), F32)],
        meta, code_col, residual, gate, cotangent, *came,
        flops=2 * length * total * 2 * cols, moved=8 * length * feats,
    )
    packed_parts = gather_four(packed)
    d_attn_cols, attn_grad, d_mixed, router_grad, gain2_grad = call(
        residual_back_kernel,
        [((length, cols), F32), ((cols, feats), BF16), ((length, cols), BF16),
         ((experts, cols), F32), ((1, cols), F32)],
        [((4, length, cols), BF16), ((4, length, cols), F32)],
        meta, *packed_parts, residual, gate, router_probs, route_col, params, cot_full, mixed,
        w_attn_out,
        flops=4 * length * feats * cols, moved=8 * length * feats,
    )
    query_grad, key_grad, value_grad, table_grad, gain1_grad, keep_in, send_in = call(
        functools.partial(attend_back_kernel, buckets=bias_table.shape[0]),
        [((feats, cols), BF16)] * 3
        + [(bias_table.shape, F32), ((1, feats), F32)]
        + [((2, length, packed_width), BF16)] * 2,
        [((length, cols), BF16)] * 3 + [((4, length, packed_width), BF16)],
        meta, tokens, gain_row, normed, query, key, value, probs, d_mixed, bucket_row,
        w_query, w_key, w_value,
        flops=16 * length * feats * cols, moved=12 * length * feats,
    )
    met_in = (keep_in.astype(F32) + swap(send_in, "tensor", 1).astype(F32)).astype(BF16)
    far = swap(met_in[1], "tensor", 2)
    (input_grad,) = call(
        input_kernel,
        [((length, cols), F32)],
        [((4, length, cols), F32), ((4, 1, cols), F32)],
        meta, tokens, gain_row, d_attn_cols, met_in[0], far,
        flops=length * feats, moved=4 * length * feats,
    )

    attn_grad = lax.psum(attn_grad, "expert")
    query_grad, key_grad, value_grad = lax.psum((query_grad, key_grad, value_grad), "expert")
    table_grad, router_grad, gain2_grad = lax.psum((table_grad, router_grad, gain2_grad), "expert")
    gain1_grad = lax.psum(gain1_grad, ("expert", "tensor"))
    return (
        block_out,
        input_grad,
        gain1_grad[0],
        query_grad.astype(F32),
        key_grad.astype(F32),
        value_grad.astype(F32),
        attn_grad.astype(F32),
        table_grad,
        gain2_grad[0],
        router_grad.T,
        expert_in_grad,
        expert_out_grad,
    )


def solution(mesh):
    return jax.shard_map(
        on_device,
        mesh=mesh,
        in_specs=(
            P("expert", None),
            P("expert", "tensor"),
            P(),
            P(None, "tensor"),
            P(None, "tensor"),
            P(None, "tensor"),
            P("tensor", None),
            P(None, "tensor"),
            P("tensor"),
            P("tensor", None),
            P("expert", None, "tensor"),
            P("expert", "tensor", None),
            P("expert"),
            P("expert"),
            P("expert"),
            P(),
        ),
        out_specs=(
            P("expert", "tensor"),
            P("expert", "tensor"),
            P(),
            P(None, "tensor"),
            P(None, "tensor"),
            P(None, "tensor"),
            P("tensor", None),
            P(None, "tensor"),
            P("tensor"),
            P("tensor", None),
            P("expert", None, "tensor"),
            P("expert", "tensor", None),
        ),
        check_vma=False,
    )
```

```python
import functools

import jax
import jax.numpy as jnp
from jax import lax
from jax.experimental import pallas as pl
from jax.experimental.pallas import tpu as pltpu
from jax.sharding import PartitionSpec as P

HDIM = 64
EPSILON = 1e-06
MASKED_SCORE = -1e30
SCORE_SCALE = 0.125
PRECISE = lax.Precision.HIGHEST
F32 = jnp.float32
BF16 = jnp.bfloat16
GELU_C = 0.7978845608028654
GELU_A = 0.044715
CHUNK = 128


def dot_nn(a, b, precision=None):
    return lax.dot_general(
        a, b, (((1,), (0,)), ((), ())), precision=precision, preferred_element_type=F32
    )


def dot_nt(a, b, precision=None):
    return lax.dot_general(
        a, b, (((1,), (1,)), ((), ())), precision=precision, preferred_element_type=F32
    )


def dot_tn(a, b, precision=None):
    return lax.dot_general(
        a, b, (((0,), (0,)), ((), ())), precision=precision, preferred_element_type=F32
    )


def row_scale(rows):
    return lax.rsqrt(jnp.mean(rows * rows, axis=1, keepdims=True) + EPSILON)


def bucket_marks(bucket_ref, count):
    width = bucket_ref.shape[1]
    return lax.broadcasted_iota(jnp.int32, (count, width), 0) == bucket_ref[...]


def in_order(blocks, rank, place, axis):
    for j, block in enumerate(blocks):
        place[rank ^ j] = block[...]
    return jnp.concatenate([place[r] for r in range(len(blocks))], axis=axis)


def as_column(row):
    return jnp.broadcast_to(row, (128, row.shape[1])).T[:, 0:1]


def softmax_rows(logits):
    shifted = jnp.exp(logits - jnp.max(logits, axis=1, keepdims=True))
    return shifted / jnp.sum(shifted, axis=1, keepdims=True)


def attend_kernel(
    tokens, gain, w_query, w_key, w_value, seg_row, bucket, table,
    normed_out, query_out, key_out, value_out, probs_out, mixed_out, band,
):
    length = tokens.shape[0]
    width = 2 * length
    heads = query_out.shape[1] // HDIM
    rows = tokens[...].astype(F32)
    normed = (rows * row_scale(rows) * gain[...]).astype(BF16)
    normed_out[...] = normed
    query = dot_nt(normed, w_query[...]).astype(BF16)
    key = dot_nt(normed, w_key[...]).astype(BF16)
    value = dot_nt(normed, w_value[...]).astype(BF16)
    query_out[...] = query
    key_out[...] = key
    value_out[...] = value
    marks = bucket_marks(bucket, table.shape[0])
    seg_col = as_column(seg_row[...])
    for h in range(heads):
        cols = slice(h * HDIM, (h + 1) * HDIM)
        offsets = jnp.sum(
            jnp.where(marks, table[:, h : h + 1], 0.0), axis=0, keepdims=True
        )
        base = jnp.concatenate(
            [offsets] + [pltpu.roll(offsets, r, 1) for r in range(1, 8)], axis=0
        )
        for b in range(length // 8):
            turned = pltpu.roll(base, (length + 1 + 8 * b) % width, 1)
            band[8 * b : 8 * b + 8, :] = turned[:, :length]
        for c in range(0, length, CHUNK):
            span = slice(c, c + CHUNK)
            scores = dot_nt(query[span, cols], key[:, cols]) * SCORE_SCALE + band[span, :]
            scores = jnp.where(seg_col[span, :] == seg_row[...], scores, MASKED_SCORE)
            probs = softmax_rows(scores)
            probs_out[h, span, :] = probs
            mixed_out[span, cols] = dot_nn(probs.astype(BF16), value[:, cols]).astype(BF16)


def dispatch(code, rows, outs, transposed=False):
    share = outs[0].shape[0]
    for k, out in enumerate(outs):
        ids = lax.broadcasted_iota(jnp.int32, (share, code.shape[1]), 0) + k * share
        marks = jnp.where(ids == code[...], 1.0, 0.0).astype(BF16)
        product = dot_nt if transposed else dot_nn
        out[...] = product(marks, rows).astype(BF16)


def cotangent_kernel(meta, code, c0, c1, c2, c3, *rest):
    full_out, *outs, place = rest
    turned = in_order((c0, c1, c2, c3), meta[0], place, 0)
    full_out[...] = turned.astype(F32).T.astype(BF16)
    dispatch(code, turned, outs, transposed=True)


def residual_kernel(
    meta, code, route, m0, m1, m2, m3, w0, w1, w2, w3, p0, p1, p2, p3, tokens,
    residual_out, gate_out, probs_out, params_out, *rest,
):
    outs, place = rest[:-1], rest[-1]
    experts = probs_out.shape[1]
    params = in_order((p0, p1, p2, p3), meta[0], place, 1)
    params_out[...] = params
    router = params[:experts]
    gain = params[experts : experts + 1]
    residual = tokens[...].astype(F32)
    for m, w in ((m0, w0), (m1, w1), (m2, w2), (m3, w3)):
        residual = residual + dot_nn(m[...], w[...])
    residual_out[...] = residual
    normed = residual * row_scale(residual) * gain
    dispatch(code, normed.astype(BF16), outs)
    probs = softmax_rows(dot_nt(normed, router, PRECISE))
    probs_out[...] = probs
    lanes = lax.broadcasted_iota(jnp.int32, probs.shape, 1)
    marked = jnp.where(lanes == as_column(route[...]), probs, 0.0)
    gate_out[...] = jnp.sum(marked, axis=1, keepdims=True)


def expert_kernel(
    meta, x0, x1, x2, x3, c0, c1, c2, c3, w_in, w_out, router,
    rows_out, act_out, cots_out, d_hidden_out, keep_out, send_out,
    x_all, c_all, part_all, *, direct,
):
    rank, expert = meta[0], meta[1]
    ranks = 4
    total = rows_out.shape[0]
    feats = rows_out.shape[1]
    cols = feats // ranks
    if direct:
        sources, _, share, _ = x_all.shape
        for j, (x, c) in enumerate(((x0, c0), (x1, c1), (x2, c2), (x3, c3))):
            for s in range(sources):
                x_all[s, rank ^ j] = x[s * share : (s + 1) * share, :]
                c_all[s, rank ^ j] = c[s * share : (s + 1) * share, :]
        step = 256 // (ranks * share)
    else:
        step = 0

    def chunk(i, carry):
        span = pl.ds(pl.multiple_of(i * 256, 256), 256)
        if direct:
            rows = x_all[pl.ds(i * step, step)].reshape(256, feats)
            cots = c_all[pl.ds(i * step, step)].reshape(256, feats)
        else:
            rows = x0[span, :]
            cots = c0[span, :]
        rows_out[span, :] = rows
        probs = softmax_rows(dot_nt(rows, router[...].astype(BF16)))
        lanes = lax.broadcasted_iota(jnp.int32, probs.shape, 1)
        gate = jnp.sum(jnp.where(lanes == expert, probs, 0.0), axis=1, keepdims=True)
        cots_out[span, :] = (gate * cots.astype(F32)).astype(BF16)
        hidden = dot_nn(rows, w_in[...])
        pull = dot_nt(cots, w_out[...])
        bent = jnp.tanh(GELU_C * (hidden + GELU_A * hidden * hidden * hidden))
        act = (0.5 * hidden * (1.0 + bent)).astype(BF16)
        act_out[span, :] = act
        slope = 0.5 * (1.0 + bent) + 0.5 * hidden * (1.0 - bent * bent) * (
            GELU_C * (1.0 + 3.0 * GELU_A * hidden * hidden)
        )
        d_hidden = (gate * pull * slope).astype(BF16)
        d_hidden_out[span, :] = d_hidden
        d_gate = jnp.sum(pull * act.astype(F32), axis=1, keepdims=True)
        d_part = dot_nt(d_hidden, w_in[...]).astype(BF16)
        tail = jnp.broadcast_to(d_gate, (256, part_all.shape[2] - cols)).astype(BF16)
        for r in range(ranks):
            j = rank ^ r
            own = slice(r * cols, (r + 1) * cols)
            part_all[(j % 2) * 2 + j // 2] = jnp.concatenate([d_part[:, own], tail], axis=1)
        keep_out[:, span, :] = part_all[0:2]
        send_out[:, span, :] = part_all[2:4]
        return carry

    lax.fori_loop(0, total // 256, chunk, 0)


def expert_out_kernel(meta, act, w_out, keep_out, send_out, part_all):
    rank = meta[0]
    ranks = 4
    total = act.shape[0]
    feats = w_out.shape[1]
    cols = feats // ranks
    _, sources, half, _ = keep_out.shape
    step = 256 // (2 * half)

    def chunk(i, carry):
        span = pl.ds(pl.multiple_of(i * 256, 256), 256)
        part = dot_nn(act[span, :], w_out[...])
        for r in range(ranks):
            j = rank ^ r
            own = slice(r * cols, (r + 1) * cols)
            for s in range(step):
                low = part[2 * half * s : 2 * half * s + half, own]
                high = part[2 * half * s + half : 2 * half * (s + 1), own]
                part_all[(j % 2) * 2 + j // 2, s] = jnp.concatenate([low, high], axis=1).astype(
                    BF16
                )
        keep_out[:, pl.ds(i * step, step)] = part_all[0:2]
        send_out[:, pl.ds(i * step, step)] = part_all[2:4]
        return carry

    lax.fori_loop(0, total // 256, chunk, 0)


def combine_kernel(code, *rest):
    *blocks, out, came = rest
    cap = blocks[0].shape[0]
    for k, block in enumerate(blocks):
        came[k * cap : (k + 1) * cap, :] = block[...]
    ids = lax.broadcasted_iota(jnp.int32, (code.shape[1], came.shape[0]), 1)
    marks = jnp.where(ids == as_column(code[...]), 1.0, 0.0).astype(BF16)
    out[...] = dot_nn(marks, came[...]).astype(BF16)


def block_out_kernel(meta, code, came, residual, gate, block_out, place):
    rank = meta[0]
    cols = block_out.shape[1]
    count = came.shape[0]
    ids = lax.broadcasted_iota(jnp.int32, (code.shape[1], count), 1)
    where = as_column(code[...])
    low = jnp.where(ids == where, 1.0, 0.0).astype(BF16)
    high = jnp.where(ids + count == where, 1.0, 0.0).astype(BF16)
    returned = dot_nn(low, came[:, :cols]) + dot_nn(high, came[:, cols:])
    for r in range(4):
        place[r] = residual[:, r * cols : (r + 1) * cols]
    block_out[...] = (place[rank] + gate[...] * returned).astype(BF16)


def put_chunks(grads, out_keep, out_send, place, expert, order):
    count = len(order)
    size = grads.shape[0] // count
    for c in range(count):
        place[c ^ expert] = grads[c * size : (c + 1) * size, :]
    half = count // 2
    for i, k in enumerate(order):
        if i < half:
            out_keep[i] = place[k]
        else:
            out_send[i - half] = place[k]


def residual_back_kernel(
    meta, r0, r1, r2, r3, residual, gate, probs, route, params, cotangent, mixed, w_attn_out,
    attn_probs, normed_one, d_attn_cols_out, d_mixed_out, d_value_out, router_grad_out,
    gain_grad_out, *rest, chunked,
):
    *grads_out, place, place_f32, chunk_place = rest
    rank, expert = meta[0], meta[1]
    experts = probs.shape[1]
    feats = residual.shape[1]
    cols = feats // 4
    length = residual.shape[0]
    router = params[:experts, :]
    gain = params[experts : experts + 1, :]
    for j, r in enumerate((r0, r1, r2, r3)):
        place[rank ^ j] = r[:, :cols]
    d_gate = r0[:, cols : cols + 1].astype(F32)
    d_routed = jnp.concatenate([place[r] for r in range(4)], axis=1).astype(F32)
    res = residual[...]
    scale = row_scale(res)
    lanes = lax.broadcasted_iota(jnp.int32, probs.shape, 1)
    onehot = jnp.where(lanes == as_column(route[...]), 1.0, 0.0)
    d_logits = d_gate * probs[...] * (onehot - gate[...])
    d_normed = d_routed + dot_nn(d_logits, router, PRECISE)
    normed = res * scale * gain
    router_grad = dot_tn(d_logits, normed, PRECISE)
    gain_grad = jnp.sum(d_normed * res * scale, axis=0, keepdims=True)
    cross = jnp.sum(gain * res * d_normed, axis=1, keepdims=True)
    d_residual = (
        cotangent[...].astype(F32)
        + scale * gain * d_normed
        - res * (scale * scale * scale * cross * (1.0 / feats))
    )
    for r in range(4):
        own = slice(r * cols, (r + 1) * cols)
        place_f32[r] = d_residual[:, own]

        @pl.when(rank == r)
        def _():
            router_grad_out[...] = router_grad[:, own]
            gain_grad_out[...] = gain_grad[:, own]

    d_attn_cols_out[...] = place_f32[rank]
    d_attn = d_residual.astype(BF16)
    attn_grad = dot_tn(mixed[...], d_attn).astype(BF16)
    d_mixed = dot_nt(d_attn, w_attn_out[...]).astype(BF16)
    d_mixed_out[...] = d_mixed
    for h in range(cols // HDIM):
        own = slice(h * HDIM, (h + 1) * HDIM)
        total = jnp.zeros((length, HDIM), F32)
        for c in range(0, length, CHUNK):
            span = slice(c, c + CHUNK)
            total = total + dot_tn(attn_probs[h, span, :].astype(BF16), d_mixed[span, own])
        d_value_out[:, own] = total.astype(BF16)
    value_grad = dot_tn(d_value_out[...], normed_one[...]).astype(BF16)
    if chunked:
        both = jnp.concatenate([attn_grad, value_grad], axis=0)
        put_chunks(both, *grads_out, chunk_place, expert, chunked)
    else:
        grads_out[0][...] = attn_grad
        grads_out[1][...] = value_grad


def attend_back_kernel(
    meta, tokens, gain, normed, query, key, value, probs, d_mixed, d_value, bucket,
    w_query, w_key, w_value, router_grad, gain2_grad,
    small_out, keep_out, send_out, *rest, buckets, chunked,
):
    *grads_out, d_query, d_key, place, chunk_place = rest
    rank, expert = meta[0], meta[1]
    length = tokens.shape[0]
    width = 2 * length
    heads = query.shape[1] // HDIM
    feats = tokens.shape[1]
    cols = feats // 4
    marks = bucket_marks(bucket, buckets)
    zeros = jnp.zeros((8, width - length), F32)
    table_cols = []
    for h in range(heads):
        own = slice(h * HDIM, (h + 1) * HDIM)
        dk = jnp.zeros((length, HDIM), F32)
        diagonals = jnp.zeros((8, width), F32)
        for c in range(0, length, CHUNK):
            span = slice(c, c + CHUNK)
            weights = probs[h, span, :]
            d_probs = dot_nt(d_mixed[span, own], value[:, own])
            inner = jnp.sum(d_probs * weights, axis=1, keepdims=True)
            d_scores = weights * (d_probs - inner)
            for b in range(CHUNK // 8):
                piece = jnp.concatenate([d_scores[8 * b : 8 * b + 8, :], zeros], axis=1)
                diagonals = diagonals + pltpu.roll(piece, (length - 1 - c - 8 * b) % width, 1)
            low = d_scores.astype(BF16)
            d_query[span, own] = (dot_nn(low, key[:, own]) * SCORE_SCALE).astype(BF16)
            dk = dk + dot_tn(low, query[span, own])
        d_key[:, own] = (dk * SCORE_SCALE).astype(BF16)
        line = diagonals[0:1]
        for r in range(1, 8):
            line = line + pltpu.roll(diagonals[r : r + 1], width - r, 1)
        table_cols.append(jnp.sum(jnp.where(marks, line, 0.0), axis=1, keepdims=True))
    normed_rows = normed[...]
    query_grad = dot_tn(d_query[...], normed_rows).astype(BF16)
    key_grad = dot_tn(d_key[...], normed_rows).astype(BF16)
    if chunked:
        both = jnp.concatenate([query_grad, key_grad], axis=0)
        put_chunks(both, *grads_out, chunk_place, expert, chunked)
    else:
        grads_out[0][...] = query_grad
        grads_out[1][...] = key_grad
    d_normed = (
        dot_nn(d_query[...], w_query[...])
        + dot_nn(d_key[...], w_key[...])
        + dot_nn(d_value[...], w_value[...])
    )
    rows = tokens[...].astype(F32)
    scale = row_scale(rows)
    product = d_normed * rows
    gain1_grad = jnp.sum(product * scale, axis=0, keepdims=True)
    small_out[...] = jnp.zeros(small_out.shape, F32)
    for r in range(4):
        small_out[r : r + 1, :cols] = gain1_grad[:, r * cols : (r + 1) * cols]
    small_out[4:5, :cols] = gain2_grad[...]
    for h in range(heads):
        spread = jnp.broadcast_to(table_cols[h], (buckets, 128)).T
        small_out[8 + h : 9 + h, :buckets] = spread[0:1, :]
    small_out[16 : 16 + router_grad.shape[0], :cols] = router_grad[...]
    cross = jnp.sum(product * gain[...], axis=1, keepdims=True)
    high = cross.astype(BF16).astype(F32)
    low = cross - high
    tail = place.shape[2] - cols
    lanes = lax.broadcasted_iota(jnp.int32, (length, tail), 1)
    extra = jnp.where(lanes == 0, high, jnp.where(lanes == 1, low, 0.0)).astype(BF16)
    for r in range(4):
        j = rank ^ r
        own = d_normed[:, r * cols : (r + 1) * cols].astype(BF16)
        place[(j % 2) * 2 + j // 2] = jnp.concatenate([own, extra], axis=1)
    keep_out[...] = place[0:2]
    send_out[...] = place[2:4]


def input_kernel(meta, tokens, gain, d_attn_cols, first, second, out, place, gain_place):
    rank = meta[0]
    feats = tokens.shape[1]
    cols = feats // 4
    rows = tokens[...].astype(F32)
    scale = row_scale(rows)
    both = first[...].astype(F32) + second[...].astype(F32)
    cross = both[:, cols : cols + 1] + both[:, cols + 1 : cols + 2]
    for r in range(4):
        place[r] = rows[:, r * cols : (r + 1) * cols]
        gain_place[r] = gain[:, r * cols : (r + 1) * cols]
    out[...] = (
        d_attn_cols[...]
        + scale * gain_place[rank] * both[:, :cols]
        - place[rank] * (scale * scale * scale * cross * (1.0 / feats))
    )


def finish_kernel(meta, mine, other, first_out, second_out, place, *, order):
    expert = meta[1]
    count = len(order)
    size = mine.shape[1]
    half = count // 2
    for i, k in enumerate(order):
        place[k] = mine[i] if i < half else other[i - half]
    rows = first_out.shape[0]
    for c in range(count):
        chunk = place[c ^ expert].astype(F32)
        start = c * size
        if start < rows:
            first_out[start : start + size, :] = chunk
        else:
            second_out[start - rows : start - rows + size, :] = chunk


def call(kernel, outs, scratch, *operands, flops=0, moved=0, smem=1):
    specs = [
        pl.BlockSpec(memory_space=pltpu.SMEM if i < smem else pltpu.VMEM)
        for i in range(len(operands))
    ]
    return pl.pallas_call(
        kernel,
        out_shape=[jax.ShapeDtypeStruct(shape, kind) for shape, kind in outs],
        in_specs=specs,
        out_specs=[pl.BlockSpec(memory_space=pltpu.VMEM)] * len(outs),
        scratch_shapes=[pltpu.VMEM(shape, kind) for shape, kind in scratch],
        compiler_params=pltpu.CompilerParams(vmem_limit_bytes=48 * 1024 * 1024),
        cost_estimate=pl.CostEstimate(flops=flops, bytes_accessed=moved, transcendentals=0),
    )(*operands)


def swap(array, axis, bit):
    size = lax.axis_size(axis)
    return lax.ppermute(array, axis, [(i, i ^ bit) for i in range(size)])


def add_low(a, b):
    return (a.astype(F32) + b.astype(F32)).astype(BF16)


def gather_four(array):
    across = swap(array, "tensor", 2)
    beside = swap(array, "tensor", 1)
    return [array, beside, across, swap(across, "tensor", 1)]


def reduce_four(keep, send):
    got = swap(send, "tensor", 1)
    far = swap(add_low(keep[1], got[1]), "tensor", 2)
    return add_low(keep[0], got[0]), far


def exchange(blocks):
    if len(blocks) > 8:
        return hyper_exchange(blocks)
    return [blocks[0]] + [swap(b, "expert", k) for k, b in enumerate(blocks) if k]


def hyper_exchange(blocks):
    count = len(blocks)
    held = {k: [b] for k, b in enumerate(blocks)}
    bit = 1
    while bit < count:
        away = [k for k in sorted(held) if k & bit]
        sent = jnp.concatenate([b for k in away for b in held[k]], axis=0)
        got = swap(sent, "expert", bit)
        size = blocks[0].shape[0]
        at = 0
        fresh = {}
        for k in away:
            pieces = [got[at + i * size : at + (i + 1) * size] for i in range(len(held[k]))]
            at += len(held[k]) * size
            fresh[k ^ bit] = held[k ^ bit] + pieces
        held = fresh
        bit *= 2
    return held[0]


def reduce_chunks(keep, send, bits):
    got = swap(send, "expert", bits[0])
    for bit in bits[1:]:
        half = keep.shape[0] // 2
        sent = add_low(keep[half:], got[half:])
        keep = add_low(keep[:half], got[:half])
        got = swap(sent, "expert", bit)
    mine = add_low(keep, got)
    for bit in bits[:0:-1]:
        mine = jnp.concatenate([mine, swap(mine, "expert", bit)], axis=0)
    return mine, swap(mine, "expert", bits[0])


def chunk_order(bits):
    order = [0]
    for bit in reversed(bits):
        order = order + [k ^ bit for k in order]
    return order


def sum_over(array, axis):
    bit = 1
    while bit < lax.axis_size(axis):
        array = array + swap(array, axis, bit)
        bit *= 2
    return array


def on_device(
    tokens, cotangent, norm1_gain, w_query, w_key, w_value, w_attn_out, bias_table, norm2_gain,
    w_router, expert_in, expert_out, route, slot, segment, rel_bucket,
):
    length, feats = tokens.shape
    cols = cotangent.shape[1]
    heads = cols // HDIM
    experts = lax.axis_size("expert")
    cap = 2 * length // experts
    share = cap // 4
    half = cap // 2
    rank = lax.axis_index("tensor").astype(jnp.int32)
    expert = lax.axis_index("expert").astype(jnp.int32)
    meta = jnp.stack([rank, expert])
    total = experts * cap
    direct = share % 16 == 0
    buckets = bias_table.shape[0]
    first_bits, second_bits = (1, 2, 4), (2, 4, 1)
    chunked = experts == 8
    first_order = chunk_order(first_bits) if chunked else None
    second_order = chunk_order(second_bits) if chunked else None

    relative = route ^ expert
    code = (relative * cap + slot)[None, :]
    half_code = (relative * half + slot % half + (slot // half) * (total // 2))[None, :]
    part_slot = slot - rank * share
    inside = (part_slot >= 0) & (part_slot < share)
    share_code = jnp.where(inside, relative * share + part_slot, -1)[None, :]
    route_row = route[None, :]

    cot_parts = gather_four(cotangent.T)
    cot_full, *cot_blocks = call(
        cotangent_kernel,
        [((length, feats), BF16)] + [((share, feats), BF16)] * experts,
        [((4, cols, length), BF16)],
        meta, share_code, *cot_parts,
        flops=2 * total // 4 * length * feats, moved=4 * length * feats,
    )
    cot_rows = gather_four(jnp.concatenate(hyper_exchange(cot_blocks), axis=0))

    attn_weights = gather_four(w_attn_out)
    pad_rows = -(experts + 1) % 8
    packed_params = jnp.concatenate(
        [w_router.astype(F32).T, norm2_gain[None, :], jnp.zeros((pad_rows, cols), F32)], axis=0
    )
    param_rows = packed_params.shape[0]
    params_parts = gather_four(packed_params)

    gain_row = norm1_gain[None, :]
    bucket_row = jnp.concatenate([rel_bucket, jnp.full((1,), -1, jnp.int32)])[None, :]
    normed, query, key, value, probs, mixed = call(
        attend_kernel,
        [((length, feats), BF16)]
        + [((length, cols), BF16)] * 3
        + [((heads, length, length), F32), ((length, cols), BF16)],
        [((length, length), F32)],
        tokens, gain_row, w_query.T, w_key.T, w_value.T, segment[None, :], bucket_row, bias_table,
        flops=8 * length * feats * cols, moved=8 * length * feats, smem=0,
    )

    mixed_parts = gather_four(mixed)
    residual, gate, router_probs, params, *row_blocks = call(
        residual_kernel,
        [
            ((length, feats), F32),
            ((length, 1), F32),
            ((length, experts), F32),
            ((param_rows, feats), F32),
        ]
        + [((share, feats), BF16)] * experts,
        [((4, param_rows, cols), F32)],
        meta, share_code, route_row, *mixed_parts, *attn_weights, *params_parts, tokens,
        flops=4 * length * feats * feats, moved=8 * length * feats,
    )
    rows = gather_four(jnp.concatenate(exchange(row_blocks), axis=0))

    if not direct:
        def assemble(parts):
            stacked = jnp.stack(parts).reshape(4, experts, share, feats)
            stacked = stacked[rank ^ jnp.arange(4, dtype=jnp.int32)]
            return [jnp.transpose(stacked, (1, 0, 2, 3)).reshape(total, feats)]

        one = jnp.zeros((16, 128), BF16)
        rows = assemble(rows) + [one] * 3
        cot_rows = assemble(cot_rows) + [one] * 3
    w_in, w_out = expert_in[0], expert_out[0]
    hidden_count = w_in.shape[1]
    all_shape = (experts, 4, share, feats) if direct else (1, 1, 16, 128)
    wide = -(-(cols + 2) // 128) * 128
    rows_all, act, cots, d_hidden, keep, send = call(
        functools.partial(expert_kernel, direct=direct),
        [((total, feats), BF16), ((total, hidden_count), BF16), ((total, feats), BF16),
         ((total, hidden_count), BF16), ((2, total, wide), BF16), ((2, total, wide), BF16)],
        [(all_shape, BF16), (all_shape, BF16), ((4, 256, wide), BF16)],
        meta, *rows, *cot_rows, w_in, w_out, params[:experts],
        flops=6 * total * feats * hidden_count, moved=16 * total * feats,
    )
    near, far = reduce_four(keep, send)
    whole = add_low(near, far)
    came = exchange([whole[k * cap : (k + 1) * cap] for k in range(experts)])
    (d_routed,) = call(
        combine_kernel,
        [((length, wide), BF16)],
        [((total, wide), BF16)],
        code, *came,
        flops=2 * length * total * wide, moved=4 * length * feats, smem=0,
    )
    routed_parts = gather_four(d_routed)

    keep_fwd, send_fwd = call(
        expert_out_kernel,
        [((2, experts, half, 2 * cols), BF16)] * 2,
        [((4, 128 // half, half, 2 * cols), BF16)],
        meta, act, w_out,
        flops=2 * total * feats * hidden_count, moved=4 * total * feats,
    )
    near_fwd, far_fwd = reduce_four(keep_fwd, send_fwd)
    whole_fwd = add_low(near_fwd, far_fwd)
    came_fwd = jnp.concatenate(hyper_exchange([whole_fwd[k] for k in range(experts)]), axis=0)
    (block_out,) = call(
        block_out_kernel,
        [((length, cols), BF16)],
        [((4, length, cols), F32)],
        meta, half_code, came_fwd, residual, gate,
        flops=2 * length * total * cols, moved=8 * length * feats,
    )
    expert_out_grad = dot_tn(act, cots)[None]
    expert_in_grad = dot_tn(rows_all, d_hidden)[None]

    if chunked:
        size = 2 * cols // experts
        grad_outs = [((experts // 2, size, feats), BF16)] * 2
        chunk_scratch = ((experts, size, feats), BF16)
    else:
        grad_outs = [((cols, feats), BF16)] * 2
        chunk_scratch = ((16, 128), BF16)
    d_attn_cols, d_mixed, d_value, router_grad, gain2_grad, *first_grads = call(
        functools.partial(residual_back_kernel, chunked=first_order),
        [((length, cols), F32), ((length, cols), BF16), ((length, cols), BF16),
         ((experts, cols), F32), ((1, cols), F32)] + grad_outs,
        [((4, length, cols), BF16), ((4, length, cols), F32), chunk_scratch],
        meta, *routed_parts, residual, gate, router_probs, route_row, params, cot_full, mixed,
        w_attn_out, probs, normed,
        flops=6 * length * feats * cols, moved=12 * length * feats,
    )
    small_rows = 16 + -(-experts // 8) * 8
    small, keep_in, send_in, *second_grads = call(
        functools.partial(attend_back_kernel, buckets=buckets, chunked=second_order),
        [((small_rows, wide), F32)] + [((2, length, wide), BF16)] * 2 + grad_outs,
        [((length, cols), BF16)] * 2 + [((4, length, wide), BF16), chunk_scratch],
        meta, tokens, gain_row, normed, query, key, value, probs, d_mixed, d_value, bucket_row,
        w_query.T, w_key.T, w_value.T, router_grad, gain2_grad,
        flops=16 * length * feats * cols, moved=12 * length * feats,
    )
    near_in, far_in = reduce_four(keep_in, send_in)
    (input_grad,) = call(
        input_kernel,
        [((length, cols), F32)],
        [((4, length, cols), F32), ((4, 1, cols), F32)],
        meta, tokens, gain_row, d_attn_cols, near_in, far_in,
        flops=length * feats, moved=4 * length * feats,
    )

    small = sum_over(small, "expert")
    gain1_grad = sum_over(small[:8], "tensor")
    if chunked:
        grads = []
        for kept, bits, order in (
            (first_grads, first_bits, first_order),
            (second_grads, second_bits, second_order),
        ):
            mine, other = reduce_chunks(*kept, bits)
            grads += call(
                functools.partial(finish_kernel, order=order),
                [((cols, feats), F32)] * 2,
                [chunk_scratch],
                meta, mine, other,
                flops=0, moved=12 * cols * feats,
            )
        attn_grad, value_grad, query_grad, key_grad = grads
    else:
        attn_grad, value_grad, query_grad, key_grad = [
            g.astype(F32) for g in lax.psum((*first_grads, *second_grads), "expert")
        ]
    return (
        block_out,
        input_grad,
        gain1_grad[:4, :cols].reshape(feats),
        query_grad.T,
        key_grad.T,
        value_grad.T,
        attn_grad,
        small[8 : 8 + heads, :buckets].T,
        small[4, :cols],
        small[16 : 16 + experts, :cols].T,
        expert_in_grad,
        expert_out_grad,
    )


def solution(mesh):
    return jax.shard_map(
        on_device,
        mesh=mesh,
        in_specs=(
            P("expert", None),
            P("expert", "tensor"),
            P(),
            P(None, "tensor"),
            P(None, "tensor"),
            P(None, "tensor"),
            P("tensor", None),
            P(None, "tensor"),
            P("tensor"),
            P("tensor", None),
            P("expert", None, "tensor"),
            P("expert", "tensor", None),
            P("expert"),
            P("expert"),
            P("expert"),
            P(),
        ),
        out_specs=(
            P("expert", "tensor"),
            P("expert", "tensor"),
            P(),
            P(None, "tensor"),
            P(None, "tensor"),
            P(None, "tensor"),
            P("tensor", None),
            P(None, "tensor"),
            P("tensor"),
            P("tensor", None),
            P("expert", None, "tensor"),
            P("expert", "tensor", None),
        ),
        check_vma=False,
    )
```

```python
import functools

import jax
import jax.numpy as jnp
from jax import lax
from jax.experimental import pallas as pl
from jax.experimental.pallas import tpu as pltpu
from jax.sharding import PartitionSpec as P

HDIM = 64
EPSILON = 1e-06
MASKED_SCORE = -1e30
SCORE_SCALE = 0.125
PRECISE = lax.Precision.HIGHEST
F32 = jnp.float32
BF16 = jnp.bfloat16
GELU_C = 0.7978845608028654
GELU_A = 0.044715
CHUNK = 128
GROUPS = 1


def dot_nn(a, b, precision=None):
    return lax.dot_general(
        a, b, (((1,), (0,)), ((), ())), precision=precision, preferred_element_type=F32
    )


def dot_nt(a, b, precision=None):
    return lax.dot_general(
        a, b, (((1,), (1,)), ((), ())), precision=precision, preferred_element_type=F32
    )


def dot_tn(a, b, precision=None):
    return lax.dot_general(
        a, b, (((0,), (0,)), ((), ())), precision=precision, preferred_element_type=F32
    )


def row_scale(rows):
    return lax.rsqrt(jnp.mean(rows * rows, axis=1, keepdims=True) + EPSILON)


def bucket_marks(bucket, count):
    width = bucket.shape[0]
    return lax.broadcasted_iota(jnp.int32, (count, width), 0) == bucket[...].reshape(1, width)


def in_order(blocks, rank, place, axis):
    for j, block in enumerate(blocks):
        place[rank ^ j] = block[...]
    return jnp.concatenate([place[r] for r in range(len(blocks))], axis=axis)


def as_column(row):
    return jnp.broadcast_to(row, (128, row.shape[1])).T[:, 0:1]


def softmax_rows(logits):
    shifted = jnp.exp(logits - jnp.max(logits, axis=1, keepdims=True))
    return shifted / jnp.sum(shifted, axis=1, keepdims=True)


def attend_kernel(
    tokens, w_query, w_key, w_value, gain, segment, bucket, table,
    normed_out, query_out, key_out, value_out, probs_out, mixed_out,
    band, token_rows, weights, sems,
):
    copies = [pltpu.make_async_copy(tokens, token_rows, sems.at[0])]
    for i, w in enumerate((w_query, w_key, w_value)):
        copies.append(pltpu.make_async_copy(w, weights.at[i], sems.at[i + 1]))
    for copy in copies:
        copy.start()
    length = tokens.shape[0]
    width = 2 * length
    heads = query_out.shape[1] // HDIM
    marks = bucket_marks(bucket, table.shape[1])
    table_rows = jnp.broadcast_to(table[...][:, None, :], (heads, 128, table.shape[1]))
    bases = []
    for h in range(heads):
        offsets = jnp.sum(
            jnp.where(marks, table_rows[h].T[:, 0:1], 0.0), axis=0, keepdims=True
        )
        bases.append(
            jnp.concatenate(
                [offsets] + [pltpu.roll(offsets, r, 1) for r in range(1, 8)], axis=0
            )
        )
    seg_row = segment[...].reshape(1, length)
    seg_col = as_column(seg_row)
    for copy in copies:
        copy.wait()
    rows = token_rows[...].astype(F32)
    normed = (rows * row_scale(rows) * gain[...].reshape(1, rows.shape[1])).astype(BF16)
    normed_out[...] = normed
    query = dot_nt(normed, weights[0]).astype(BF16)
    key = dot_nt(normed, weights[1]).astype(BF16)
    query_out[...] = query
    key_out[...] = key
    value_out[...] = dot_nt(normed, weights[2]).astype(BF16)
    value_turned = dot_nt(weights[2], normed).astype(BF16)
    for h in range(heads):
        cols = slice(h * HDIM, (h + 1) * HDIM)
        for b in range(length // 8):
            turned = pltpu.roll(bases[h], (length + 1 + 8 * b) % width, 1)
            band[8 * b : 8 * b + 8, :] = turned[:, :length]
        for c in range(0, length, CHUNK):
            span = slice(c, c + CHUNK)
            scores = dot_nt(query[span, cols], key[:, cols]) * SCORE_SCALE + band[span, :]
            scores = jnp.where(seg_col[span, :] == seg_row, scores, MASKED_SCORE)
            probs = softmax_rows(scores)
            probs_out[h, span, :] = probs
            mixed_out[cols, span] = dot_nt(value_turned[cols, :], probs.astype(BF16)).astype(BF16)


def dispatch(code, rows, outs, transposed=False):
    share = outs[0].shape[0]
    for k, out in enumerate(outs):
        ids = lax.broadcasted_iota(jnp.int32, (share, code.shape[1]), 0) + k * share
        marks = jnp.where(ids == code[...], 1.0, 0.0).astype(BF16)
        product = dot_nt if transposed else dot_nn
        out[...] = product(marks, rows).astype(BF16)


def slot_codes(meta, route, slot, size):
    count = route.shape[0]
    return ((route[...] ^ meta[1]) * size + slot[...]).reshape(1, count)


def first_kernel(
    meta, route, slot, cotangent, w_attn_out, w_router, gain, packed_out, *outs
):
    cap = outs[0].shape[1]
    count = len(outs) * cap
    code = slot_codes(meta, route, slot, cap)
    ids = lax.broadcasted_iota(jnp.int32, (count, code.shape[1]), 0)
    marks = jnp.where(ids == code, 1.0, 0.0).astype(BF16)
    placed = dot_nt(cotangent[...], marks).astype(BF16)
    for k, out in enumerate(outs):
        out[...] = placed[:, k * cap : (k + 1) * cap]
    rows, feats = w_attn_out.shape
    experts = w_router.shape[0]
    packed_out[:rows, :] = w_attn_out[...]
    line = gain[...].reshape(1, rows)
    high = line.astype(BF16)
    rest = line - high.astype(F32)
    mid = rest.astype(BF16)
    low = (rest - mid.astype(F32)).astype(BF16)
    pad = packed_out.shape[0] - rows - experts - 3
    extra = [w_router[...].astype(F32)] + [p.astype(F32) for p in (high, mid, low)]
    extra = jnp.concatenate(extra + [jnp.zeros((pad, rows), F32)], axis=0)
    wide = jnp.concatenate([extra, jnp.zeros((extra.shape[0], feats - rows), F32)], axis=1)
    packed_out[rows:, :] = wide.astype(BF16)


def dispatch(code, rows, outs):
    share = outs[0].shape[0]
    for k, out in enumerate(outs):
        ids = lax.broadcasted_iota(jnp.int32, (share, code.shape[1]), 0) + k * share
        marks = jnp.where(ids == code, 1.0, 0.0).astype(BF16)
        out[...] = dot_nn(marks, rows).astype(BF16)


def residual_kernel(
    meta, route, slot, m0, m1, m2, m3, w0, w1, w2, w3, tokens,
    residual_out, gate_out, probs_out, params_out, *rest,
):
    outs, place = rest[:-1], rest[-1]
    share = outs[0].shape[0]
    experts = probs_out.shape[1]
    cols = m0.shape[0]
    for j, w in enumerate((w0, w1, w2, w3)):
        place[meta[0] ^ j] = w[cols:, :cols].astype(F32)
    params = jnp.concatenate([place[r] for r in range(4)], axis=1)
    router = params[:experts]
    gain = params[experts : experts + 1]
    for i in (1, 2):
        gain = gain + params[experts + i : experts + i + 1]
    params_out[...] = jnp.concatenate([router, jnp.broadcast_to(gain, (8, gain.shape[1]))], axis=0)
    residual = tokens[...].astype(F32)
    for m, w in ((m0, w0), (m1, w1), (m2, w2), (m3, w3)):
        residual = residual + dot_tn(m[...], w[:cols, :])
    residual_out[...] = residual
    normed = residual * row_scale(residual) * gain
    part = slot[...] - meta[0] * share
    code = jnp.where(
        (part >= 0) & (part < share), (route[...] ^ meta[1]) * share + part, -1
    ).reshape(1, part.shape[0])
    dispatch(code, normed.astype(BF16), outs)
    probs = softmax_rows(dot_nt(normed, router, PRECISE))
    probs_out[...] = probs
    lanes = lax.broadcasted_iota(jnp.int32, probs.shape, 1)
    where = as_column(route[...].reshape(1, part.shape[0]))
    gate_out[...] = jnp.sum(jnp.where(lanes == where, probs, 0.0), axis=1, keepdims=True)


def assemble_kernel(*refs, count):
    out = refs[-1]
    size = refs[0].shape[0]
    for i, block in enumerate(refs[:count]):
        out[i * size : (i + 1) * size, :] = block[...]


def expert_kernel(
    meta, x0, x1, x2, x3, c0, c1, c2, c3, w_in, w_out, router,
    rows_out, act_out, cots_out, d_hidden_out, keep_out, send_out,
    x_all, c_all, part_all, *, first, direct,
):
    rank, expert = meta[0], meta[1]
    ranks = 4
    total = rows_out.shape[0]
    feats = rows_out.shape[1]
    cols = feats // ranks
    if direct:
        sources, _, share, _ = x_all.shape
        cap = ranks * share
        for j, (x, c) in enumerate(((x0, c0), (x1, c1), (x2, c2), (x3, c3))):
            for s in range(sources):
                x_all[s, rank ^ j] = x[s * share : (s + 1) * share, :]
                at = (first + s) * cols
                c_all[rank ^ j, :, s * cap : (s + 1) * cap] = c[at : at + cols, :]
        step = 256 // cap
    for i in range(total // 256):
        span = slice(i * 256, (i + 1) * 256)
        if direct:
            rows = x_all[i * step : (i + 1) * step].reshape(256, feats)
            turned = jnp.concatenate([c_all[r, :, span] for r in range(ranks)], axis=0)
            cots = turned.astype(F32).T.astype(BF16)
        else:
            rows = x0[span, :]
            cots = c0[span, :]
        rows_out[span, :] = rows
        probs = softmax_rows(dot_nt(rows, router[...].astype(BF16)))
        lanes = lax.broadcasted_iota(jnp.int32, probs.shape, 1)
        gate = jnp.sum(jnp.where(lanes == expert, probs, 0.0), axis=1, keepdims=True)
        cots_out[span, :] = (gate * cots.astype(F32)).astype(BF16)
        hidden = dot_nn(rows, w_in[...])
        pull = dot_nt(cots, w_out[...])
        bent = jnp.tanh(GELU_C * (hidden + GELU_A * hidden * hidden * hidden))
        act = (0.5 * hidden * (1.0 + bent)).astype(BF16)
        act_out[span, :] = act
        slope = 0.5 * (1.0 + bent) + 0.5 * hidden * (1.0 - bent * bent) * (
            GELU_C * (1.0 + 3.0 * GELU_A * hidden * hidden)
        )
        d_hidden = (gate * pull * slope).astype(BF16)
        d_hidden_out[span, :] = d_hidden
        d_gate = jnp.sum(pull * act.astype(F32), axis=1, keepdims=True)
        d_part = dot_nt(w_in[...], d_hidden).astype(BF16)
        tail = jnp.broadcast_to(d_gate, (256, 128)).T[: part_all.shape[1] - cols].astype(BF16)
        for r in range(ranks):
            j = rank ^ r
            place = (j % 2) * 2 + j // 2
            part_all[place, :cols, span] = d_part[r * cols : (r + 1) * cols, :]
            part_all[place, cols:, span] = tail
    keep_out[...] = part_all[0:2]
    send_out[...] = part_all[2:4]


def expert_out_kernel(meta, w_out, *refs, groups):
    acts, (keep_out, send_out, part_all) = refs[:groups], refs[-3:]
    rank = meta[0]
    ranks = 4
    cols = part_all.shape[1]
    at = 0
    for act in acts:
        for i in range(0, act.shape[0], 256):
            part = dot_nn(act[i : i + 256, :], w_out[...]).T.astype(BF16)
            for r in range(ranks):
                j = rank ^ r
                part_all[(j % 2) * 2 + j // 2, :, at : at + 256] = part[r * cols : (r + 1) * cols]
            at += 256
    keep_out[...] = part_all[0:2]
    send_out[...] = part_all[2:4]


def slot_marks(meta, route, slot, cap, count):
    code = slot_codes(meta, route, slot, cap)
    ids = lax.broadcasted_iota(jnp.int32, (code.shape[1], count), 1)
    return jnp.where(ids == as_column(code), 1.0, 0.0).astype(BF16)


def fence_kernel(*refs):
    del refs


def side_by_side(blocks, came):
    size = blocks[0].shape[1]
    for k, block in enumerate(blocks):
        came[:, k * size : (k + 1) * size] = block[...]
    return came[...]


def combine_kernel(meta, route, slot, *rest, cap):
    *blocks, _, out, came = rest
    marks = slot_marks(meta, route, slot, cap, came.shape[1])
    out[...] = dot_nt(side_by_side(blocks, came), marks).astype(BF16)


def block_out_kernel(meta, route, slot, residual, gate, *rest, cap):
    *blocks, block_out, came, place = rest
    rank = meta[0]
    cols = block_out.shape[1]
    marks = slot_marks(meta, route, slot, cap, came.shape[1])
    returned = dot_nt(marks, side_by_side(blocks, came))
    for r in range(4):
        place[r] = residual[:, r * cols : (r + 1) * cols]
    block_out[...] = (place[rank] + gate[...] * returned).astype(BF16)


def put_chunks(grads, out_keep, out_send, place, expert, order):
    count = len(order)
    size = grads.shape[0] // count
    for c in range(count):
        place[c ^ expert] = grads[c * size : (c + 1) * size, :]
    half = count // 2
    for i, k in enumerate(order):
        if i < half:
            out_keep[i] = place[k]
        else:
            out_send[i - half] = place[k]


def residual_back_kernel(
    meta, r0, r1, r2, r3, k0, k1, k2, k3, residual, gate, probs, route, params, mixed, w_attn_out,
    attn_probs, normed_one, _, d_attn_cols_out, d_mixed_out, d_value_out, router_grad_out,
    gain_grad_out, *rest, chunked,
):
    *grads_out, place, cot_place, place_f32, chunk_place = rest
    rank, expert = meta[0], meta[1]
    experts = probs.shape[1]
    feats = residual.shape[1]
    cols = feats // 4
    length = residual.shape[0]
    router = params[:experts, :]
    gain = params[experts : experts + 1, :]
    for j, r in enumerate((r0, r1, r2, r3)):
        place[rank ^ j] = r[:cols, :]
    d_gate = as_column(r0[cols : cols + 1, :].astype(F32))
    d_routed = jnp.concatenate([place[r] for r in range(4)], axis=0).astype(F32).T
    for j, k in enumerate((k0, k1, k2, k3)):
        cot_place[rank ^ j] = k[...]
    cotangent = jnp.concatenate([cot_place[r] for r in range(4)], axis=0).astype(F32).T
    res = residual[...]
    scale = row_scale(res)
    lanes = lax.broadcasted_iota(jnp.int32, probs.shape, 1)
    onehot = jnp.where(lanes == as_column(route[...].reshape(1, length)), 1.0, 0.0)
    d_logits = d_gate * probs[...] * (onehot - gate[...])
    d_normed = d_routed + dot_nn(d_logits, router, PRECISE)
    normed = res * scale * gain
    router_grad = dot_tn(d_logits, normed, PRECISE)
    gain_grad = jnp.sum(d_normed * res * scale, axis=0, keepdims=True)
    cross = jnp.sum(gain * res * d_normed, axis=1, keepdims=True)
    d_residual = (
        cotangent
        + scale * gain * d_normed
        - res * (scale * scale * scale * cross * (1.0 / feats))
    )
    for r in range(4):
        own = slice(r * cols, (r + 1) * cols)
        place_f32[r] = d_residual[:, own]

        @pl.when(rank == r)
        def _():
            router_grad_out[...] = router_grad[:, own]
            gain_grad_out[...] = gain_grad[:, own]

    d_attn_cols_out[...] = place_f32[rank]
    d_attn = d_residual.astype(BF16)
    attn_grad = dot_nn(mixed[...], d_attn).astype(BF16)
    d_mixed = dot_nt(d_attn, w_attn_out[...]).astype(BF16)
    d_mixed_out[...] = d_mixed
    for h in range(cols // HDIM):
        own = slice(h * HDIM, (h + 1) * HDIM)
        total = jnp.zeros((length, HDIM), F32)
        for c in range(0, length, CHUNK):
            span = slice(c, c + CHUNK)
            total = total + dot_tn(attn_probs[h, span, :].astype(BF16), d_mixed[span, own])
        d_value_out[:, own] = total.astype(BF16)
    value_grad = dot_tn(d_value_out[...], normed_one[...]).astype(BF16)
    if chunked:
        both = jnp.concatenate([attn_grad, value_grad], axis=0)
        put_chunks(both, *grads_out, chunk_place, expert, chunked)
    else:
        grads_out[0][...] = attn_grad
        grads_out[1][...] = value_grad


def attend_back_kernel(
    query, key, value, probs, d_mixed, bucket, d_query, d_key, table_out, *, buckets
):
    length = query.shape[0]
    width = 2 * length
    heads = query.shape[1] // HDIM
    marks = bucket_marks(bucket, buckets)
    zeros = jnp.zeros((8, width - length), F32)
    table_out[...] = jnp.zeros(table_out.shape, F32)
    for h in range(heads):
        own = slice(h * HDIM, (h + 1) * HDIM)
        dk = jnp.zeros((length, HDIM), F32)
        diagonals = jnp.zeros((8, width), F32)
        for c in range(0, length, CHUNK):
            span = slice(c, c + CHUNK)
            weights = probs[h, span, :]
            d_probs = dot_nt(d_mixed[span, own], value[:, own])
            inner = jnp.sum(d_probs * weights, axis=1, keepdims=True)
            d_scores = weights * (d_probs - inner)
            for b in range(CHUNK // 8):
                piece = jnp.concatenate([d_scores[8 * b : 8 * b + 8, :], zeros], axis=1)
                diagonals = diagonals + pltpu.roll(piece, (length - 1 - c - 8 * b) % width, 1)
            low = d_scores.astype(BF16)
            d_query[span, own] = (dot_nn(low, key[:, own]) * SCORE_SCALE).astype(BF16)
            dk = dk + dot_tn(low, query[span, own])
        d_key[:, own] = (dk * SCORE_SCALE).astype(BF16)
        line = diagonals[0:1]
        for r in range(1, 8):
            line = line + pltpu.roll(diagonals[r : r + 1], width - r, 1)
        table_col = jnp.sum(jnp.where(marks, line, 0.0), axis=1, keepdims=True)
        table_out[h : h + 1, :buckets] = jnp.broadcast_to(table_col, (buckets, 128)).T[0:1, :]


def query_grads_kernel(meta, normed, d_query, d_key, *rest, chunked):
    *_, first_out, second_out, chunk_place = rest
    expert = meta[1]
    normed_rows = normed[...]
    query_grad = dot_tn(d_query[...], normed_rows).astype(BF16)
    key_grad = dot_tn(d_key[...], normed_rows).astype(BF16)
    if chunked:
        both = jnp.concatenate([query_grad, key_grad], axis=0)
        put_chunks(both, first_out, second_out, chunk_place, expert, chunked)
    else:
        first_out[...] = query_grad
        second_out[...] = key_grad


def normed_back_kernel(
    meta, tokens, gain, d_query, d_key, d_value, w_query, w_key, w_value, *rest
):
    *_, keep_out, send_out, place = rest
    rank = meta[0]
    length, feats = tokens.shape
    cols = feats // 4
    d_normed = (
        dot_nn(d_query[...], w_query[...])
        + dot_nn(d_key[...], w_key[...])
        + dot_nn(d_value[...], w_value[...])
    )
    product = d_normed * tokens[...].astype(F32)
    cross = jnp.sum(product * gain[...].reshape(1, feats), axis=1, keepdims=True)
    high = cross.astype(BF16).astype(F32)
    low = cross - high
    lanes = lax.broadcasted_iota(jnp.int32, (length, place.shape[2] - cols), 1)
    extra = jnp.where(lanes == 0, high, jnp.where(lanes == 1, low, 0.0)).astype(BF16)
    for r in range(4):
        j = rank ^ r
        own = d_normed[:, r * cols : (r + 1) * cols].astype(BF16)
        place[(j % 2) * 2 + j // 2] = jnp.concatenate([own, extra], axis=1)
    keep_out[...] = place[0:2]
    send_out[...] = place[2:4]


def input_kernel(
    meta, tokens, gain, d_attn_cols, first, second, gain2_grad, table_grad, router_grad, *rest
):
    *_, out, small_out, place, gain_place = rest
    rank = meta[0]
    feats = tokens.shape[1]
    cols = feats // 4
    rows = tokens[...].astype(F32)
    scale = row_scale(rows)
    both = first[...].astype(F32) + second[...].astype(F32)
    cross = both[:, cols : cols + 1] + both[:, cols + 1 : cols + 2]
    gain_row = gain[...].reshape(1, feats)
    for r in range(4):
        place[r] = rows[:, r * cols : (r + 1) * cols]
        gain_place[r] = gain_row[:, r * cols : (r + 1) * cols]
    own = both[:, :cols]
    own_rows = place[rank]
    out[...] = (
        d_attn_cols[...]
        + scale * gain_place[rank] * own
        - own_rows * (scale * scale * scale * cross * (1.0 / feats))
    )
    small_out[...] = jnp.zeros(small_out.shape, F32)
    small_out[0:1, :cols] = jnp.sum(own * own_rows * scale, axis=0, keepdims=True)
    small_out[4:5, :cols] = gain2_grad[...]
    small_out[8:16, :128] = table_grad[...]
    small_out[16 : 16 + router_grad.shape[0], :cols] = router_grad[...]


def sum_kernel(keep, got, *rest):
    outs = rest[-4:]
    for i, out in enumerate(outs):
        out[...] = (keep[i].astype(F32) + got[i].astype(F32)).astype(BF16)


def last_sum_kernel(a, b, c, d, *rest):
    out = rest[-1]
    out[...] = (
        a[...].astype(F32) + b[...].astype(F32) + c[...].astype(F32) + d[...].astype(F32)
    ).astype(BF16)


def finish_kernel(meta, m0, m2, m4, m6, other, *rest, order):
    *_, first_out, second_out, place = rest
    expert = meta[1]
    count = len(order)
    size = m0.shape[0]
    half = count // 2
    for i, m in enumerate((m0, m2, m4, m6)):
        place[order[i]] = m[...]
    for i in range(half):
        place[order[half + i]] = other[i * size : (i + 1) * size, :]
    rows = first_out.shape[0]
    for c in range(count):
        chunk = place[c ^ expert].astype(F32)
        start = c * size
        if start < rows:
            first_out[start : start + size, :] = chunk
        else:
            second_out[start - rows : start - rows + size, :] = chunk


def call(kernel, outs, scratch, *operands, weight=1.0, smem=1, loose=(), after=()):
    specs = []
    for i in range(len(operands)):
        if i < smem:
            specs.append(pl.BlockSpec(memory_space=pltpu.SMEM))
        elif i in loose:
            specs.append(pl.BlockSpec(memory_space=pl.ANY))
        else:
            specs.append(pl.BlockSpec(memory_space=pltpu.VMEM))
    specs += [pl.BlockSpec(memory_space=pl.ANY)] * len(after)
    return pl.pallas_call(
        kernel,
        out_shape=[jax.ShapeDtypeStruct(shape, kind) for shape, kind in outs],
        in_specs=specs,
        out_specs=[pl.BlockSpec(memory_space=pltpu.VMEM)] * len(outs),
        scratch_shapes=[
            s if not isinstance(s, tuple) else pltpu.VMEM(s[0], s[1]) for s in scratch
        ],
        compiler_params=pltpu.CompilerParams(vmem_limit_bytes=48 * 1024 * 1024),
        cost_estimate=pl.CostEstimate(
            flops=int(weight * 1.1e9), bytes_accessed=1 << 16, transcendentals=0
        ),
    )(*operands, *after)


def swap(array, axis, bit):
    size = lax.axis_size(axis)
    return lax.ppermute(array, axis, [(i, i ^ bit) for i in range(size)])


def add_low(a, b):
    return (a.astype(F32) + b.astype(F32)).astype(BF16)


def gather_four(array):
    across = swap(array, "tensor", 2)
    beside = swap(array, "tensor", 1)
    return [array, beside, across, swap(across, "tensor", 1)]


def reduce_four(keep, send):
    got = swap(send, "tensor", 1)
    far = add_low(keep[1], got[1])
    return add_low(keep[0], got[0]), swap(far, "tensor", 2), far


def exchange(blocks):
    if len(blocks) > 8:
        return hyper_exchange(blocks)[0]
    return [blocks[0]] + [swap(b, "expert", k) for k, b in enumerate(blocks) if k]


def hyper_exchange(blocks, after=()):
    count = len(blocks)
    held = {k: [b] for k, b in enumerate(blocks)}
    steps = []
    bit = 1
    while bit < count:
        away = [k for k in sorted(held) if k & bit]
        sent = jnp.concatenate([b for k in away for b in held[k]], axis=0)
        got = swap(sent, "expert", bit)
        if bit == 1 and after:
            (got,) = fence([got], after)
        steps.append(got)
        size = blocks[0].shape[0]
        at = 0
        fresh = {}
        for k in away:
            pieces = [got[at + i * size : at + (i + 1) * size] for i in range(len(held[k]))]
            at += len(held[k]) * size
            fresh[k ^ bit] = held[k ^ bit] + pieces
        held = fresh
        bit *= 2
    return held[0], steps


ORDER = (0, 2, 4, 6, 1, 3, 5, 7)


def first_step(keep, got):
    _, rows, feats = keep.shape
    return call(
        sum_kernel, [((rows, feats), BF16)] * 4, [], keep, got, weight=1.0, smem=0
    )


def fence(arrays, after):
    count = len(arrays)
    return pl.pallas_call(
        fence_kernel,
        out_shape=[jax.ShapeDtypeStruct(a.shape, a.dtype) for a in arrays],
        in_specs=[pl.BlockSpec(memory_space=pl.ANY)] * (count + len(after)),
        out_specs=[pl.BlockSpec(memory_space=pl.ANY)] * count,
        input_output_aliases={i: i for i in range(count)},
    )(*arrays, *after)


def second_step(sums, after=()):
    parts = [swap(part, "expert", k) for k, part in zip((2, 4, 6), sums[1:])]
    (mine,) = call(
        last_sum_kernel, [(sums[0].shape, BF16)], [], sums[0], *parts, smem=0, after=after
    )
    return mine


def spread(mine):
    held = [mine] + [swap(mine, "expert", k) for k in (2, 4, 6)]
    return held + [swap(jnp.concatenate(held, axis=0), "expert", 1)]


def sum_experts(array):
    size = lax.axis_size("expert")
    array = array + swap(array, "expert", 1)
    if size == 8:
        return array + sum(swap(array, "expert", k) for k in (2, 4, 6))
    bit = 2
    while bit < size:
        array = array + swap(array, "expert", bit)
        bit *= 2
    return array


def on_device(
    tokens, cotangent, norm1_gain, w_query, w_key, w_value, w_attn_out, bias_table, norm2_gain,
    w_router, expert_in, expert_out, route, slot, segment, rel_bucket,
):
    length, feats = tokens.shape
    cols = cotangent.shape[1]
    heads = cols // HDIM
    experts = lax.axis_size("expert")
    cap = 2 * length // experts
    share = cap // 4
    rank = lax.axis_index("tensor").astype(jnp.int32)
    expert = lax.axis_index("expert").astype(jnp.int32)
    meta = jnp.stack([rank, expert])
    total = experts * cap
    direct = share % 16 == 0
    buckets = bias_table.shape[0]
    chunked = ORDER if experts == len(ORDER) else None

    w_query_t, w_key_t, w_value_t = w_query.T, w_key.T, w_value.T
    packed_rows = cols + -(-(experts + 3) // 16) * 16
    packed, *cot_blocks = call(
        first_kernel,
        [((packed_rows, feats), BF16)] + [((cols, cap), BF16)] * experts,
        [],
        meta, route, slot, cotangent.T, w_attn_out, w_router.T, norm2_gain,
        weight=2.0,
    )
    packed_parts = gather_four(packed)
    bucket = jnp.concatenate([rel_bucket, jnp.full((1,), -1, jnp.int32)])
    normed, query, key, value, probs, mixed = call(
        attend_kernel,
        [((length, feats), BF16)]
        + [((length, cols), BF16)] * 3
        + [((heads, length, length), F32), ((cols, length), BF16)],
        [((length, length), F32), ((length, feats), BF16), ((3, cols, feats), BF16),
         pltpu.SemaphoreType.DMA((4,))],
        tokens, w_query.T, w_key.T, w_value.T, norm1_gain, segment, bucket, bias_table.T,
        weight=7.0, smem=0, loose=(0, 1, 2, 3),
    )

    mixed_parts = gather_four(mixed)
    cot_arrived, _ = hyper_exchange(cot_blocks, (mixed, packed_parts[1], packed_parts[2]))
    cot_rows = gather_four(jnp.concatenate(cot_arrived, axis=0))
    residual, gate, router_probs, params, *row_blocks = call(
        residual_kernel,
        [
            ((length, feats), F32),
            ((length, 1), F32),
            ((length, experts), F32),
            ((experts + 8, feats), F32),
        ]
        + [((share, feats), BF16)] * experts,
        [((4, packed_rows - cols, cols), F32)],
        meta, route, slot, *mixed_parts, *packed_parts, tokens,
        weight=5.8,
    )
    cot_parts = gather_four(cotangent.T)
    arrived = exchange(row_blocks)
    groups = GROUPS if direct else 1
    group_size = experts // groups
    row_groups = []
    for g in range(groups):
        blocks = arrived[g * group_size : (g + 1) * group_size]
        if direct:
            (packed,) = call(
                functools.partial(assemble_kernel, count=group_size),
                [((group_size * share, feats), BF16)],
                [],
                *blocks,
                weight=1.0, smem=0, after=(cot_rows[2],),
            )
        else:
            packed = jnp.concatenate(blocks, axis=0)
        row_groups.append(gather_four(packed))

    if not direct:
        def assemble(parts, shape, turn):
            stacked = jnp.stack(parts).reshape(4, experts, *shape)
            stacked = stacked[rank ^ jnp.arange(4, dtype=jnp.int32)]
            return [jnp.transpose(stacked, turn).reshape(total, feats)]

        one = jnp.zeros((16, 128), BF16)
        row_groups = [assemble(row_groups[0], (share, feats), (1, 0, 2, 3)) + [one] * 3]
        cot_rows = assemble(cot_rows, (cols, cap), (1, 3, 0, 2)) + [one] * 3
    w_in, w_out = expert_in[0], expert_out[0]
    hidden_count = w_in.shape[1]
    part_rows = cols + 16
    count = total // groups
    x_shape = (group_size, 4, share, feats) if direct else (1, 1, 16, 128)
    c_shape = (4, cols, count) if direct else (1, 16, 128)
    acts, returning, kept = [], [], []
    for g in range(groups):
        rows_all, act, cots, d_hidden, keep, send = call(
            functools.partial(expert_kernel, first=g * group_size, direct=direct),
            [((count, feats), BF16), ((count, hidden_count), BF16), ((count, feats), BF16),
             ((count, hidden_count), BF16), ((2, part_rows, count), BF16),
             ((2, part_rows, count), BF16)],
            [(x_shape, BF16), (c_shape, BF16), ((4, part_rows, count), BF16)],
            meta, *row_groups[g], *cot_rows, w_in, w_out, params[:experts],
            weight=10.0,
        )
        near, far, _ = reduce_four(keep, send)
        whole = add_low(near, far)
        returning += [whole[:, k * cap : (k + 1) * cap] for k in range(group_size)]
        acts.append(act)
        kept += [act, cots, rows_all, d_hidden]

    def unite(blocks):
        return blocks if cap % 128 == 0 else [jnp.concatenate(blocks, axis=1)]

    keep_fwd, send_fwd = call(
        functools.partial(expert_out_kernel, groups=groups),
        [((2, cols, total), BF16)] * 2,
        [((4, cols, total), BF16)],
        meta, w_out, *acts,
        weight=2.9, after=(whole,),
    )
    (d_routed,) = call(
        functools.partial(combine_kernel, cap=cap),
        [((part_rows, length), BF16)],
        [((part_rows, total), BF16)],
        meta, route, slot, *unite(exchange(returning)), after=(keep_fwd,),
        weight=1.0,
    )
    routed_parts = gather_four(d_routed)

    near_fwd, far_fwd, met_fwd = reduce_four(keep_fwd, send_fwd)
    whole_fwd = add_low(near_fwd, far_fwd)
    fwd_arrived, fwd_steps = hyper_exchange(
        [whole_fwd[:, k * cap : (k + 1) * cap] for k in range(experts)]
    )
    came_fwd = unite(fwd_arrived)
    (block_out,) = call(
        functools.partial(block_out_kernel, cap=cap),
        [((length, cols), BF16)],
        [((cols, total), BF16), ((4, length, cols), F32)],
        meta, route, slot, residual, gate, *came_fwd,
        weight=1.2,
    )

    if chunked:
        size = 2 * cols // experts
        grad_outs = [((experts // 2, size, feats), BF16)] * 2
        chunk_scratch = ((experts, size, feats), BF16)
    else:
        grad_outs = [((cols, feats), BF16)] * 2
        chunk_scratch = ((16, 128), BF16)
    d_attn_cols, d_mixed, d_value, router_grad, gain2_grad, *first_grads = call(
        functools.partial(residual_back_kernel, chunked=chunked),
        [((length, cols), F32), ((length, cols), BF16), ((length, cols), BF16),
         ((experts, cols), F32), ((1, cols), F32)] + grad_outs,
        [((4, cols, length), BF16)] * 2 + [((4, length, cols), F32), chunk_scratch],
        meta, *routed_parts, *cot_parts, residual, gate, router_probs, route, params, mixed,
        w_attn_out, probs, normed, after=(met_fwd,),
        weight=8.0,
    )
    d_query, d_key, table_grad = call(
        functools.partial(attend_back_kernel, buckets=buckets),
        [((length, cols), BF16)] * 2 + [((8, 128), F32)],
        [],
        query, key, value, probs, d_mixed, bucket, smem=0,
        weight=7.0,
    )
    first_got = swap(first_grads[1], "expert", 1) if chunked else d_query
    second_grads = call(
        functools.partial(query_grads_kernel, chunked=chunked),
        grad_outs,
        [chunk_scratch],
        meta, normed, d_query, d_key, after=(first_got, whole_fwd),
        weight=1.5,
    )
    if chunked:
        first_sums = first_step(first_grads[0], first_got)
        second_got = swap(second_grads[1], "expert", 1)
        second_sums = first_step(second_grads[0], second_got)
        first_after = (first_sums[1], second_grads[0])
    else:
        first_after = ()
    wide = -(-(cols + 2) // 128) * 128
    keep_in, send_in = call(
        normed_back_kernel,
        [((2, length, wide), BF16)] * 2,
        [((4, length, wide), BF16)],
        meta, tokens, norm1_gain, d_query, d_key, d_value, w_query.T, w_key.T, w_value.T,
        weight=3.0, after=first_after,
    )
    near_in, far_in, met_in = reduce_four(keep_in, send_in)
    if chunked:
        first_mine = second_step(first_sums, (second_got,))
        second_mine = second_step(second_sums)
        mine_after = (first_mine, second_sums[1])
    else:
        mine_after = ()
    small_rows = 16 + -(-experts // 8) * 8
    input_grad, small = call(
        input_kernel,
        [((length, cols), F32), ((small_rows, wide), F32)],
        [((4, length, cols), F32), ((4, 1, cols), F32)],
        meta, tokens, norm1_gain, d_attn_cols, near_in, far_in, gain2_grad, table_grad,
        router_grad,
        weight=1.0, after=(*mine_after, fwd_steps[0]),
    )

    kept = fence(kept, (met_in,))
    expert_out_grad = sum(dot_tn(kept[4 * g], kept[4 * g + 1]) for g in range(groups))
    expert_in_grad = sum(dot_tn(kept[4 * g + 2], kept[4 * g + 3]) for g in range(groups))
    small = sum_experts(small)
    gain1_parts = jnp.stack([small[0, :cols]] + [swap(small[:8], "tensor", j)[0, :cols] for j in (1, 2, 3)])
    gain1_grad = gain1_parts[rank ^ jnp.arange(4, dtype=jnp.int32)]
    if chunked:
        finish = functools.partial(finish_kernel, order=ORDER)
        outs = [((cols, feats), F32)] * 2
        attn_grad, value_grad = call(
            finish, outs, [chunk_scratch], meta, *spread(first_mine), weight=1.6,
            after=(fwd_steps[1],),
        )
        query_grad, key_grad = call(
            finish, outs, [chunk_scratch], meta, *spread(second_mine), weight=1.6,
            after=(attn_grad, input_grad, block_out, gain1_grad),
        )
    else:
        attn_grad, value_grad, query_grad, key_grad = [
            g.astype(F32) for g in lax.psum((*first_grads, *second_grads), "expert")
        ]
    return (
        block_out,
        input_grad,
        gain1_grad.reshape(feats),
        query_grad.T,
        key_grad.T,
        value_grad.T,
        attn_grad,
        small[8 : 8 + heads, :buckets].T,
        small[4, :cols],
        small[16 : 16 + experts, :cols].T,
        expert_in_grad[None],
        expert_out_grad[None],
    )


def solution(mesh):
    return jax.shard_map(
        on_device,
        mesh=mesh,
        in_specs=(
            P("expert", None),
            P("expert", "tensor"),
            P(),
            P(None, "tensor"),
            P(None, "tensor"),
            P(None, "tensor"),
            P("tensor", None),
            P(None, "tensor"),
            P("tensor"),
            P("tensor", None),
            P("expert", None, "tensor"),
            P("expert", "tensor", None),
            P("expert"),
            P("expert"),
            P("expert"),
            P(),
        ),
        out_specs=(
            P("expert", "tensor"),
            P("expert", "tensor"),
            P(),
            P(None, "tensor"),
            P(None, "tensor"),
            P(None, "tensor"),
            P("tensor", None),
            P(None, "tensor"),
            P("tensor"),
            P("tensor", None),
            P("expert", None, "tensor"),
            P("expert", "tensor", None),
        ),
        check_vma=False,
    )
```

```python
import functools

import jax
import jax.numpy as jnp
from jax import lax
from jax.experimental import pallas as pl
from jax.experimental.pallas import tpu as pltpu
from jax.sharding import PartitionSpec as P

HDIM = 64
EPSILON = 1e-06
MASKED_SCORE = -1e30
SCORE_SCALE = 0.125
PRECISE = lax.Precision.HIGHEST
F32 = jnp.float32
BF16 = jnp.bfloat16
GELU_C = 0.7978845608028654
GELU_A = 0.044715
CHUNK = 128
GROUPS = 1


def dot_nn(a, b, precision=None):
    return lax.dot_general(
        a, b, (((1,), (0,)), ((), ())), precision=precision, preferred_element_type=F32
    )


def dot_nt(a, b, precision=None):
    return lax.dot_general(
        a, b, (((1,), (1,)), ((), ())), precision=precision, preferred_element_type=F32
    )


def dot_tn(a, b, precision=None):
    return lax.dot_general(
        a, b, (((0,), (0,)), ((), ())), precision=precision, preferred_element_type=F32
    )


def row_scale(rows):
    return lax.rsqrt(jnp.mean(rows * rows, axis=1, keepdims=True) + EPSILON)


def bucket_marks(bucket, count):
    width = bucket.shape[0]
    return lax.broadcasted_iota(jnp.int32, (count, width), 0) == bucket[...].reshape(1, width)


def in_order(blocks, rank, place, axis):
    for j, block in enumerate(blocks):
        place[rank ^ j] = block[...]
    return jnp.concatenate([place[r] for r in range(len(blocks))], axis=axis)


def as_column(row):
    return jnp.broadcast_to(row, (128, row.shape[1])).T[:, 0:1]


def softmax_rows(logits):
    shifted = jnp.exp(logits - jnp.max(logits, axis=1, keepdims=True))
    return shifted / jnp.sum(shifted, axis=1, keepdims=True)


def attend_kernel(
    tokens, w_query, w_key, w_value, gain, segment, bucket, table,
    normed_out, query_out, key_out, value_out, probs_out, mixed_out,
    band,
):
    length = tokens.shape[0]
    width = 2 * length
    heads = query_out.shape[1] // HDIM
    marks = bucket_marks(bucket, table.shape[1])
    table_rows = jnp.broadcast_to(table[...][:, None, :], (heads, 128, table.shape[1]))
    bases = []
    for h in range(heads):
        offsets = jnp.sum(
            jnp.where(marks, table_rows[h].T[:, 0:1], 0.0), axis=0, keepdims=True
        )
        bases.append(
            jnp.concatenate(
                [offsets] + [pltpu.roll(offsets, r, 1) for r in range(1, 8)], axis=0
            )
        )
    seg_row = segment[...].reshape(1, length)
    seg_col = as_column(seg_row)
    rows = tokens[...].astype(F32)
    normed = (rows * row_scale(rows) * gain[...].reshape(1, rows.shape[1])).astype(BF16)
    normed_out[...] = normed
    query = dot_nt(normed, w_query[...]).astype(BF16)
    key = dot_nt(normed, w_key[...]).astype(BF16)
    query_out[...] = query
    key_out[...] = key
    value_out[...] = dot_nt(normed, w_value[...]).astype(BF16)
    value_turned = dot_nt(w_value[...], normed).astype(BF16)
    for h in range(heads):
        cols = slice(h * HDIM, (h + 1) * HDIM)
        for b in range(length // 8):
            turned = pltpu.roll(bases[h], (length + 1 + 8 * b) % width, 1)
            band[8 * b : 8 * b + 8, :] = turned[:, :length]
        for c in range(0, length, CHUNK):
            span = slice(c, c + CHUNK)
            scores = dot_nt(query[span, cols], key[:, cols]) * SCORE_SCALE + band[span, :]
            scores = jnp.where(seg_col[span, :] == seg_row, scores, MASKED_SCORE)
            probs = softmax_rows(scores)
            probs_out[h, span, :] = probs
            mixed_out[cols, span] = dot_nt(value_turned[cols, :], probs.astype(BF16)).astype(BF16)


def dispatch(code, rows, outs, transposed=False):
    share = outs[0].shape[0]
    for k, out in enumerate(outs):
        ids = lax.broadcasted_iota(jnp.int32, (share, code.shape[1]), 0) + k * share
        marks = jnp.where(ids == code[...], 1.0, 0.0).astype(BF16)
        product = dot_nt if transposed else dot_nn
        out[...] = product(marks, rows).astype(BF16)


def slot_codes(meta, route, slot, size):
    count = route.shape[0]
    return ((route[...] ^ meta[1]) * size + slot[...]).reshape(1, count)


def first_kernel(
    meta, route, slot, cotangent, w_attn_out, w_router, gain, packed_out, *outs
):
    cap = outs[0].shape[1]
    count = len(outs) * cap
    code = slot_codes(meta, route, slot, cap)
    ids = lax.broadcasted_iota(jnp.int32, (count, code.shape[1]), 0)
    marks = jnp.where(ids == code, 1.0, 0.0).astype(BF16)
    placed = dot_nt(cotangent[...], marks).astype(BF16)
    for k, out in enumerate(outs):
        out[...] = placed[:, k * cap : (k + 1) * cap]
    rows, feats = w_attn_out.shape
    experts = w_router.shape[0]
    packed_out[:rows, :] = w_attn_out[...]
    length = cotangent.shape[1]
    top = packed_out.shape[0] - rows
    packed_out[top:, :length] = cotangent[...]
    packed_out[top:, length:] = jnp.zeros((rows, feats - length), BF16)
    line = gain[...].reshape(1, rows)
    high = line.astype(BF16)
    rest = line - high.astype(F32)
    mid = rest.astype(BF16)
    low = (rest - mid.astype(F32)).astype(BF16)
    pad = top - rows - experts - 3
    extra = [w_router[...].astype(F32)] + [p.astype(F32) for p in (high, mid, low)]
    extra = jnp.concatenate(extra + [jnp.zeros((pad, rows), F32)], axis=0)
    wide = jnp.concatenate([extra, jnp.zeros((extra.shape[0], feats - rows), F32)], axis=1)
    packed_out[rows:top, :] = wide.astype(BF16)


def dispatch(code, rows, outs):
    share = outs[0].shape[0]
    for k, out in enumerate(outs):
        ids = lax.broadcasted_iota(jnp.int32, (share, code.shape[1]), 0) + k * share
        marks = jnp.where(ids == code, 1.0, 0.0).astype(BF16)
        out[...] = dot_nn(marks, rows).astype(BF16)


def residual_kernel(
    meta, route, slot, m0, m1, m2, m3, w0, w1, w2, w3, tokens,
    residual_out, gate_out, probs_out, params_out, turned_out, *rest,
):
    outs, place, cot_place = rest[:-2], rest[-2], rest[-1]
    share = outs[0].shape[0]
    experts = probs_out.shape[1]
    cols = m0.shape[0]
    for j, w in enumerate((w0, w1, w2, w3)):
        place[meta[0] ^ j] = w[cols : w.shape[0] - cols, :cols].astype(F32)
        cot_place[meta[0] ^ j] = w[w.shape[0] - cols :, : tokens.shape[0]]
    for r in range(4):
        turned_out[r * cols : (r + 1) * cols, :] = cot_place[r]
    params = jnp.concatenate([place[r] for r in range(4)], axis=1)
    router = params[:experts]
    gain = params[experts : experts + 1]
    for i in (1, 2):
        gain = gain + params[experts + i : experts + i + 1]
    params_out[...] = jnp.concatenate([router, jnp.broadcast_to(gain, (8, gain.shape[1]))], axis=0)
    residual = tokens[...].astype(F32)
    for m, w in ((m0, w0), (m1, w1), (m2, w2), (m3, w3)):
        residual = residual + dot_tn(m[...], w[:cols, :])
    residual_out[...] = residual
    normed = residual * row_scale(residual) * gain
    part = slot[...] - meta[0] * share
    code = jnp.where(
        (part >= 0) & (part < share), (route[...] ^ meta[1]) * share + part, -1
    ).reshape(1, part.shape[0])
    dispatch(code, normed.astype(BF16), outs)
    probs = softmax_rows(dot_nt(normed, router, PRECISE))
    probs_out[...] = probs
    lanes = lax.broadcasted_iota(jnp.int32, probs.shape, 1)
    where = as_column(route[...].reshape(1, part.shape[0]))
    gate_out[...] = jnp.sum(jnp.where(lanes == where, probs, 0.0), axis=1, keepdims=True)


def assemble_kernel(*refs, count):
    out = refs[-1]
    size = refs[0].shape[0]
    for i, block in enumerate(refs[:count]):
        out[i * size : (i + 1) * size, :] = block[...]


def expert_kernel(
    meta, x0, x1, x2, x3, c0, c1, c2, c3, w_in, w_out, router,
    rows_out, act_out, cots_out, d_hidden_out, keep_out, send_out,
    x_all, c_all, part_all, *, first, direct,
):
    rank, expert = meta[0], meta[1]
    ranks = 4
    total = rows_out.shape[0]
    feats = rows_out.shape[1]
    cols = feats // ranks
    if direct:
        sources, _, share, _ = x_all.shape
        cap = ranks * share
        for j, (x, c) in enumerate(((x0, c0), (x1, c1), (x2, c2), (x3, c3))):
            for s in range(sources):
                x_all[s, rank ^ j] = x[s * share : (s + 1) * share, :]
                at = (first + s) * cols
                c_all[rank ^ j, :, s * cap : (s + 1) * cap] = c[at : at + cols, :]
        step = 256 // cap
    for i in range(total // 256):
        span = slice(i * 256, (i + 1) * 256)
        if direct:
            rows = x_all[i * step : (i + 1) * step].reshape(256, feats)
            turned = jnp.concatenate([c_all[r, :, span] for r in range(ranks)], axis=0)
            cots = turned.astype(F32).T.astype(BF16)
        else:
            rows = x0[span, :]
            cots = c0[span, :]
        rows_out[span, :] = rows
        probs = softmax_rows(dot_nt(rows, router[...].astype(BF16)))
        lanes = lax.broadcasted_iota(jnp.int32, probs.shape, 1)
        gate = jnp.sum(jnp.where(lanes == expert, probs, 0.0), axis=1, keepdims=True)
        cots_out[span, :] = (gate * cots.astype(F32)).astype(BF16)
        hidden = dot_nn(rows, w_in[...])
        pull = dot_nt(cots, w_out[...])
        bent = jnp.tanh(GELU_C * (hidden + GELU_A * hidden * hidden * hidden))
        act = (0.5 * hidden * (1.0 + bent)).astype(BF16)
        act_out[span, :] = act
        slope = 0.5 * (1.0 + bent) + 0.5 * hidden * (1.0 - bent * bent) * (
            GELU_C * (1.0 + 3.0 * GELU_A * hidden * hidden)
        )
        d_hidden = (gate * pull * slope).astype(BF16)
        d_hidden_out[span, :] = d_hidden
        d_gate = jnp.sum(pull * act.astype(F32), axis=1, keepdims=True)
        d_part = dot_nt(w_in[...], d_hidden).astype(BF16)
        tail = jnp.broadcast_to(d_gate, (256, 128)).T[: part_all.shape[1] - cols].astype(BF16)
        for r in range(ranks):
            j = rank ^ r
            place = (j % 2) * 2 + j // 2
            part_all[place, :cols, span] = d_part[r * cols : (r + 1) * cols, :]
            part_all[place, cols:, span] = tail
    keep_out[...] = part_all[0:2]
    send_out[...] = part_all[2:4]


def expert_out_kernel(meta, w_out, *refs, groups):
    acts, (keep_out, send_out, part_all) = refs[:groups], refs[-3:]
    rank = meta[0]
    ranks = 4
    cols = part_all.shape[1]
    at = 0
    for act in acts:
        for i in range(0, act.shape[0], 256):
            part = dot_nn(act[i : i + 256, :], w_out[...]).T.astype(BF16)
            for r in range(ranks):
                j = rank ^ r
                part_all[(j % 2) * 2 + j // 2, :, at : at + 256] = part[r * cols : (r + 1) * cols]
            at += 256
    keep_out[...] = part_all[0:2]
    send_out[...] = part_all[2:4]


def slot_marks(meta, route, slot, cap, count):
    code = slot_codes(meta, route, slot, cap)
    ids = lax.broadcasted_iota(jnp.int32, (code.shape[1], count), 1)
    return jnp.where(ids == as_column(code), 1.0, 0.0).astype(BF16)


def fence_kernel(*refs):
    del refs


def side_by_side(blocks, came):
    size = blocks[0].shape[1]
    for k, block in enumerate(blocks):
        came[:, k * size : (k + 1) * size] = block[...]
    return came[...]


def combine_kernel(meta, route, slot, *rest, cap):
    *blocks, _, out, came = rest
    marks = slot_marks(meta, route, slot, cap, came.shape[1])
    out[...] = dot_nt(side_by_side(blocks, came), marks).astype(BF16)


def block_out_kernel(meta, route, slot, residual, gate, *rest, cap):
    *blocks, block_out, came, place = rest
    rank = meta[0]
    cols = block_out.shape[1]
    marks = slot_marks(meta, route, slot, cap, came.shape[1])
    returned = dot_nt(marks, side_by_side(blocks, came))
    for r in range(4):
        place[r] = residual[:, r * cols : (r + 1) * cols]
    block_out[...] = (place[rank] + gate[...] * returned).astype(BF16)


def residual_back_kernel(
    meta, r0, r1, r2, r3, residual, gate, probs, route, params, cotangent, mixed, w_attn_out,
    attn_probs, normed_one, _, d_attn_cols_out, d_mixed_out, d_value_out, router_grad_out,
    gain_grad_out, *rest,
):
    attn_grad_out, value_grad_out, place, place_f32 = rest
    rank, expert = meta[0], meta[1]
    experts = probs.shape[1]
    feats = residual.shape[1]
    cols = feats // 4
    length = residual.shape[0]
    router = params[:experts, :]
    gain = params[experts : experts + 1, :]
    for j, r in enumerate((r0, r1, r2, r3)):
        place[rank ^ j] = r[:cols, :]
    d_gate = as_column(r0[cols : cols + 1, :].astype(F32))
    d_routed = jnp.concatenate([place[r] for r in range(4)], axis=0).astype(F32).T
    res = residual[...]
    scale = row_scale(res)
    lanes = lax.broadcasted_iota(jnp.int32, probs.shape, 1)
    onehot = jnp.where(lanes == as_column(route[...].reshape(1, length)), 1.0, 0.0)
    d_logits = d_gate * probs[...] * (onehot - gate[...])
    d_normed = d_routed + dot_nn(d_logits, router, PRECISE)
    normed = res * scale * gain
    router_grad = dot_tn(d_logits, normed, PRECISE)
    gain_grad = jnp.sum(d_normed * res * scale, axis=0, keepdims=True)
    cross = jnp.sum(gain * res * d_normed, axis=1, keepdims=True)
    d_residual = (
        cotangent[...].astype(F32).T
        + scale * gain * d_normed
        - res * (scale * scale * scale * cross * (1.0 / feats))
    )
    for r in range(4):
        own = slice(r * cols, (r + 1) * cols)
        place_f32[r] = d_residual[:, own]

        @pl.when(rank == r)
        def _():
            router_grad_out[...] = router_grad[:, own]
            gain_grad_out[...] = gain_grad[:, own]

    d_attn_cols_out[...] = place_f32[rank]
    d_attn = d_residual.astype(BF16)
    attn_grad_out[...] = dot_nn(mixed[...], d_attn).astype(BF16)
    d_mixed = dot_nt(d_attn, w_attn_out[...]).astype(BF16)
    d_mixed_out[...] = d_mixed
    for h in range(cols // HDIM):
        own = slice(h * HDIM, (h + 1) * HDIM)
        total = jnp.zeros((length, HDIM), F32)
        for c in range(0, length, CHUNK):
            span = slice(c, c + CHUNK)
            total = total + dot_tn(attn_probs[h, span, :].astype(BF16), d_mixed[span, own])
        d_value_out[:, own] = total.astype(BF16)
    value_grad_out[...] = dot_tn(d_value_out[...], normed_one[...]).astype(BF16)


def attend_back_kernel(
    query, key, value, probs, d_mixed, bucket, d_query, d_key, table_out, *, buckets
):
    length = query.shape[0]
    width = 2 * length
    heads = query.shape[1] // HDIM
    marks = bucket_marks(bucket, buckets)
    zeros = jnp.zeros((8, width - length), F32)
    table_out[...] = jnp.zeros(table_out.shape, F32)
    for h in range(heads):
        own = slice(h * HDIM, (h + 1) * HDIM)
        dk = jnp.zeros((length, HDIM), F32)
        diagonals = jnp.zeros((8, width), F32)
        for c in range(0, length, CHUNK):
            span = slice(c, c + CHUNK)
            weights = probs[h, span, :]
            d_probs = dot_nt(d_mixed[span, own], value[:, own])
            inner = jnp.sum(d_probs * weights, axis=1, keepdims=True)
            d_scores = weights * (d_probs - inner)
            for b in range(CHUNK // 8):
                piece = jnp.concatenate([d_scores[8 * b : 8 * b + 8, :], zeros], axis=1)
                diagonals = diagonals + pltpu.roll(piece, (length - 1 - c - 8 * b) % width, 1)
            low = d_scores.astype(BF16)
            d_query[span, own] = (dot_nn(low, key[:, own]) * SCORE_SCALE).astype(BF16)
            dk = dk + dot_tn(low, query[span, own])
        d_key[:, own] = (dk * SCORE_SCALE).astype(BF16)
        line = diagonals[0:1]
        for r in range(1, 8):
            line = line + pltpu.roll(diagonals[r : r + 1], width - r, 1)
        table_col = jnp.sum(jnp.where(marks, line, 0.0), axis=1, keepdims=True)
        table_out[h : h + 1, :buckets] = jnp.broadcast_to(table_col, (buckets, 128)).T[0:1, :]


def put_split(out, at, row, value):
    high = value.astype(BF16).astype(F32)
    out[row : row + 1, at : at + value.shape[1]] = high
    out[row + 8 : row + 9, at : at + value.shape[1]] = value - high


def query_back_kernel(
    meta, tokens, gain, normed, d_query, d_key, d_value, w_query, w_key, w_value, gain2_grad,
    table_grad, router_grad, _, *rest, chunked, heads, buckets,
):
    keep_in, send_in, gain1_out, first_out, second_out, place, chunk_place, pack = rest
    rank, expert = meta[0], meta[1]
    length, feats = tokens.shape
    cols = feats // 4
    normed_rows = normed[...]
    query_grad = dot_tn(d_query[...], normed_rows).astype(BF16)
    key_grad = dot_tn(d_key[...], normed_rows).astype(BF16)
    d_normed = (
        dot_nn(d_query[...], w_query[...])
        + dot_nn(d_key[...], w_key[...])
        + dot_nn(d_value[...], w_value[...])
    )
    rows = tokens[...].astype(F32)
    product = d_normed * rows
    gain1_grad = jnp.sum(product * row_scale(rows), axis=0, keepdims=True)
    gain1_out[...] = jnp.broadcast_to(gain1_grad, gain1_out.shape)
    if chunked:
        pack[...] = jnp.zeros(pack.shape, F32)
        put_split(pack, 0, 0, gain1_grad)
        put_split(pack, 0, 1, gain2_grad[...])
        for h in range(heads):
            put_split(pack, 256 * h, 2, table_grad[h : h + 1, :])
        for e in range(router_grad.shape[0]):
            put_split(pack, 256 * (e % 3), 3 + e // 3, router_grad[e : e + 1, :])
        small = pack[...].astype(BF16)
        both = jnp.concatenate([query_grad, key_grad], axis=0)
        count = len(chunked)
        size = both.shape[0] // count
        for c in range(count):
            chunk_place[c ^ expert] = both[c * size : (c + 1) * size, :]
        for i, k in enumerate(chunked):
            out = first_out if i < count // 2 else second_out
            at = (i % (count // 2)) * size
            out[at : at + size, :] = chunk_place[k]
        for out in (first_out, second_out):
            out[out.shape[0] - 16 :, :] = small
    else:
        first_out[...] = query_grad
        second_out[...] = key_grad
    cross = jnp.sum(product * gain[...].reshape(1, feats), axis=1, keepdims=True)
    high = cross.astype(BF16).astype(F32)
    low = cross - high
    lanes = lax.broadcasted_iota(jnp.int32, (length, place.shape[2] - cols), 1)
    extra = jnp.where(lanes == 0, high, jnp.where(lanes == 1, low, 0.0)).astype(BF16)
    for r in range(4):
        j = rank ^ r
        own = d_normed[:, r * cols : (r + 1) * cols].astype(BF16)
        place[(j % 2) * 2 + j // 2] = jnp.concatenate([own, extra], axis=1)
    keep_in[...] = place[0:2]
    send_in[...] = place[2:4]


def input_kernel(
    meta, tokens, gain, d_attn_cols, first, second, *rest
):
    *_, out, place, gain_place = rest
    rank = meta[0]
    feats = tokens.shape[1]
    cols = feats // 4
    rows = tokens[...].astype(F32)
    scale = row_scale(rows)
    both = first[...].astype(F32) + second[...].astype(F32)
    cross = both[:, cols : cols + 1] + both[:, cols + 1 : cols + 2]
    gain_row = gain[...].reshape(1, feats)
    for r in range(4):
        place[r] = rows[:, r * cols : (r + 1) * cols]
        gain_place[r] = gain_row[:, r * cols : (r + 1) * cols]
    own = both[:, :cols]
    own_rows = place[rank]
    out[...] = (
        d_attn_cols[...]
        + scale * gain_place[rank] * own
        - own_rows * (scale * scale * scale * cross * (1.0 / feats))
    )


def add_small(a, b):
    at = a.shape[0] - 16
    total = (
        a[at : at + 8, :].astype(F32)
        + b[at : at + 8, :].astype(F32)
        + a[at + 8 :, :].astype(F32)
        + b[at + 8 :, :].astype(F32)
    )
    high = total.astype(BF16).astype(F32)
    return total, jnp.concatenate([high, total - high], axis=0).astype(BF16)


def sum_kernel(keep, got, keep_out, send_out):
    half = (keep.shape[0] - 16) // 2
    total = (keep[: 2 * half, :].astype(F32) + got[: 2 * half, :].astype(F32)).astype(BF16)
    _, small = add_small(keep, got)
    keep_out[:half, :] = total[:half]
    send_out[:half, :] = total[half:]
    keep_out[half:, :] = small
    send_out[half:, :] = small


def last_sum_kernel(keep, got, mine_out, small_out, gain1_out):
    size = mine_out.shape[0]
    mine_out[...] = (keep[:size, :].astype(F32) + got[:size, :].astype(F32)).astype(BF16)
    total, _ = add_small(keep, got)
    small_out[...] = total
    gain1_out[...] = jnp.broadcast_to(total[0:1], gain1_out.shape)


def finish_kernel(
    meta, mine, second, other, small, attn, value, *rest, order, heads
):
    attn_out, value_out, first_out, second_out, gain2_out, table_out, router_out, place = rest[-8:]
    attn_out[...] = attn[...].astype(F32)
    value_out[...] = value[...].astype(F32)
    expert = meta[1]
    count = len(order)
    size = mine.shape[0] // 2
    quarter = count // 4
    for i in range(count):
        block, at = (
            (mine, i)
            if i < quarter
            else (second, i - quarter) if i < 2 * quarter else (other, i - 2 * quarter)
        )
        place[order[i]] = block[at * size : (at + 1) * size, :]
    rows = first_out.shape[0]
    for c in range(count):
        chunk = place[c ^ expert].astype(F32)
        start = c * size
        if start < rows:
            first_out[start : start + size, :] = chunk
        else:
            second_out[start - rows : start - rows + size, :] = chunk
    cols = gain2_out.shape[1]
    gain2_out[...] = small[1:2, :cols]
    for h in range(heads):
        table_out[h : h + 1, :] = small[2:3, 256 * h : 256 * h + table_out.shape[1]]
    for e in range(router_out.shape[0]):
        at = 256 * (e % 3)
        router_out[e : e + 1, :] = small[3 + e // 3 : 4 + e // 3, at : at + cols]


def fetching(kernel, smem, fetch):
    def run(*refs):
        scalars, far = refs[:smem], refs[smem : smem + fetch]
        rest, near, sems = refs[smem + fetch : -fetch - 1], refs[-fetch - 1 : -1], refs[-1]
        copies = [
            pltpu.make_async_copy(a, b, sems.at[i]) for i, (a, b) in enumerate(zip(far, near))
        ]
        for copy in copies:
            copy.start()
        for copy in copies:
            copy.wait()
        kernel(*scalars, *near, *rest)

    return run


def call(kernel, outs, scratch, *operands, weight=1.0, smem=1, fetch=0, after=()):
    specs = []
    for i in range(len(operands)):
        if i < smem:
            specs.append(pl.BlockSpec(memory_space=pltpu.SMEM))
        elif i < smem + fetch:
            specs.append(pl.BlockSpec(memory_space=pltpu.HBM))
        else:
            specs.append(pl.BlockSpec(memory_space=pltpu.VMEM))
    specs += [pl.BlockSpec(memory_space=pl.ANY)] * len(after)
    scratch_shapes = [pltpu.VMEM(shape, kind) for shape, kind in scratch]
    if fetch:
        kernel = fetching(kernel, smem, fetch)
        scratch_shapes += [pltpu.VMEM(a.shape, a.dtype) for a in operands[smem : smem + fetch]]
        scratch_shapes.append(pltpu.SemaphoreType.DMA((fetch,)))
    return pl.pallas_call(
        kernel,
        out_shape=[jax.ShapeDtypeStruct(shape, kind) for shape, kind in outs],
        in_specs=specs,
        out_specs=[pl.BlockSpec(memory_space=pltpu.VMEM)] * len(outs),
        scratch_shapes=scratch_shapes,
        compiler_params=pltpu.CompilerParams(vmem_limit_bytes=28 * 1024 * 1024),
        cost_estimate=pl.CostEstimate(
            flops=int(weight * 1.1e9), bytes_accessed=1 << 16, transcendentals=0
        ),
    )(*operands, *after)


def swap(array, axis, bit):
    size = lax.axis_size(axis)
    return lax.ppermute(array, axis, [(i, i ^ bit) for i in range(size)])


def add_low(a, b):
    return (a.astype(F32) + b.astype(F32)).astype(BF16)


def gather_four(array):
    across = swap(array, "tensor", 2)
    beside = swap(array, "tensor", 1)
    return [array, beside, across, swap(across, "tensor", 1)]


def reduce_four(keep, send):
    got = swap(send, "tensor", 1)
    far = add_low(keep[1], got[1])
    return add_low(keep[0], got[0]), swap(far, "tensor", 2), far


def exchange(blocks):
    if len(blocks) > 8:
        return hyper_exchange(blocks)[0]
    return [blocks[0]] + [swap(b, "expert", k) for k, b in enumerate(blocks) if k]


def hyper_exchange(blocks, after=()):
    count = len(blocks)
    held = {k: [b] for k, b in enumerate(blocks)}
    steps = []
    bit = 1
    while bit < count:
        away = [k for k in sorted(held) if k & bit]
        sent = jnp.concatenate([b for k in away for b in held[k]], axis=0)
        got = swap(sent, "expert", bit)
        if bit == 1 and after:
            (got,) = fence([got], after)
        steps.append(got)
        size = blocks[0].shape[0]
        at = 0
        fresh = {}
        for k in away:
            pieces = [got[at + i * size : at + (i + 1) * size] for i in range(len(held[k]))]
            at += len(held[k]) * size
            fresh[k ^ bit] = held[k ^ bit] + pieces
        held = fresh
        bit *= 2
    return held[0], steps


ORDER = (0, 4, 2, 6, 1, 5, 3, 7)


def halve(keep, send):
    feats = keep.shape[1]
    for bit in (1, 2):
        rows = (keep.shape[0] - 16) // 2 + 16
        keep, send = call(
            sum_kernel, [((rows, feats), BF16)] * 2, [], keep, swap(send, "expert", bit), smem=0
        )
    return call(
        last_sum_kernel,
        [((keep.shape[0] - 16, feats), BF16), ((8, feats), F32), ((8, feats), F32)],
        [],
        keep, swap(send, "expert", 4), smem=0,
    )


def fence(arrays, after):
    count = len(arrays)
    return pl.pallas_call(
        fence_kernel,
        out_shape=[jax.ShapeDtypeStruct(a.shape, a.dtype) for a in arrays],
        in_specs=[pl.BlockSpec(memory_space=pl.ANY)] * (count + len(after)),
        out_specs=[pl.BlockSpec(memory_space=pl.ANY)] * count,
        input_output_aliases={i: i for i in range(count)},
    )(*arrays, *after)


def on_device(
    tokens, cotangent, norm1_gain, w_query, w_key, w_value, w_attn_out, bias_table, norm2_gain,
    w_router, expert_in, expert_out, route, slot, segment, rel_bucket,
):
    length, feats = tokens.shape
    cols = cotangent.shape[1]
    heads = cols // HDIM
    experts = lax.axis_size("expert")
    cap = 2 * length // experts
    share = cap // 4
    rank = lax.axis_index("tensor").astype(jnp.int32)
    expert = lax.axis_index("expert").astype(jnp.int32)
    meta = jnp.stack([rank, expert])
    total = experts * cap
    direct = share % 16 == 0
    buckets = bias_table.shape[0]
    chunked = ORDER if experts == len(ORDER) else None

    w_query_t, w_key_t, w_value_t = w_query.T, w_key.T, w_value.T
    packed_rows = 2 * cols + -(-(experts + 3) // 16) * 16
    packed, *cot_blocks = call(
        first_kernel,
        [((packed_rows, feats), BF16)] + [((cols, cap), BF16)] * experts,
        [],
        meta, route, slot, cotangent.T, w_attn_out, w_router.T, norm2_gain,
        weight=2.0, fetch=6,
    )
    packed_parts = gather_four(packed)
    bucket = jnp.concatenate([rel_bucket, jnp.full((1,), -1, jnp.int32)])
    normed, query, key, value, probs, mixed = call(
        attend_kernel,
        [((length, feats), BF16)]
        + [((length, cols), BF16)] * 3
        + [((heads, length, length), F32), ((cols, length), BF16)],
        [((length, length), F32)],
        tokens, w_query.T, w_key.T, w_value.T, norm1_gain, segment, bucket, bias_table.T,
        weight=7.0, smem=0, fetch=8,
    )

    mixed_parts = gather_four(mixed)
    cot_arrived, _ = hyper_exchange(cot_blocks, (mixed, packed_parts[1], packed_parts[2]))
    residual, gate, router_probs, params, cot_turned, *row_blocks = call(
        residual_kernel,
        [
            ((length, feats), F32),
            ((length, 1), F32),
            ((length, experts), F32),
            ((experts + 8, feats), F32),
            ((feats, length), BF16),
        ]
        + [((share, feats), BF16)] * experts,
        [((4, packed_rows - 2 * cols, cols), F32), ((4, cols, length), BF16)],
        meta, route, slot, *mixed_parts, *packed_parts, tokens,
        weight=5.8,
    )
    (cot_own,) = fence([jnp.concatenate(cot_arrived, axis=0)], (residual,))
    cot_rows = gather_four(cot_own)
    arrived = exchange(row_blocks)
    groups = GROUPS if direct else 1
    group_size = experts // groups
    row_groups = []
    for g in range(groups):
        blocks = arrived[g * group_size : (g + 1) * group_size]
        if direct:
            (packed,) = call(
                functools.partial(assemble_kernel, count=group_size),
                [((group_size * share, feats), BF16)],
                [],
                *blocks,
                weight=1.0, smem=0, after=(cot_rows[2],),
            )
        else:
            packed = jnp.concatenate(blocks, axis=0)
        row_groups.append(gather_four(packed))

    if not direct:
        def assemble(parts, shape, turn):
            stacked = jnp.stack(parts).reshape(4, experts, *shape)
            stacked = stacked[rank ^ jnp.arange(4, dtype=jnp.int32)]
            return [jnp.transpose(stacked, turn).reshape(total, feats)]

        one = jnp.zeros((16, 128), BF16)
        row_groups = [assemble(row_groups[0], (share, feats), (1, 0, 2, 3)) + [one] * 3]
        cot_rows = assemble(cot_rows, (cols, cap), (1, 3, 0, 2)) + [one] * 3
    w_in, w_out = expert_in[0], expert_out[0]
    hidden_count = w_in.shape[1]
    part_rows = cols + 16
    count = total // groups
    x_shape = (group_size, 4, share, feats) if direct else (1, 1, 16, 128)
    c_shape = (4, cols, count) if direct else (1, 16, 128)
    acts, returning, kept = [], [], []
    for g in range(groups):
        rows_all, act, cots, d_hidden, keep, send = call(
            functools.partial(expert_kernel, first=g * group_size, direct=direct),
            [((count, feats), BF16), ((count, hidden_count), BF16), ((count, feats), BF16),
             ((count, hidden_count), BF16), ((2, part_rows, count), BF16),
             ((2, part_rows, count), BF16)],
            [(x_shape, BF16), (c_shape, BF16), ((4, part_rows, count), BF16)],
            meta, *row_groups[g], *cot_rows, w_in, w_out, params[:experts],
            weight=10.0,
        )
        near, far, _ = reduce_four(keep, send)
        whole = add_low(near, far)
        returning += [whole[:, k * cap : (k + 1) * cap] for k in range(group_size)]
        acts.append(act)
        kept += [act, cots, rows_all, d_hidden]

    def unite(blocks):
        return blocks if cap % 128 == 0 else [jnp.concatenate(blocks, axis=1)]

    keep_fwd, send_fwd = call(
        functools.partial(expert_out_kernel, groups=groups),
        [((2, cols, total), BF16)] * 2,
        [((4, cols, total), BF16)],
        meta, w_out, *acts,
        weight=2.9, after=(whole,),
    )
    (d_routed,) = call(
        functools.partial(combine_kernel, cap=cap),
        [((part_rows, length), BF16)],
        [((part_rows, total), BF16)],
        meta, route, slot, *unite(exchange(returning)), after=(keep_fwd,),
        weight=1.0,
    )
    routed_parts = gather_four(d_routed)

    near_fwd, far_fwd, met_fwd = reduce_four(keep_fwd, send_fwd)
    whole_fwd = add_low(near_fwd, far_fwd)
    fwd_arrived, fwd_steps = hyper_exchange(
        [whole_fwd[:, k * cap : (k + 1) * cap] for k in range(experts)]
    )
    came_fwd = unite(fwd_arrived)
    (block_out,) = call(
        functools.partial(block_out_kernel, cap=cap),
        [((length, cols), BF16)],
        [((cols, total), BF16), ((4, length, cols), F32)],
        meta, route, slot, residual, gate, *came_fwd,
        weight=1.2,
    )

    d_attn_cols, d_mixed, d_value, router_grad, gain2_grad, *first_grads = call(
        residual_back_kernel,
        [((length, cols), F32), ((length, cols), BF16), ((length, cols), BF16),
         ((experts, cols), F32), ((1, cols), F32)] + [((cols, feats), BF16)] * 2,
        [((4, cols, length), BF16), ((4, length, cols), F32)],
        meta, *routed_parts, residual, gate, router_probs, route, params, cot_turned, mixed,
        w_attn_out, probs, normed, after=(met_fwd,),
        weight=8.0,
    )
    d_query, d_key, table_grad = call(
        functools.partial(attend_back_kernel, buckets=buckets),
        [((length, cols), BF16)] * 2 + [((8, 128), F32)],
        [],
        query, key, value, probs, d_mixed, bucket, smem=0,
        weight=7.0,
    )
    wide = -(-(cols + 2) // 128) * 128
    if chunked:
        size = 2 * cols // experts
        grad_outs = [((experts // 2 * size + 16, feats), BF16)] * 2
        chunk_scratch = ((experts, size, feats), BF16)
    else:
        grad_outs = [((cols, feats), BF16)] * 2
        chunk_scratch = ((16, 128), BF16)
    keep_in, send_in, gain1_grad, *second_grads = call(
        functools.partial(query_back_kernel, chunked=chunked, heads=heads, buckets=buckets),
        [((2, length, wide), BF16)] * 2 + [((8, feats), F32)] + grad_outs,
        [((4, length, wide), BF16), chunk_scratch, ((16, feats), F32)],
        meta, tokens, norm1_gain, normed, d_query, d_key, d_value, w_query_t, w_key_t,
        w_value_t, gain2_grad, table_grad, router_grad, after=(whole_fwd,),
        weight=4.0,
    )
    first_grads = lax.psum(tuple(first_grads), "expert")
    near_in, far_in, met_in = reduce_four(keep_in, send_in)
    (input_grad,) = call(
        input_kernel,
        [((length, cols), F32)],
        [((4, length, cols), F32), ((4, 1, cols), F32)],
        meta, tokens, norm1_gain, d_attn_cols, near_in, far_in,
        weight=1.0,
    )

    kept = fence(kept, (met_in,))
    expert_out_grad = sum(dot_tn(kept[4 * g], kept[4 * g + 1]) for g in range(groups))
    expert_in_grad = sum(dot_tn(kept[4 * g + 2], kept[4 * g + 3]) for g in range(groups))
    if chunked:
        mine, small, gain1_grad = halve(*second_grads)
        held = jnp.concatenate([mine, swap(mine, "expert", 4)], axis=0)
        beside = swap(held, "expert", 2)
        other = swap(jnp.concatenate([held, beside], axis=0), "expert", 1)
        for bit in (1, 2):
            gain1_grad = gain1_grad + swap(gain1_grad, "tensor", bit)
        attn_grad, value_grad, query_grad, key_grad, gain2_grad, table_grad, router_grad = call(
            functools.partial(finish_kernel, order=ORDER, heads=heads),
            [((cols, feats), F32)] * 4
            + [((1, cols), F32), ((heads, buckets), F32), ((experts, cols), F32)],
            [chunk_scratch],
            meta, held, beside, other, small, *first_grads,
            weight=1.6, after=(input_grad, block_out, gain1_grad),
        )
    else:
        query_grad, key_grad, gain2_grad, table_grad, router_grad = lax.psum(
            (*second_grads, gain2_grad, table_grad[:heads, :buckets], router_grad), "expert"
        )
        gain1_grad = lax.psum(gain1_grad, ("expert", "tensor"))
        attn_grad, value_grad = first_grads
    return (
        block_out,
        input_grad,
        gain1_grad[0],
        query_grad.astype(F32).T,
        key_grad.astype(F32).T,
        value_grad.astype(F32).T,
        attn_grad.astype(F32),
        table_grad.T,
        gain2_grad[0],
        router_grad.T,
        expert_in_grad[None],
        expert_out_grad[None],
    )


def solution(mesh):
    return jax.shard_map(
        on_device,
        mesh=mesh,
        in_specs=(
            P("expert", None),
            P("expert", "tensor"),
            P(),
            P(None, "tensor"),
            P(None, "tensor"),
            P(None, "tensor"),
            P("tensor", None),
            P(None, "tensor"),
            P("tensor"),
            P("tensor", None),
            P("expert", None, "tensor"),
            P("expert", "tensor", None),
            P("expert"),
            P("expert"),
            P("expert"),
            P(),
        ),
        out_specs=(
            P("expert", "tensor"),
            P("expert", "tensor"),
            P(),
            P(None, "tensor"),
            P(None, "tensor"),
            P(None, "tensor"),
            P("tensor", None),
            P(None, "tensor"),
            P("tensor"),
            P("tensor", None),
            P("expert", None, "tensor"),
            P("expert", "tensor", None),
        ),
        check_vma=False,
    )
```

```python
import functools

import jax
import jax.numpy as jnp
from jax import lax
from jax.experimental import pallas as pl
from jax.experimental.pallas import tpu as pltpu
from jax.sharding import PartitionSpec as P

HDIM = 64
EPSILON = 1e-06
MASKED_SCORE = -1e30
SCORE_SCALE = 0.125
PRECISE = lax.Precision.HIGHEST
F32 = jnp.float32
BF16 = jnp.bfloat16
GELU_C = 0.7978845608028654
GELU_A = 0.044715
CHUNK = 128
GROUPS = 1


def dot_nn(a, b, precision=None):
    return lax.dot_general(
        a, b, (((1,), (0,)), ((), ())), precision=precision, preferred_element_type=F32
    )


def dot_nt(a, b, precision=None):
    return lax.dot_general(
        a, b, (((1,), (1,)), ((), ())), precision=precision, preferred_element_type=F32
    )


def dot_tn(a, b, precision=None):
    return lax.dot_general(
        a, b, (((0,), (0,)), ((), ())), precision=precision, preferred_element_type=F32
    )


def row_scale(rows):
    return lax.rsqrt(jnp.mean(rows * rows, axis=1, keepdims=True) + EPSILON)


def bucket_marks(bucket, count):
    width = bucket.shape[0]
    return lax.broadcasted_iota(jnp.int32, (count, width), 0) == bucket[...].reshape(1, width)


def in_order(blocks, rank, place, axis):
    for j, block in enumerate(blocks):
        place[rank ^ j] = block[...]
    return jnp.concatenate([place[r] for r in range(len(blocks))], axis=axis)


def as_column(row):
    return jnp.broadcast_to(row, (128, row.shape[1])).T[:, 0:1]


def softmax_rows(logits):
    shifted = jnp.exp(logits - jnp.max(logits, axis=1, keepdims=True))
    return shifted / jnp.sum(shifted, axis=1, keepdims=True)


def attend_kernel(
    tokens, w_query, w_key, w_value, gain, segment, bucket, table,
    normed_out, query_out, key_out, value_out, probs_out, mixed_out,
    band,
):
    length = tokens.shape[0]
    width = 2 * length
    heads = query_out.shape[1] // HDIM
    marks = bucket_marks(bucket, table.shape[1])
    table_rows = jnp.broadcast_to(table[...][:, None, :], (heads, 128, table.shape[1]))
    bases = []
    for h in range(heads):
        offsets = jnp.sum(
            jnp.where(marks, table_rows[h].T[:, 0:1], 0.0), axis=0, keepdims=True
        )
        bases.append(
            jnp.concatenate(
                [offsets] + [pltpu.roll(offsets, r, 1) for r in range(1, 8)], axis=0
            )
        )
    seg_row = segment[...].reshape(1, length)
    seg_col = as_column(seg_row)
    rows = tokens[...].astype(F32)
    normed = (rows * row_scale(rows) * gain[...].reshape(1, rows.shape[1])).astype(BF16)
    normed_out[...] = normed
    query = dot_nt(normed, w_query[...]).astype(BF16)
    key = dot_nt(normed, w_key[...]).astype(BF16)
    query_out[...] = query
    key_out[...] = key
    value_out[...] = dot_nt(normed, w_value[...]).astype(BF16)
    value_turned = dot_nt(w_value[...], normed).astype(BF16)
    for h in range(heads):
        cols = slice(h * HDIM, (h + 1) * HDIM)
        for b in range(length // 8):
            turned = pltpu.roll(bases[h], (length + 1 + 8 * b) % width, 1)
            band[8 * b : 8 * b + 8, :] = turned[:, :length]
        for c in range(0, length, CHUNK):
            span = slice(c, c + CHUNK)
            scores = dot_nt(query[span, cols], key[:, cols]) * SCORE_SCALE + band[span, :]
            scores = jnp.where(seg_col[span, :] == seg_row, scores, MASKED_SCORE)
            probs = softmax_rows(scores)
            probs_out[h, span, :] = probs
            mixed_out[cols, span] = dot_nt(value_turned[cols, :], probs.astype(BF16)).astype(BF16)


def dispatch(code, rows, outs, transposed=False):
    share = outs[0].shape[0]
    for k, out in enumerate(outs):
        ids = lax.broadcasted_iota(jnp.int32, (share, code.shape[1]), 0) + k * share
        marks = jnp.where(ids == code[...], 1.0, 0.0).astype(BF16)
        product = dot_nt if transposed else dot_nn
        out[...] = product(marks, rows).astype(BF16)


def slot_codes(meta, route, slot, size):
    count = route.shape[0]
    return ((route[...] ^ meta[1]) * size + slot[...]).reshape(1, count)


def first_kernel(
    meta, route, slot, cotangent, w_attn_out, w_router, gain, packed_out, *outs
):
    cap = outs[0].shape[1]
    count = len(outs) * cap
    code = slot_codes(meta, route, slot, cap)
    ids = lax.broadcasted_iota(jnp.int32, (count, code.shape[1]), 0)
    marks = jnp.where(ids == code, 1.0, 0.0).astype(BF16)
    placed = dot_nt(cotangent[...], marks).astype(BF16)
    for k, out in enumerate(outs):
        out[...] = placed[:, k * cap : (k + 1) * cap]
    rows, feats = w_attn_out.shape
    experts = w_router.shape[0]
    packed_out[:rows, :] = w_attn_out[...]
    length = cotangent.shape[1]
    top = packed_out.shape[0] - rows
    packed_out[top:, :length] = cotangent[...]
    packed_out[top:, length:] = jnp.zeros((rows, feats - length), BF16)
    line = gain[...].reshape(1, rows)
    high = line.astype(BF16)
    rest = line - high.astype(F32)
    mid = rest.astype(BF16)
    low = (rest - mid.astype(F32)).astype(BF16)
    pad = top - rows - experts - 3
    extra = [w_router[...].astype(F32)] + [p.astype(F32) for p in (high, mid, low)]
    extra = jnp.concatenate(extra + [jnp.zeros((pad, rows), F32)], axis=0)
    wide = jnp.concatenate([extra, jnp.zeros((extra.shape[0], feats - rows), F32)], axis=1)
    packed_out[rows:top, :] = wide.astype(BF16)


def dispatch(code, rows, outs):
    share = outs[0].shape[0]
    for k, out in enumerate(outs):
        ids = lax.broadcasted_iota(jnp.int32, (share, code.shape[1]), 0) + k * share
        marks = jnp.where(ids == code, 1.0, 0.0).astype(BF16)
        out[...] = dot_nn(marks, rows).astype(BF16)


def residual_kernel(
    meta, route, slot, tokens, m0, m1, m2, m3, w0, w1, w2, w3,
    residual_out, gate_out, probs_out, params_out, turned_out, *rest,
):
    outs, place, cot_place = rest[:-2], rest[-2], rest[-1]
    share = outs[0].shape[0]
    experts = probs_out.shape[1]
    cols = m0.shape[0]
    for j, w in enumerate((w0, w1, w2, w3)):
        place[meta[0] ^ j] = w[cols : w.shape[0] - cols, :cols].astype(F32)
        cot_place[meta[0] ^ j] = w[w.shape[0] - cols :, : tokens.shape[0]]
    for r in range(4):
        turned_out[r * cols : (r + 1) * cols, :] = cot_place[r]
    params = jnp.concatenate([place[r] for r in range(4)], axis=1)
    router = params[:experts]
    gain = params[experts : experts + 1]
    for i in (1, 2):
        gain = gain + params[experts + i : experts + i + 1]
    params_out[...] = jnp.concatenate([router, jnp.broadcast_to(gain, (8, gain.shape[1]))], axis=0)
    residual = tokens[...].astype(F32)
    for m, w in ((m0, w0), (m1, w1), (m2, w2), (m3, w3)):
        residual = residual + dot_tn(m[...], w[:cols, :])
    residual_out[...] = residual
    normed = residual * row_scale(residual) * gain
    part = slot[...] - meta[0] * share
    code = jnp.where(
        (part >= 0) & (part < share), (route[...] ^ meta[1]) * share + part, -1
    ).reshape(1, part.shape[0])
    dispatch(code, normed.astype(BF16), outs)
    probs = softmax_rows(dot_nt(normed, router, PRECISE))
    probs_out[...] = probs
    lanes = lax.broadcasted_iota(jnp.int32, probs.shape, 1)
    where = as_column(route[...].reshape(1, part.shape[0]))
    gate_out[...] = jnp.sum(jnp.where(lanes == where, probs, 0.0), axis=1, keepdims=True)


def assemble_kernel(*refs, count):
    out = refs[-1]
    size = refs[0].shape[0]
    for i, block in enumerate(refs[:count]):
        out[i * size : (i + 1) * size, :] = block[...]


def expert_kernel(
    meta, x0, x1, x2, x3, c0, c1, c2, c3, w_in, w_out, router,
    rows_out, act_out, cots_out, d_hidden_out, keep_out, send_out,
    x_all, c_all, part_all, *, first, direct,
):
    rank, expert = meta[0], meta[1]
    ranks = 4
    total = rows_out.shape[0]
    feats = rows_out.shape[1]
    cols = feats // ranks
    if direct:
        sources, _, share, _ = x_all.shape
        cap = ranks * share
        for j, (x, c) in enumerate(((x0, c0), (x1, c1), (x2, c2), (x3, c3))):
            for s in range(sources):
                x_all[s, rank ^ j] = x[s * share : (s + 1) * share, :]
                at = (first + s) * cols
                c_all[rank ^ j, :, s * cap : (s + 1) * cap] = c[at : at + cols, :]
        step = 256 // cap
    for i in range(total // 256):
        span = slice(i * 256, (i + 1) * 256)
        if direct:
            rows = x_all[i * step : (i + 1) * step].reshape(256, feats)
            turned = jnp.concatenate([c_all[r, :, span] for r in range(ranks)], axis=0)
            cots = turned.astype(F32).T.astype(BF16)
        else:
            rows = x0[span, :]
            cots = c0[span, :]
        rows_out[span, :] = rows
        probs = softmax_rows(dot_nt(rows, router[...].astype(BF16)))
        lanes = lax.broadcasted_iota(jnp.int32, probs.shape, 1)
        gate = jnp.sum(jnp.where(lanes == expert, probs, 0.0), axis=1, keepdims=True)
        cots_out[span, :] = (gate * cots.astype(F32)).astype(BF16)
        hidden = dot_nn(rows, w_in[...])
        pull = dot_nt(cots, w_out[...])
        bent = jnp.tanh(GELU_C * (hidden + GELU_A * hidden * hidden * hidden))
        act = (0.5 * hidden * (1.0 + bent)).astype(BF16)
        act_out[span, :] = act
        slope = 0.5 * (1.0 + bent) + 0.5 * hidden * (1.0 - bent * bent) * (
            GELU_C * (1.0 + 3.0 * GELU_A * hidden * hidden)
        )
        d_hidden = (gate * pull * slope).astype(BF16)
        d_hidden_out[span, :] = d_hidden
        d_gate = jnp.sum(pull * act.astype(F32), axis=1, keepdims=True)
        d_part = dot_nt(w_in[...], d_hidden).astype(BF16)
        tail = jnp.broadcast_to(d_gate, (256, 128)).T[: part_all.shape[1] - cols].astype(BF16)
        for r in range(ranks):
            j = rank ^ r
            place = (j % 2) * 2 + j // 2
            part_all[place, :cols, span] = d_part[r * cols : (r + 1) * cols, :]
            part_all[place, cols:, span] = tail
    keep_out[...] = part_all[0:2]
    send_out[...] = part_all[2:4]


def expert_out_kernel(meta, w_out, *refs, groups):
    acts, (keep_out, send_out, part_all) = refs[:groups], refs[-3:]
    rank = meta[0]
    ranks = 4
    cols = part_all.shape[1]
    at = 0
    for act in acts:
        for i in range(0, act.shape[0], 256):
            part = dot_nn(act[i : i + 256, :], w_out[...]).T.astype(BF16)
            for r in range(ranks):
                j = rank ^ r
                part_all[(j % 2) * 2 + j // 2, :, at : at + 256] = part[r * cols : (r + 1) * cols]
            at += 256
    keep_out[...] = part_all[0:2]
    send_out[...] = part_all[2:4]


def slot_marks(meta, route, slot, cap, count):
    code = slot_codes(meta, route, slot, cap)
    ids = lax.broadcasted_iota(jnp.int32, (code.shape[1], count), 1)
    return jnp.where(ids == as_column(code), 1.0, 0.0).astype(BF16)


def fence_kernel(*refs):
    del refs


def side_by_side(blocks, came):
    size = blocks[0].shape[1]
    for k, block in enumerate(blocks):
        came[:, k * size : (k + 1) * size] = block[...]
    return came[...]


def combine_kernel(meta, route, slot, *rest, cap):
    *blocks, _, out, came = rest
    marks = slot_marks(meta, route, slot, cap, came.shape[1])
    out[...] = dot_nt(side_by_side(blocks, came), marks).astype(BF16)


def block_out_kernel(meta, route, slot, residual, gate, *rest, cap):
    *blocks, block_out, came, place = rest
    rank = meta[0]
    cols = block_out.shape[1]
    marks = slot_marks(meta, route, slot, cap, came.shape[1])
    returned = dot_nt(marks, side_by_side(blocks, came))
    for r in range(4):
        place[r] = residual[:, r * cols : (r + 1) * cols]
    block_out[...] = (place[rank] + gate[...] * returned).astype(BF16)


def put_chunks(grads, keep, send, place, expert, order):
    count = len(order)
    size = grads.shape[0] // count
    for c in range(count):
        place[c ^ expert] = grads[c * size : (c + 1) * size, :]
    for i, k in enumerate(order):
        out = keep if i < count // 2 else send
        at = (i % (count // 2)) * size
        out[at : at + size, :] = place[k]


def residual_back_kernel(
    meta, r0, r1, r2, r3, residual, gate, probs, route, params, cotangent, mixed, w_attn_out,
    attn_probs, normed_one, _, d_attn_cols_out, d_mixed_out, d_value_out, router_grad_out,
    gain_grad_out, first_out, second_out, place, place_f32, chunk_place, *, chunked,
):
    rank, expert = meta[0], meta[1]
    experts = probs.shape[1]
    feats = residual.shape[1]
    cols = feats // 4
    length = residual.shape[0]
    router = params[:experts, :]
    gain = params[experts : experts + 1, :]
    for j, r in enumerate((r0, r1, r2, r3)):
        place[rank ^ j] = r[:cols, :]
    d_gate = as_column(r0[cols : cols + 1, :].astype(F32))
    d_routed = jnp.concatenate([place[r] for r in range(4)], axis=0).astype(F32).T
    res = residual[...]
    scale = row_scale(res)
    lanes = lax.broadcasted_iota(jnp.int32, probs.shape, 1)
    onehot = jnp.where(lanes == as_column(route[...].reshape(1, length)), 1.0, 0.0)
    d_logits = d_gate * probs[...] * (onehot - gate[...])
    d_normed = d_routed + dot_nn(d_logits, router, PRECISE)
    normed = res * scale * gain
    router_grad = dot_tn(d_logits, normed, PRECISE)
    gain_grad = jnp.sum(d_normed * res * scale, axis=0, keepdims=True)
    cross = jnp.sum(gain * res * d_normed, axis=1, keepdims=True)
    d_residual = (
        cotangent[...].astype(F32).T
        + scale * gain * d_normed
        - res * (scale * scale * scale * cross * (1.0 / feats))
    )
    for r in range(4):
        own = slice(r * cols, (r + 1) * cols)
        place_f32[r] = d_residual[:, own]

        @pl.when(rank == r)
        def _():
            router_grad_out[...] = router_grad[:, own]
            gain_grad_out[...] = gain_grad[:, own]

    d_attn_cols_out[...] = place_f32[rank]
    d_attn = d_residual.astype(BF16)
    attn_grad = dot_nn(mixed[...], d_attn).astype(BF16)
    d_mixed = dot_nt(d_attn, w_attn_out[...]).astype(BF16)
    d_mixed_out[...] = d_mixed
    for h in range(cols // HDIM):
        own = slice(h * HDIM, (h + 1) * HDIM)
        total = jnp.zeros((length, HDIM), F32)
        for c in range(0, length, CHUNK):
            span = slice(c, c + CHUNK)
            total = total + dot_tn(attn_probs[h, span, :].astype(BF16), d_mixed[span, own])
        d_value_out[:, own] = total.astype(BF16)
    value_grad = dot_tn(d_value_out[...], normed_one[...]).astype(BF16)
    if chunked:
        both = jnp.concatenate([attn_grad, value_grad], axis=0)
        put_chunks(both, first_out, second_out, chunk_place, expert, chunked)
    else:
        first_out[...] = attn_grad
        second_out[...] = value_grad


def attend_back_kernel(
    query, key, value, probs, d_mixed, bucket, d_query, d_key, table_out, *, buckets
):
    length = query.shape[0]
    width = 2 * length
    heads = query.shape[1] // HDIM
    marks = bucket_marks(bucket, buckets)
    zeros = jnp.zeros((8, width - length), F32)
    table_out[...] = jnp.zeros(table_out.shape, F32)
    for h in range(heads):
        own = slice(h * HDIM, (h + 1) * HDIM)
        dk = jnp.zeros((length, HDIM), F32)
        diagonals = jnp.zeros((8, width), F32)
        for c in range(0, length, CHUNK):
            span = slice(c, c + CHUNK)
            weights = probs[h, span, :]
            d_probs = dot_nt(d_mixed[span, own], value[:, own])
            inner = jnp.sum(d_probs * weights, axis=1, keepdims=True)
            d_scores = weights * (d_probs - inner)
            for b in range(CHUNK // 8):
                piece = jnp.concatenate([d_scores[8 * b : 8 * b + 8, :], zeros], axis=1)
                diagonals = diagonals + pltpu.roll(piece, (length - 1 - c - 8 * b) % width, 1)
            low = d_scores.astype(BF16)
            d_query[span, own] = (dot_nn(low, key[:, own]) * SCORE_SCALE).astype(BF16)
            dk = dk + dot_tn(low, query[span, own])
        d_key[:, own] = (dk * SCORE_SCALE).astype(BF16)
        line = diagonals[0:1]
        for r in range(1, 8):
            line = line + pltpu.roll(diagonals[r : r + 1], width - r, 1)
        table_col = jnp.sum(jnp.where(marks, line, 0.0), axis=1, keepdims=True)
        table_out[h : h + 1, :buckets] = jnp.broadcast_to(table_col, (buckets, 128)).T[0:1, :]


def put_split(out, at, row, value):
    high = value.astype(BF16).astype(F32)
    out[row : row + 1, at : at + value.shape[1]] = high
    out[row + 8 : row + 9, at : at + value.shape[1]] = value - high


def query_back_kernel(
    meta, tokens, gain, normed, d_query, d_key, d_value, w_query, w_key, w_value, gain2_grad,
    table_grad, router_grad, _, _got, *rest, chunked, heads, buckets,
):
    keep_in, send_in, gain1_out, first_out, second_out, place, chunk_place, pack = rest
    rank, expert = meta[0], meta[1]
    length, feats = tokens.shape
    cols = feats // 4
    normed_rows = normed[...]
    query_grad = dot_tn(d_query[...], normed_rows).astype(BF16)
    key_grad = dot_tn(d_key[...], normed_rows).astype(BF16)
    d_normed = (
        dot_nn(d_query[...], w_query[...])
        + dot_nn(d_key[...], w_key[...])
        + dot_nn(d_value[...], w_value[...])
    )
    rows = tokens[...].astype(F32)
    product = d_normed * rows
    gain1_grad = jnp.sum(product * row_scale(rows), axis=0, keepdims=True)
    gain1_out[...] = jnp.broadcast_to(gain1_grad, gain1_out.shape)
    if chunked:
        pack[...] = jnp.zeros(pack.shape, F32)
        put_split(pack, 0, 0, gain1_grad)
        put_split(pack, 0, 1, gain2_grad[...])
        for h in range(heads):
            put_split(pack, 256 * h, 2, table_grad[h : h + 1, :])
        for e in range(router_grad.shape[0]):
            put_split(pack, 256 * (e % 3), 3 + e // 3, router_grad[e : e + 1, :])
        small = pack[...].astype(BF16)
        both = jnp.concatenate([query_grad, key_grad], axis=0)
        put_chunks(both, first_out, second_out, chunk_place, expert, chunked)
        for out in (first_out, second_out):
            out[out.shape[0] - 16 :, :] = small
    else:
        first_out[...] = query_grad
        second_out[...] = key_grad
    cross = jnp.sum(product * gain[...].reshape(1, feats), axis=1, keepdims=True)
    high = cross.astype(BF16).astype(F32)
    low = cross - high
    lanes = lax.broadcasted_iota(jnp.int32, (length, place.shape[2] - cols), 1)
    extra = jnp.where(lanes == 0, high, jnp.where(lanes == 1, low, 0.0)).astype(BF16)
    for r in range(4):
        j = rank ^ r
        own = d_normed[:, r * cols : (r + 1) * cols].astype(BF16)
        place[(j % 2) * 2 + j // 2] = jnp.concatenate([own, extra], axis=1)
    keep_in[...] = place[0:2]
    send_in[...] = place[2:4]


def input_kernel(
    meta, tokens, gain, d_attn_cols, first, second, *rest
):
    *_, out, place, gain_place = rest
    rank = meta[0]
    feats = tokens.shape[1]
    cols = feats // 4
    rows = tokens[...].astype(F32)
    scale = row_scale(rows)
    both = first[...].astype(F32) + second[...].astype(F32)
    cross = both[:, cols : cols + 1] + both[:, cols + 1 : cols + 2]
    gain_row = gain[...].reshape(1, feats)
    for r in range(4):
        place[r] = rows[:, r * cols : (r + 1) * cols]
        gain_place[r] = gain_row[:, r * cols : (r + 1) * cols]
    own = both[:, :cols]
    own_rows = place[rank]
    out[...] = (
        d_attn_cols[...]
        + scale * gain_place[rank] * own
        - own_rows * (scale * scale * scale * cross * (1.0 / feats))
    )


def add_small(a, b):
    at = a.shape[0] - 16
    total = (
        a[at : at + 8, :].astype(F32)
        + b[at : at + 8, :].astype(F32)
        + a[at + 8 :, :].astype(F32)
        + b[at + 8 :, :].astype(F32)
    )
    high = total.astype(BF16).astype(F32)
    return total, jnp.concatenate([high, total - high], axis=0).astype(BF16)


def sum_kernel(keep, got, keep_out, send_out):
    half = (keep.shape[0] - 16) // 2
    total = (keep[: 2 * half, :].astype(F32) + got[: 2 * half, :].astype(F32)).astype(BF16)
    _, small = add_small(keep, got)
    keep_out[:half, :] = total[:half]
    send_out[:half, :] = total[half:]
    keep_out[half:, :] = small
    send_out[half:, :] = small


def last_sum_kernel(keep, got, mine_out, small_out, gain1_out):
    size = mine_out.shape[0]
    mine_out[...] = (keep[:size, :].astype(F32) + got[:size, :].astype(F32)).astype(BF16)
    total, _ = add_small(keep, got)
    small_out[...] = total
    gain1_out[...] = jnp.broadcast_to(total[0:1], gain1_out.shape)


def spread_kernel(meta, mine, second, other, first_out, second_out, place, *, order):
    expert = meta[1]
    count = len(order)
    size = mine.shape[0] // 2
    quarter = count // 4
    for i in range(count):
        block, at = (
            (mine, i)
            if i < quarter
            else (second, i - quarter) if i < 2 * quarter else (other, i - 2 * quarter)
        )
        place[order[i]] = block[at * size : (at + 1) * size, :]
    rows = first_out.shape[0]
    for c in range(count):
        chunk = place[c ^ expert].astype(F32)
        start = c * size
        if start < rows:
            first_out[start : start + size, :] = chunk
        else:
            second_out[start - rows : start - rows + size, :] = chunk


def finish_kernel(
    meta, mine, second, other, small, *rest, order, heads
):
    first_out, second_out, gain2_out, table_out, router_out, place = rest[-6:]
    spread_kernel(meta, mine, second, other, first_out, second_out, place, order=order)
    cols = gain2_out.shape[1]
    gain2_out[...] = small[1:2, :cols]
    for h in range(heads):
        table_out[h : h + 1, :] = small[2:3, 256 * h : 256 * h + table_out.shape[1]]
    for e in range(router_out.shape[0]):
        at = 256 * (e % 3)
        router_out[e : e + 1, :] = small[3 + e // 3 : 4 + e // 3, at : at + cols]


def moving(kernel, smem, fetch, total, far):
    def run(*refs):
        rest = list(refs[: len(refs) - 1])
        sems = refs[-1]
        near_out = rest[len(rest) - len(far) :] if far else []
        rest = rest[: len(rest) - len(far)]
        near_in = rest[len(rest) - fetch :] if fetch else []
        rest = rest[: len(rest) - fetch]
        copies = [
            pltpu.make_async_copy(rest[smem + i], b, sems.at[i]) for i, b in enumerate(near_in)
        ]
        for copy in copies:
            copy.start()
        for copy in copies:
            copy.wait()
        inner = list(rest)
        for i, b in enumerate(near_in):
            inner[smem + i] = b
        for b, at in zip(near_out, far):
            inner[total + at] = b
        kernel(*inner)
        copies = [
            pltpu.make_async_copy(b, rest[total + at], sems.at[fetch + i])
            for i, (b, at) in enumerate(zip(near_out, far))
        ]
        for copy in copies:
            copy.start()
        for copy in copies:
            copy.wait()

    return run


def call(kernel, outs, scratch, *operands, weight=1.0, smem=1, fetch=0, far=(), after=()):
    specs, given = [], []
    for i, operand in enumerate(operands):
        if i < smem:
            specs.append(pl.BlockSpec(memory_space=pltpu.SMEM))
        elif i < smem + fetch:
            specs.append(pl.BlockSpec(memory_space=pltpu.HBM))
            operand = pltpu.with_memory_space_constraint(operand, pltpu.HBM)
        else:
            specs.append(pl.BlockSpec(memory_space=pltpu.VMEM))
        given.append(operand)
    specs += [pl.BlockSpec(memory_space=pl.ANY)] * len(after)
    scratch_shapes = [pltpu.VMEM(shape, kind) for shape, kind in scratch]
    shapes, out_specs = [], []
    for i, (shape, kind) in enumerate(outs):
        shapes.append(pltpu.HBM(shape, kind) if i in far else jax.ShapeDtypeStruct(shape, kind))
        out_specs.append(pl.BlockSpec(memory_space=pltpu.HBM if i in far else pltpu.VMEM))
    if fetch or far:
        kernel = moving(kernel, smem, fetch, len(operands) + len(after), far)
        scratch_shapes += [pltpu.VMEM(a.shape, a.dtype) for a in operands[smem : smem + fetch]]
        scratch_shapes += [pltpu.VMEM(*outs[i]) for i in far]
        scratch_shapes.append(pltpu.SemaphoreType.DMA((fetch + len(far),)))
    return pl.pallas_call(
        kernel,
        out_shape=shapes,
        in_specs=specs,
        out_specs=out_specs,
        scratch_shapes=scratch_shapes,
        compiler_params=pltpu.CompilerParams(vmem_limit_bytes=32 * 1024 * 1024),
        cost_estimate=pl.CostEstimate(
            flops=int(weight * 1.1e9), bytes_accessed=1 << 16, transcendentals=0
        ),
    )(*given, *after)


def swap(array, axis, bit):
    size = lax.axis_size(axis)
    return lax.ppermute(array, axis, [(i, i ^ bit) for i in range(size)])


def add_low(a, b):
    return (a.astype(F32) + b.astype(F32)).astype(BF16)


def gather_four(array):
    across = swap(array, "tensor", 2)
    beside = swap(array, "tensor", 1)
    return [array, beside, across, swap(across, "tensor", 1)]


def reduce_four(keep, send):
    got = swap(send, "tensor", 1)
    far = add_low(keep[1], got[1])
    return add_low(keep[0], got[0]), swap(far, "tensor", 2), far


def exchange(blocks):
    if len(blocks) > 8:
        return hyper_exchange(blocks)[0]
    return [blocks[0]] + [swap(b, "expert", k) for k, b in enumerate(blocks) if k]


def hyper_exchange(blocks, gates=None):
    count = len(blocks)
    held = {k: [b] for k, b in enumerate(blocks)}
    steps = []
    bit = 1
    while bit < count:
        away = [k for k in sorted(held) if k & bit]
        sent = jnp.concatenate([b for k in away for b in held[k]], axis=0)
        if gates and bit in gates:
            (sent,) = fence([sent], gates[bit])
        got = swap(sent, "expert", bit)
        if gates and -bit in gates:
            (got,) = fence([got], gates[-bit])
        steps.append(got)
        size = blocks[0].shape[0]
        at = 0
        fresh = {}
        for k in away:
            pieces = [got[at + i * size : at + (i + 1) * size] for i in range(len(held[k]))]
            at += len(held[k]) * size
            fresh[k ^ bit] = held[k ^ bit] + pieces
        held = fresh
        bit *= 2
    return held[0], steps


ORDER = (0, 4, 2, 6, 1, 5, 3, 7)


def gather_chunks(mine, gates=None):
    held = swap(mine, "expert", 4)
    if gates:
        (held,) = fence([held], (gates[0],))
    held = jnp.concatenate([mine, held], axis=0)
    beside = swap(held, "expert", 2)
    if gates:
        (beside,) = fence([beside], (gates[1],))
    return held, beside, swap(jnp.concatenate([held, beside], axis=0), "expert", 1)


def halve_plain(keep, got, gates):
    for bit, gate in zip((2, 4), gates):
        half = keep.shape[0] // 2
        sent = add_low(keep[half:], got[half:])
        keep = add_low(keep[:half], got[:half])
        (got,) = fence([swap(sent, "expert", bit)], (gate,))
    return add_low(keep, got)


def halve(keep, send):
    feats = keep.shape[1]
    steps = []
    for bit in (1, 2):
        rows = (keep.shape[0] - 16) // 2 + 16
        keep, send = call(
            sum_kernel, [((rows, feats), BF16)] * 2, [], keep, swap(send, "expert", bit), smem=0
        )
        steps.append(send)
    last = call(
        last_sum_kernel,
        [((keep.shape[0] - 16, feats), BF16), ((8, feats), F32), ((8, feats), F32)],
        [],
        keep, swap(send, "expert", 4), smem=0,
    )
    return last, steps


def fence(arrays, after):
    count = len(arrays)
    return pl.pallas_call(
        fence_kernel,
        out_shape=[jax.ShapeDtypeStruct(a.shape, a.dtype) for a in arrays],
        in_specs=[pl.BlockSpec(memory_space=pl.ANY)] * (count + len(after)),
        out_specs=[pl.BlockSpec(memory_space=pl.ANY)] * count,
        input_output_aliases={i: i for i in range(count)},
    )(*arrays, *after)


def on_device(
    tokens, cotangent, norm1_gain, w_query, w_key, w_value, w_attn_out, bias_table, norm2_gain,
    w_router, expert_in, expert_out, route, slot, segment, rel_bucket,
):
    length, feats = tokens.shape
    cols = cotangent.shape[1]
    heads = cols // HDIM
    experts = lax.axis_size("expert")
    cap = 2 * length // experts
    share = cap // 4
    rank = lax.axis_index("tensor").astype(jnp.int32)
    expert = lax.axis_index("expert").astype(jnp.int32)
    meta = jnp.stack([rank, expert])
    total = experts * cap
    direct = share % 16 == 0
    buckets = bias_table.shape[0]
    chunked = ORDER if experts == len(ORDER) else None

    w_query_t, w_key_t, w_value_t = w_query.T, w_key.T, w_value.T
    packed_rows = 2 * cols + -(-(experts + 3) // 16) * 16
    packed, *cot_blocks = call(
        first_kernel,
        [((packed_rows, feats), BF16)] + [((cols, cap), BF16)] * experts,
        [],
        meta, route, slot, cotangent.T, w_attn_out, w_router.T, norm2_gain,
        weight=2.0, fetch=6,
    )
    packed_parts = gather_four(packed)
    bucket = jnp.concatenate([rel_bucket, jnp.full((1,), -1, jnp.int32)])
    normed, query, key, value, probs, mixed = call(
        attend_kernel,
        [((length, feats), BF16)]
        + [((length, cols), BF16)] * 3
        + [((heads, length, length), F32), ((cols, length), BF16)],
        [((length, length), F32)],
        tokens, w_query.T, w_key.T, w_value.T, norm1_gain, segment, bucket, bias_table.T,
        weight=7.0, smem=0, fetch=8, far=(0, 1, 2, 3, 4),
    )

    mixed_parts = gather_four(mixed)
    residual, gate, router_probs, params, cot_turned, *row_blocks = call(
        residual_kernel,
        [
            ((length, feats), F32),
            ((length, 1), F32),
            ((length, experts), F32),
            ((experts + 8, feats), F32),
            ((feats, length), BF16),
        ]
        + [((share, feats), BF16)] * experts,
        [((4, packed_rows - 2 * cols, cols), F32), ((4, cols, length), BF16)],
        meta, route, slot, tokens, *mixed_parts, *packed_parts,
        weight=5.8, fetch=3, far=(0, 1, 2, 4),
    )
    cot_arrived, _ = hyper_exchange(
        cot_blocks, {2: (mixed, packed_parts[1], packed_parts[2]), -4: (residual,)}
    )
    cot_rows = gather_four(jnp.concatenate(cot_arrived, axis=0))
    arrived = exchange(row_blocks)
    groups = GROUPS if direct else 1
    group_size = experts // groups
    row_groups = []
    for g in range(groups):
        blocks = arrived[g * group_size : (g + 1) * group_size]
        if direct:
            (packed,) = call(
                functools.partial(assemble_kernel, count=group_size),
                [((group_size * share, feats), BF16)],
                [],
                *blocks,
                weight=1.0, smem=0, after=(cot_rows[2],),
            )
        else:
            packed = jnp.concatenate(blocks, axis=0)
        row_groups.append(gather_four(packed))

    if not direct:
        def assemble(parts, shape, turn):
            stacked = jnp.stack(parts).reshape(4, experts, *shape)
            stacked = stacked[rank ^ jnp.arange(4, dtype=jnp.int32)]
            return [jnp.transpose(stacked, turn).reshape(total, feats)]

        one = jnp.zeros((16, 128), BF16)
        row_groups = [assemble(row_groups[0], (share, feats), (1, 0, 2, 3)) + [one] * 3]
        cot_rows = assemble(cot_rows, (cols, cap), (1, 3, 0, 2)) + [one] * 3
    w_in, w_out = expert_in[0], expert_out[0]
    hidden_count = w_in.shape[1]
    part_rows = cols + 16
    count = total // groups
    x_shape = (group_size, 4, share, feats) if direct else (1, 1, 16, 128)
    c_shape = (4, cols, count) if direct else (1, 16, 128)
    acts, returning, kept = [], [], []
    for g in range(groups):
        rows_all, act, cots, d_hidden, keep, send = call(
            functools.partial(expert_kernel, first=g * group_size, direct=direct),
            [((count, feats), BF16), ((count, hidden_count), BF16), ((count, feats), BF16),
             ((count, hidden_count), BF16), ((2, part_rows, count), BF16),
             ((2, part_rows, count), BF16)],
            [(x_shape, BF16), (c_shape, BF16), ((4, part_rows, count), BF16)],
            meta, *row_groups[g], *cot_rows, w_in, w_out, params[:experts],
            weight=10.0, far=(0, 1, 2, 3) if direct else (),
        )
        near, far, _ = reduce_four(keep, send)
        whole = add_low(near, far)
        returning += [whole[:, k * cap : (k + 1) * cap] for k in range(group_size)]
        acts.append(act)
        kept += [act, cots, rows_all, d_hidden]

    def unite(blocks):
        return blocks if cap % 128 == 0 else [jnp.concatenate(blocks, axis=1)]

    keep_fwd, send_fwd = call(
        functools.partial(expert_out_kernel, groups=groups),
        [((2, cols, total), BF16)] * 2,
        [((4, cols, total), BF16)],
        meta, w_out, *acts,
        weight=2.9, after=(whole,),
    )
    (d_routed,) = call(
        functools.partial(combine_kernel, cap=cap),
        [((part_rows, length), BF16)],
        [((part_rows, total), BF16)],
        meta, route, slot, *unite(exchange(returning)), after=(keep_fwd,),
        weight=1.0,
    )
    routed_parts = gather_four(d_routed)

    near_fwd, far_fwd, met_fwd = reduce_four(keep_fwd, send_fwd)
    whole_fwd = add_low(near_fwd, far_fwd)
    fwd_arrived, fwd_steps = hyper_exchange(
        [whole_fwd[:, k * cap : (k + 1) * cap] for k in range(experts)]
    )
    came_fwd = unite(fwd_arrived)
    (block_out,) = call(
        functools.partial(block_out_kernel, cap=cap),
        [((length, cols), BF16)],
        [((cols, total), BF16), ((4, length, cols), F32)],
        meta, route, slot, residual, gate, *came_fwd,
        weight=1.2,
    )

    if chunked:
        size = 2 * cols // experts
        grad_outs = [((experts // 2 * size + 16, feats), BF16)] * 2
        chunk_scratch = ((experts, size, feats), BF16)
    else:
        grad_outs = [((cols, feats), BF16)] * 2
        chunk_scratch = ((16, 128), BF16)
    d_attn_cols, d_mixed, d_value, router_grad, gain2_grad, *first_grads = call(
        functools.partial(residual_back_kernel, chunked=chunked),
        [((length, cols), F32), ((length, cols), BF16), ((length, cols), BF16),
         ((experts, cols), F32), ((1, cols), F32)]
        + [((cols, feats), BF16)] * 2,
        [((4, cols, length), BF16), ((4, length, cols), F32), chunk_scratch],
        meta, *routed_parts, residual, gate, router_probs, route, params, cot_turned, mixed,
        w_attn_out, probs, normed, after=(met_fwd,),
        weight=8.0, far=(0,),
    )
    d_query, d_key, table_grad = call(
        functools.partial(attend_back_kernel, buckets=buckets),
        [((length, cols), BF16)] * 2 + [((8, 128), F32)],
        [],
        query, key, value, probs, d_mixed, bucket, smem=0,
        weight=7.0,
    )
    wide = -(-(cols + 2) // 128) * 128
    first_got = swap(first_grads[1], "expert", 1) if chunked else d_query
    keep_in, send_in, gain1_grad, *second_grads = call(
        functools.partial(query_back_kernel, chunked=chunked, heads=heads, buckets=buckets),
        [((2, length, wide), BF16)] * 2 + [((8, feats), F32)] + grad_outs,
        [((4, length, wide), BF16), chunk_scratch, ((16, feats), F32)],
        meta, tokens, norm1_gain, normed, d_query, d_key, d_value, w_query_t, w_key_t,
        w_value_t, gain2_grad, table_grad, router_grad, after=(whole_fwd, first_got),
        weight=4.0,
    )
    near_in, far_in, met_in = reduce_four(keep_in, send_in)
    (input_grad,) = call(
        input_kernel,
        [((length, cols), F32)],
        [((4, length, cols), F32), ((4, 1, cols), F32)],
        meta, tokens, norm1_gain, d_attn_cols, near_in, far_in,
        weight=1.0,
    )

    kept = fence(kept, (met_in,))
    expert_out_grad = sum(dot_tn(kept[4 * g], kept[4 * g + 1]) for g in range(groups))
    expert_in_grad = sum(dot_tn(kept[4 * g + 2], kept[4 * g + 3]) for g in range(groups))
    if chunked:
        (mine, small, gain1_grad), steps = halve(*second_grads)
        second_chunks = gather_chunks(mine)
        attn_grad, value_grad = call(
            functools.partial(spread_kernel, order=ORDER),
            [((cols, feats), F32)] * 2,
            [chunk_scratch],
            meta,
            *gather_chunks(
                halve_plain(first_grads[0], *fence([first_got], (keep_in,)), steps),
                (mine, second_chunks[0]),
            ),
            weight=1.6,
        )
        for bit in (1, 2):
            gain1_grad = gain1_grad + swap(gain1_grad, "tensor", bit)
        query_grad, key_grad, gain2_grad, table_grad, router_grad = call(
            functools.partial(finish_kernel, order=ORDER, heads=heads),
            [((cols, feats), F32)] * 2
            + [((1, cols), F32), ((heads, buckets), F32), ((experts, cols), F32)],
            [chunk_scratch],
            meta, *second_chunks, small,
            weight=1.6, after=(input_grad, block_out, gain1_grad, attn_grad),
        )
    else:
        query_grad, key_grad, gain2_grad, table_grad, router_grad = lax.psum(
            (*second_grads, gain2_grad, table_grad[:heads, :buckets], router_grad), "expert"
        )
        gain1_grad = lax.psum(gain1_grad, ("expert", "tensor"))
        attn_grad, value_grad = lax.psum(tuple(first_grads), "expert")
    return (
        block_out,
        input_grad,
        gain1_grad[0],
        query_grad.astype(F32).T,
        key_grad.astype(F32).T,
        value_grad.astype(F32).T,
        attn_grad.astype(F32),
        table_grad.T,
        gain2_grad[0],
        router_grad.T,
        expert_in_grad[None],
        expert_out_grad[None],
    )


def solution(mesh):
    return jax.shard_map(
        on_device,
        mesh=mesh,
        in_specs=(
            P("expert", None),
            P("expert", "tensor"),
            P(),
            P(None, "tensor"),
            P(None, "tensor"),
            P(None, "tensor"),
            P("tensor", None),
            P(None, "tensor"),
            P("tensor"),
            P("tensor", None),
            P("expert", None, "tensor"),
            P("expert", "tensor", None),
            P("expert"),
            P("expert"),
            P("expert"),
            P(),
        ),
        out_specs=(
            P("expert", "tensor"),
            P("expert", "tensor"),
            P(),
            P(None, "tensor"),
            P(None, "tensor"),
            P(None, "tensor"),
            P("tensor", None),
            P(None, "tensor"),
            P("tensor"),
            P("tensor", None),
            P("expert", None, "tensor"),
            P("expert", "tensor", None),
        ),
        check_vma=False,
    )
```

```python
import functools

import jax
import jax.numpy as jnp
from jax import lax
from jax.experimental import pallas as pl
from jax.experimental.pallas import tpu as pltpu
from jax.sharding import PartitionSpec as P

HDIM = 64
EPSILON = 1e-06
MASKED_SCORE = -1e30
SCORE_SCALE = 0.125
PRECISE = lax.Precision.HIGHEST
F32 = jnp.float32
BF16 = jnp.bfloat16
GELU_C = 0.7978845608028654
GELU_A = 0.044715
CHUNK = 128
GROUPS = 1


def dot_nn(a, b, precision=None):
    return lax.dot_general(
        a, b, (((1,), (0,)), ((), ())), precision=precision, preferred_element_type=F32
    )


def dot_nt(a, b, precision=None):
    return lax.dot_general(
        a, b, (((1,), (1,)), ((), ())), precision=precision, preferred_element_type=F32
    )


def dot_tn(a, b, precision=None):
    return lax.dot_general(
        a, b, (((0,), (0,)), ((), ())), precision=precision, preferred_element_type=F32
    )


def row_scale(rows):
    return lax.rsqrt(jnp.mean(rows * rows, axis=1, keepdims=True) + EPSILON)


def bucket_marks(bucket, count):
    width = bucket.shape[0]
    return lax.broadcasted_iota(jnp.int32, (count, width), 0) == bucket[...].reshape(1, width)


def in_order(blocks, rank, place, axis):
    for j, block in enumerate(blocks):
        place[rank ^ j] = block[...]
    return jnp.concatenate([place[r] for r in range(len(blocks))], axis=axis)


def as_column(row):
    return jnp.broadcast_to(row, (128, row.shape[1])).T[:, 0:1]


def softmax_rows(logits):
    shifted = jnp.exp(logits - jnp.max(logits, axis=1, keepdims=True))
    return shifted / jnp.sum(shifted, axis=1, keepdims=True)


def attend_kernel(
    tokens, w_query, w_key, w_value, gain, segment, bucket, table,
    normed_out, query_out, key_out, value_out, probs_out, mixed_out, token_out,
    band,
):
    length = tokens.shape[0]
    width = 2 * length
    heads = query_out.shape[1] // HDIM
    marks = bucket_marks(bucket, table.shape[1])
    table_rows = jnp.broadcast_to(table[...][:, None, :], (heads, 128, table.shape[1]))
    bases = []
    for h in range(heads):
        offsets = jnp.sum(
            jnp.where(marks, table_rows[h].T[:, 0:1], 0.0), axis=0, keepdims=True
        )
        bases.append(
            jnp.concatenate(
                [offsets] + [pltpu.roll(offsets, r, 1) for r in range(1, 8)], axis=0
            )
        )
    token_out[...] = jnp.zeros(token_out.shape, F32)
    seg_row = segment[...].reshape(1, length)
    seg_col = as_column(seg_row)
    rows = tokens[...].astype(F32)
    normed = (rows * row_scale(rows) * gain[...].reshape(1, rows.shape[1])).astype(BF16)
    normed_out[...] = normed
    query = dot_nt(normed, w_query[...]).astype(BF16)
    key = dot_nt(normed, w_key[...]).astype(BF16)
    query_out[...] = query
    key_out[...] = key
    value_out[...] = dot_nt(normed, w_value[...]).astype(BF16)
    value_turned = dot_nt(w_value[...], normed).astype(BF16)
    for h in range(heads):
        cols = slice(h * HDIM, (h + 1) * HDIM)
        for b in range(length // 8):
            turned = pltpu.roll(bases[h], (length + 1 + 8 * b) % width, 1)
            band[8 * b : 8 * b + 8, :] = turned[:, :length]
        for c in range(0, length, CHUNK):
            span = slice(c, c + CHUNK)
            scores = dot_nt(query[span, cols], key[:, cols]) * SCORE_SCALE + band[span, :]
            scores = jnp.where(seg_col[span, :] == seg_row, scores, MASKED_SCORE)
            probs = softmax_rows(scores)
            probs = probs.astype(BF16)
            probs_out[h, span, :] = probs
            mixed_out[cols, span] = dot_nt(value_turned[cols, :], probs).astype(BF16)


def dispatch(code, rows, outs, transposed=False):
    share = outs[0].shape[0]
    for k, out in enumerate(outs):
        ids = lax.broadcasted_iota(jnp.int32, (share, code.shape[1]), 0) + k * share
        marks = jnp.where(ids == code[...], 1.0, 0.0).astype(BF16)
        product = dot_nt if transposed else dot_nn
        out[...] = product(marks, rows).astype(BF16)


def slot_codes(meta, route, slot, size):
    count = route.shape[0]
    return ((route[...] ^ meta[1]) * size + slot[...]).reshape(1, count)


def first_kernel(
    meta, route, slot, cotangent, w_attn_out, w_router, gain, packed_out, own_out, *outs
):
    cap = outs[0].shape[1]
    count = len(outs) * cap
    code = slot_codes(meta, route, slot, cap)
    ids = lax.broadcasted_iota(jnp.int32, (count, code.shape[1]), 0)
    marks = jnp.where(ids == code, 1.0, 0.0).astype(BF16)
    placed = dot_nt(cotangent[...], marks).astype(BF16)
    for k, out in enumerate(outs):
        out[...] = placed[:, k * cap : (k + 1) * cap]
    rows, feats = w_attn_out.shape
    for i in range(0, cotangent.shape[1], cap):
        at = i // cap * rows
        own_out[at : at + rows, :] = cotangent[:, i : i + cap]
    experts = w_router.shape[0]
    packed_out[:rows, :] = w_attn_out[...]
    top = packed_out.shape[0]
    line = gain[...].reshape(1, rows)
    high = line.astype(BF16)
    rest = line - high.astype(F32)
    mid = rest.astype(BF16)
    low = (rest - mid.astype(F32)).astype(BF16)
    pad = top - rows - experts - 3
    extra = [w_router[...].astype(F32)] + [p.astype(F32) for p in (high, mid, low)]
    extra = jnp.concatenate(extra + [jnp.zeros((pad, rows), F32)], axis=0)
    wide = jnp.concatenate([extra, jnp.zeros((extra.shape[0], feats - rows), F32)], axis=1)
    packed_out[rows:top, :] = wide.astype(BF16)


def dispatch(code, rows, outs):
    share = outs[0].shape[0]
    for k, out in enumerate(outs):
        ids = lax.broadcasted_iota(jnp.int32, (share, code.shape[1]), 0) + k * share
        marks = jnp.where(ids == code, 1.0, 0.0).astype(BF16)
        out[...] = dot_nn(marks, rows).astype(BF16)


def residual_kernel(
    meta, route, slot, tokens, m0, m1, m2, m3, w0, w1, w2, w3,
    residual_out, gate_out, probs_out, params_out, *rest,
):
    outs, place = rest[:-1], rest[-1]
    share = outs[0].shape[0]
    experts = probs_out.shape[1]
    cols = m0.shape[0]
    for j, w in enumerate((w0, w1, w2, w3)):
        place[meta[0] ^ j] = w[cols:, :cols].astype(F32)
    params = jnp.concatenate([place[r] for r in range(4)], axis=1)
    router = params[:experts]
    gain = params[experts : experts + 1]
    for i in (1, 2):
        gain = gain + params[experts + i : experts + i + 1]
    params_out[...] = jnp.concatenate([router, jnp.broadcast_to(gain, (8, gain.shape[1]))], axis=0)
    residual = tokens[...].astype(F32)
    for m, w in ((m0, w0), (m1, w1), (m2, w2), (m3, w3)):
        residual = residual + dot_tn(m[...], w[:cols, :])
    residual_out[...] = residual
    normed = residual * row_scale(residual) * gain
    part = slot[...] - meta[0] * share
    code = jnp.where(
        (part >= 0) & (part < share), (route[...] ^ meta[1]) * share + part, -1
    ).reshape(1, part.shape[0])
    dispatch(code, normed.astype(BF16), outs)
    probs = softmax_rows(dot_nt(normed, router, PRECISE))
    probs_out[...] = probs
    lanes = lax.broadcasted_iota(jnp.int32, probs.shape, 1)
    where = as_column(route[...].reshape(1, part.shape[0]))
    gate_out[...] = jnp.sum(jnp.where(lanes == where, probs, 0.0), axis=1, keepdims=True)


def assemble_kernel(*refs, count):
    out = refs[-1]
    size = refs[0].shape[0]
    for i, block in enumerate(refs[:count]):
        out[i * size : (i + 1) * size, :] = block[...]


def expert_kernel(
    meta, x0, x1, x2, x3, c0, c1, c2, c3, w_in, w_out, router,
    rows_out, act_out, cots_out, d_hidden_out, keep_out, send_out, turned_out,
    x_all, c_all, part_all, *, first, direct,
):
    rank, expert = meta[0], meta[1]
    ranks = 4
    total = rows_out.shape[0]
    feats = rows_out.shape[1]
    cols = feats // ranks
    if direct:
        sources, _, share, _ = x_all.shape
        cap = ranks * share
        for j, (x, c) in enumerate(((x0, c0), (x1, c1), (x2, c2), (x3, c3))):
            for s in range(sources):
                x_all[s, rank ^ j] = x[s * share : (s + 1) * share, :]
                at = (first + s) * cols
                c_all[rank ^ j, :, s * cap : (s + 1) * cap] = c[at : at + cols, :]
            at = c.shape[0] - turned_out.shape[2] // cap * cols
            for i in range(turned_out.shape[2] // cap):
                turned_out[rank ^ j, :, i * cap : (i + 1) * cap] = c[
                    at + i * cols : at + (i + 1) * cols, :
                ]
        step = 256 // cap
    for i in range(total // 256):
        span = slice(i * 256, (i + 1) * 256)
        if direct:
            rows = x_all[i * step : (i + 1) * step].reshape(256, feats)
            turned = jnp.concatenate([c_all[r, :, span] for r in range(ranks)], axis=0)
            cots = turned.astype(F32).T.astype(BF16)
        else:
            rows = x0[span, :]
            cots = c0[span, :]
        rows_out[span, :] = rows
        probs = softmax_rows(dot_nt(rows, router[...].astype(BF16)))
        lanes = lax.broadcasted_iota(jnp.int32, probs.shape, 1)
        gate = jnp.sum(jnp.where(lanes == expert, probs, 0.0), axis=1, keepdims=True)
        cots_out[span, :] = (gate * cots.astype(F32)).astype(BF16)
        hidden = dot_nn(rows, w_in[...])
        pull = dot_nt(cots, w_out[...])
        bent = jnp.tanh(GELU_C * (hidden + GELU_A * hidden * hidden * hidden))
        act = (0.5 * hidden * (1.0 + bent)).astype(BF16)
        act_out[span, :] = act
        slope = 0.5 * (1.0 + bent) + 0.5 * hidden * (1.0 - bent * bent) * (
            GELU_C * (1.0 + 3.0 * GELU_A * hidden * hidden)
        )
        d_hidden = (gate * pull * slope).astype(BF16)
        d_hidden_out[span, :] = d_hidden
        d_gate = jnp.sum(pull * act.astype(F32), axis=1, keepdims=True)
        d_part = dot_nt(w_in[...], d_hidden).astype(BF16)
        tail = jnp.broadcast_to(d_gate, (256, 128)).T[: part_all.shape[1] - cols].astype(BF16)
        for r in range(ranks):
            j = rank ^ r
            place = (j % 2) * 2 + j // 2
            part_all[place, :cols, span] = d_part[r * cols : (r + 1) * cols, :]
            part_all[place, cols:, span] = tail
    keep_out[...] = part_all[0:2]
    send_out[...] = part_all[2:4]


def expert_out_kernel(meta, w_out, *refs, groups):
    acts, (keep_out, send_out, part_all) = refs[:groups], refs[-3:]
    rank = meta[0]
    ranks = 4
    cols = part_all.shape[1]
    at = 0
    for act in acts:
        for i in range(0, act.shape[0], 256):
            part = dot_nn(act[i : i + 256, :], w_out[...]).T.astype(BF16)
            for r in range(ranks):
                j = rank ^ r
                part_all[(j % 2) * 2 + j // 2, :, at : at + 256] = part[r * cols : (r + 1) * cols]
            at += 256
    keep_out[...] = part_all[0:2]
    send_out[...] = part_all[2:4]


def slot_marks(meta, route, slot, cap, count):
    code = slot_codes(meta, route, slot, cap)
    ids = lax.broadcasted_iota(jnp.int32, (code.shape[1], count), 1)
    return jnp.where(ids == as_column(code), 1.0, 0.0).astype(BF16)


def fence_kernel(*refs):
    del refs


def side_by_side(blocks, came):
    size = blocks[0].shape[1]
    for k, block in enumerate(blocks):
        came[:, k * size : (k + 1) * size] = block[...]
    return came[...]


def combine_kernel(meta, route, slot, *rest, cap):
    *blocks, _, out, came = rest
    marks = slot_marks(meta, route, slot, cap, came.shape[1])
    out[...] = dot_nt(side_by_side(blocks, came), marks).astype(BF16)


def block_out_kernel(meta, route, slot, residual, gate, *rest, cap):
    *blocks, block_out, came, place = rest
    rank = meta[0]
    cols = block_out.shape[1]
    marks = slot_marks(meta, route, slot, cap, came.shape[1])
    returned = dot_nt(marks, side_by_side(blocks, came))
    for r in range(4):
        place[r] = residual[:, r * cols : (r + 1) * cols]
    block_out[...] = (place[rank] + gate[...] * returned).astype(BF16)


def put_chunks(grads, keep, send, place, expert, order):
    count = len(order)
    size = grads.shape[0] // count
    for c in range(count):
        place[c ^ expert] = grads[c * size : (c + 1) * size, :]
    for i, k in enumerate(order):
        out = keep if i < count // 2 else send
        at = (i % (count // 2)) * size
        out[at : at + size, :] = place[k]


def residual_back_kernel(
    meta, r0, r1, r2, r3, residual, gate, probs, route, params, cotangent, mixed, w_attn_out,
    attn_probs, normed_one, _, d_attn_cols_out, d_mixed_out, d_value_out, router_grad_out,
    gain_grad_out, first_out, second_out, place, place_f32, chunk_place, *, chunked,
):
    rank, expert = meta[0], meta[1]
    experts = probs.shape[1]
    feats = residual.shape[1]
    cols = feats // 4
    length = residual.shape[0]
    router = params[:experts, :]
    gain = params[experts : experts + 1, :]
    for j, r in enumerate((r0, r1, r2, r3)):
        place[rank ^ j] = r[:cols, :]
    d_gate = as_column(r0[cols : cols + 1, :].astype(F32))
    d_routed = jnp.concatenate([place[r] for r in range(4)], axis=0).astype(F32).T
    res = residual[...]
    scale = row_scale(res)
    lanes = lax.broadcasted_iota(jnp.int32, probs.shape, 1)
    onehot = jnp.where(lanes == as_column(route[...].reshape(1, length)), 1.0, 0.0)
    d_logits = d_gate * probs[...] * (onehot - gate[...])
    d_normed = d_routed + dot_nn(d_logits, router, PRECISE)
    normed = res * scale * gain
    router_grad = dot_tn(d_logits, normed, PRECISE)
    gain_grad = jnp.sum(d_normed * res * scale, axis=0, keepdims=True)
    cross = jnp.sum(gain * res * d_normed, axis=1, keepdims=True)
    d_residual = (
        cotangent[...].astype(F32).T
        + scale * gain * d_normed
        - res * (scale * scale * scale * cross * (1.0 / feats))
    )
    for r in range(4):
        own = slice(r * cols, (r + 1) * cols)
        place_f32[r] = d_residual[:, own]

        @pl.when(rank == r)
        def _():
            router_grad_out[...] = router_grad[:, own]
            gain_grad_out[...] = gain_grad[:, own]

    d_attn_cols_out[...] = place_f32[rank]
    d_attn = d_residual.astype(BF16)
    attn_grad = dot_nn(mixed[...], d_attn).astype(BF16)
    d_mixed = dot_nt(d_attn, w_attn_out[...]).astype(BF16)
    d_mixed_out[...] = d_mixed
    for h in range(cols // HDIM):
        own = slice(h * HDIM, (h + 1) * HDIM)
        total = jnp.zeros((length, HDIM), F32)
        for c in range(0, length, CHUNK):
            span = slice(c, c + CHUNK)
            total = total + dot_tn(attn_probs[h, span, :], d_mixed[span, own])
        d_value_out[:, own] = total.astype(BF16)
    value_grad = dot_tn(d_value_out[...], normed_one[...]).astype(BF16)
    if chunked:
        both = jnp.concatenate([attn_grad, value_grad], axis=0)
        put_chunks(both, first_out, second_out, chunk_place, expert, chunked)
    else:
        first_out[...] = attn_grad
        second_out[...] = value_grad


def attend_back_kernel(
    query, key, value, probs, d_mixed, bucket, d_query, d_key, table_out, *, buckets
):
    length = query.shape[0]
    width = 2 * length
    heads = query.shape[1] // HDIM
    marks = bucket_marks(bucket, buckets)
    zeros = jnp.zeros((8, width - length), F32)
    table_out[...] = jnp.zeros(table_out.shape, F32)
    for h in range(heads):
        own = slice(h * HDIM, (h + 1) * HDIM)
        dk = jnp.zeros((length, HDIM), F32)
        diagonals = jnp.zeros((8, width), F32)
        for c in range(0, length, CHUNK):
            span = slice(c, c + CHUNK)
            weights = probs[h, span, :].astype(F32)
            d_probs = dot_nt(d_mixed[span, own], value[:, own])
            inner = jnp.sum(d_probs * weights, axis=1, keepdims=True)
            d_scores = weights * (d_probs - inner)
            for b in range(CHUNK // 8):
                piece = jnp.concatenate([d_scores[8 * b : 8 * b + 8, :], zeros], axis=1)
                diagonals = diagonals + pltpu.roll(piece, (length - 1 - c - 8 * b) % width, 1)
            low = d_scores.astype(BF16)
            d_query[span, own] = (dot_nn(low, key[:, own]) * SCORE_SCALE).astype(BF16)
            dk = dk + dot_tn(low, query[span, own])
        d_key[:, own] = (dk * SCORE_SCALE).astype(BF16)
        line = diagonals[0:1]
        for r in range(1, 8):
            line = line + pltpu.roll(diagonals[r : r + 1], width - r, 1)
        table_col = jnp.sum(jnp.where(marks, line, 0.0), axis=1, keepdims=True)
        table_out[h : h + 1, :buckets] = jnp.broadcast_to(table_col, (buckets, 128)).T[0:1, :]


def put_split(out, at, row, value):
    high = value.astype(BF16).astype(F32)
    out[row : row + 1, at : at + value.shape[1]] = high
    out[row + 8 : row + 9, at : at + value.shape[1]] = value - high


def query_back_kernel(
    meta, tokens, gain, normed, d_query, d_key, d_value, w_query, w_key, w_value, gain2_grad,
    table_grad, router_grad, _, _got, *rest, chunked, heads, buckets,
):
    keep_in, send_in, gain1_out, first_out, second_out, place, chunk_place, pack = rest
    rank, expert = meta[0], meta[1]
    length, feats = tokens.shape
    cols = feats // 4
    normed_rows = normed[...]
    query_grad = dot_tn(d_query[...], normed_rows).astype(BF16)
    key_grad = dot_tn(d_key[...], normed_rows).astype(BF16)
    d_normed = (
        dot_nn(d_query[...], w_query[...])
        + dot_nn(d_key[...], w_key[...])
        + dot_nn(d_value[...], w_value[...])
    )
    rows = tokens[...].astype(F32)
    product = d_normed * rows
    gain1_grad = jnp.sum(product * row_scale(rows), axis=0, keepdims=True)
    gain1_out[...] = jnp.broadcast_to(gain1_grad, gain1_out.shape)
    if chunked:
        pack[...] = jnp.zeros(pack.shape, F32)
        put_split(pack, 0, 0, gain1_grad)
        put_split(pack, 0, 1, gain2_grad[...])
        for h in range(heads):
            put_split(pack, 256 * h, 2, table_grad[h : h + 1, :])
        for e in range(router_grad.shape[0]):
            put_split(pack, 256 * (e % 3), 3 + e // 3, router_grad[e : e + 1, :])
        small = pack[...].astype(BF16)
        both = jnp.concatenate([query_grad, key_grad], axis=0)
        put_chunks(both, first_out, second_out, chunk_place, expert, chunked)
        for out in (first_out, second_out):
            out[out.shape[0] - 16 :, :] = small
    else:
        first_out[...] = query_grad
        second_out[...] = key_grad
    cross = jnp.sum(product * gain[...].reshape(1, feats), axis=1, keepdims=True)
    high = cross.astype(BF16).astype(F32)
    low = cross - high
    lanes = lax.broadcasted_iota(jnp.int32, (length, place.shape[2] - cols), 1)
    extra = jnp.where(lanes == 0, high, jnp.where(lanes == 1, low, 0.0)).astype(BF16)
    for r in range(4):
        j = rank ^ r
        own = d_normed[:, r * cols : (r + 1) * cols].astype(BF16)
        place[(j % 2) * 2 + j // 2] = jnp.concatenate([own, extra], axis=1)
    keep_in[...] = place[0:2]
    send_in[...] = place[2:4]


def input_kernel(
    meta, tokens, gain, d_attn_cols, first, second, *rest
):
    *_, out, place, gain_place = rest
    rank = meta[0]
    feats = tokens.shape[1]
    cols = feats // 4
    rows = tokens[...].astype(F32)
    scale = row_scale(rows)
    both = first[...].astype(F32) + second[...].astype(F32)
    cross = both[:, cols : cols + 1] + both[:, cols + 1 : cols + 2]
    gain_row = gain[...].reshape(1, feats)
    for r in range(4):
        place[r] = rows[:, r * cols : (r + 1) * cols]
        gain_place[r] = gain_row[:, r * cols : (r + 1) * cols]
    own = both[:, :cols]
    own_rows = place[rank]
    out[...] = (
        d_attn_cols[...]
        + scale * gain_place[rank] * own
        - own_rows * (scale * scale * scale * cross * (1.0 / feats))
    )


def add_small(a, b):
    at = a.shape[0] - 16
    total = (
        a[at : at + 8, :].astype(F32)
        + b[at : at + 8, :].astype(F32)
        + a[at + 8 :, :].astype(F32)
        + b[at + 8 :, :].astype(F32)
    )
    high = total.astype(BF16).astype(F32)
    return total, jnp.concatenate([high, total - high], axis=0).astype(BF16)


def sum_kernel(keep, got, keep_out, send_out, token_out):
    token_out[...] = jnp.zeros(token_out.shape, F32)
    half = (keep.shape[0] - 16) // 2
    total = (keep[: 2 * half, :].astype(F32) + got[: 2 * half, :].astype(F32)).astype(BF16)
    _, small = add_small(keep, got)
    keep_out[:half, :] = total[:half]
    send_out[:half, :] = total[half:]
    keep_out[half:, :] = small
    send_out[half:, :] = small


def last_sum_kernel(keep, got, mine_out, small_out, gain1_out):
    size = mine_out.shape[0]
    mine_out[...] = (keep[:size, :].astype(F32) + got[:size, :].astype(F32)).astype(BF16)
    total, _ = add_small(keep, got)
    small_out[...] = total
    gain1_out[...] = jnp.broadcast_to(total[0:1], gain1_out.shape)


def spread_kernel(meta, mine, second, other, first_out, second_out, place, *, order):
    expert = meta[1]
    count = len(order)
    size = mine.shape[0] // 2
    quarter = count // 4
    for i in range(count):
        block, at = (
            (mine, i)
            if i < quarter
            else (second, i - quarter) if i < 2 * quarter else (other, i - 2 * quarter)
        )
        place[order[i]] = block[at * size : (at + 1) * size, :]
    rows = first_out.shape[0]
    for c in range(count):
        chunk = place[c ^ expert].astype(F32)
        start = c * size
        if start < rows:
            first_out[start : start + size, :] = chunk
        else:
            second_out[start - rows : start - rows + size, :] = chunk


def finish_kernel(
    meta, mine, second, other, small, *rest, order, heads
):
    first_out, second_out, gain2_out, table_out, router_out, place = rest[-6:]
    spread_kernel(meta, mine, second, other, first_out, second_out, place, order=order)
    cols = gain2_out.shape[1]
    gain2_out[...] = small[1:2, :cols]
    for h in range(heads):
        table_out[h : h + 1, :] = small[2:3, 256 * h : 256 * h + table_out.shape[1]]
    for e in range(router_out.shape[0]):
        at = 256 * (e % 3)
        router_out[e : e + 1, :] = small[3 + e // 3 : 4 + e // 3, at : at + cols]


def moving(kernel, smem, fetch, total, far):
    def run(*refs):
        rest = list(refs[: len(refs) - 1])
        sems = refs[-1]
        near_out = rest[len(rest) - len(far) :] if far else []
        rest = rest[: len(rest) - len(far)]
        near_in = rest[len(rest) - fetch :] if fetch else []
        rest = rest[: len(rest) - fetch]
        copies = [
            pltpu.make_async_copy(rest[smem + i], b, sems.at[i]) for i, b in enumerate(near_in)
        ]
        for copy in copies:
            copy.start()
        for copy in copies:
            copy.wait()
        inner = list(rest)
        for i, b in enumerate(near_in):
            inner[smem + i] = b
        for b, at in zip(near_out, far):
            inner[total + at] = b
        kernel(*inner)
        copies = [
            pltpu.make_async_copy(b, rest[total + at], sems.at[fetch + i])
            for i, (b, at) in enumerate(zip(near_out, far))
        ]
        for copy in copies:
            copy.start()
        for copy in copies:
            copy.wait()

    return run


def call(kernel, outs, scratch, *operands, weight=1.0, smem=1, fetch=0, far=(), after=()):
    specs, given = [], []
    for i, operand in enumerate(operands):
        if i < smem:
            specs.append(pl.BlockSpec(memory_space=pltpu.SMEM))
        elif i < smem + fetch:
            specs.append(pl.BlockSpec(memory_space=pltpu.HBM))
            operand = pltpu.with_memory_space_constraint(operand, pltpu.HBM)
        else:
            specs.append(pl.BlockSpec(memory_space=pltpu.VMEM))
        given.append(operand)
    specs += [pl.BlockSpec(memory_space=pl.ANY)] * len(after)
    scratch_shapes = [pltpu.VMEM(shape, kind) for shape, kind in scratch]
    shapes, out_specs = [], []
    for i, (shape, kind) in enumerate(outs):
        shapes.append(pltpu.HBM(shape, kind) if i in far else jax.ShapeDtypeStruct(shape, kind))
        out_specs.append(pl.BlockSpec(memory_space=pltpu.HBM if i in far else pltpu.VMEM))
    if fetch or far:
        kernel = moving(kernel, smem, fetch, len(operands) + len(after), far)
        scratch_shapes += [pltpu.VMEM(a.shape, a.dtype) for a in operands[smem : smem + fetch]]
        scratch_shapes += [pltpu.VMEM(*outs[i]) for i in far]
        scratch_shapes.append(pltpu.SemaphoreType.DMA((fetch + len(far),)))
    return pl.pallas_call(
        kernel,
        out_shape=shapes,
        in_specs=specs,
        out_specs=out_specs,
        scratch_shapes=scratch_shapes,
        compiler_params=pltpu.CompilerParams(vmem_limit_bytes=32 * 1024 * 1024),
        cost_estimate=pl.CostEstimate(
            flops=int(weight * 1.1e9), bytes_accessed=1 << 16, transcendentals=0
        ),
    )(*given, *after)


def swap(array, axis, bit):
    size = lax.axis_size(axis)
    return lax.ppermute(array, axis, [(i, i ^ bit) for i in range(size)])


def add_low(a, b):
    return (a.astype(F32) + b.astype(F32)).astype(BF16)


def gather_four(array):
    across = swap(array, "tensor", 2)
    beside = swap(array, "tensor", 1)
    return [array, beside, across, swap(across, "tensor", 1)]


def reduce_four(keep, send):
    got = swap(send, "tensor", 1)
    far = add_low(keep[1], got[1])
    return add_low(keep[0], got[0]), swap(far, "tensor", 2), far


def exchange(blocks):
    if len(blocks) > 8:
        return hyper_exchange(blocks)[0]
    return [blocks[0]] + [swap(b, "expert", k) for k, b in enumerate(blocks) if k]


def hyper_exchange(blocks, gates=None):
    count = len(blocks)
    held = {k: [b] for k, b in enumerate(blocks)}
    steps = []
    bit = 1
    while bit < count:
        away = [k for k in sorted(held) if k & bit]
        sent = jnp.concatenate([b for k in away for b in held[k]], axis=0)
        if gates and bit in gates:
            (sent,) = fence([sent], gates[bit])
        got = swap(sent, "expert", bit)
        if gates and -bit in gates:
            (got,) = fence([got], gates[-bit])
        steps.append(got)
        size = blocks[0].shape[0]
        at = 0
        fresh = {}
        for k in away:
            pieces = [got[at + i * size : at + (i + 1) * size] for i in range(len(held[k]))]
            at += len(held[k]) * size
            fresh[k ^ bit] = held[k ^ bit] + pieces
        held = fresh
        bit *= 2
    return held[0], steps


ORDER = (0, 4, 2, 6, 1, 5, 3, 7)


def gather_chunks(mine, gates=None):
    held = swap(mine, "expert", 4)
    if gates:
        (held,) = fence([held], (gates[0],))
    held = jnp.concatenate([mine, held], axis=0)
    beside = swap(held, "expert", 2)
    if gates:
        (beside,) = fence([beside], (gates[1],))
    return held, beside, swap(jnp.concatenate([held, beside], axis=0), "expert", 1)


def halve_plain(keep, got, gates):
    for bit, gate in zip((2, 4), gates):
        half = keep.shape[0] // 2
        sent = add_low(keep[half:], got[half:])
        keep = add_low(keep[:half], got[:half])
        (got,) = fence([swap(sent, "expert", bit)], (gate,))
    return add_low(keep, got)


def halve(keep, send):
    feats = keep.shape[1]
    steps = []
    for bit in (1, 2):
        rows = (keep.shape[0] - 16) // 2 + 16
        keep, send, token = call(
            sum_kernel, [((rows, feats), BF16)] * 2 + [((8, 128), F32)], [], keep, swap(send, "expert", bit), smem=0
        )
        steps.append(token)
    last = call(
        last_sum_kernel,
        [((keep.shape[0] - 16, feats), BF16), ((8, feats), F32), ((8, feats), F32)],
        [],
        keep, swap(send, "expert", 4), smem=0,
    )
    return last, steps


def fence(arrays, after):
    count = len(arrays)
    return pl.pallas_call(
        fence_kernel,
        out_shape=[jax.ShapeDtypeStruct(a.shape, a.dtype) for a in arrays],
        in_specs=[pl.BlockSpec(memory_space=pl.ANY)] * (count + len(after)),
        out_specs=[pl.BlockSpec(memory_space=pl.ANY)] * count,
        input_output_aliases={i: i for i in range(count)},
    )(*arrays, *after)


def on_device(
    tokens, cotangent, norm1_gain, w_query, w_key, w_value, w_attn_out, bias_table, norm2_gain,
    w_router, expert_in, expert_out, route, slot, segment, rel_bucket,
):
    length, feats = tokens.shape
    cols = cotangent.shape[1]
    heads = cols // HDIM
    experts = lax.axis_size("expert")
    cap = 2 * length // experts
    share = cap // 4
    rank = lax.axis_index("tensor").astype(jnp.int32)
    expert = lax.axis_index("expert").astype(jnp.int32)
    meta = jnp.stack([rank, expert])
    total = experts * cap
    direct = share % 16 == 0
    buckets = bias_table.shape[0]
    chunked = ORDER if experts == len(ORDER) else None

    w_query_t, w_key_t, w_value_t = w_query.T, w_key.T, w_value.T
    packed_rows = cols + -(-(experts + 3) // 16) * 16
    packed, cot_own, *cot_blocks = call(
        first_kernel,
        [((packed_rows, feats), BF16), ((length // cap * cols, cap), BF16)] + [((cols, cap), BF16)] * experts,
        [],
        meta, route, slot, cotangent.T, w_attn_out, w_router.T, norm2_gain,
        weight=2.0, fetch=6,
    )
    packed_parts = gather_four(packed)
    bucket = jnp.concatenate([rel_bucket, jnp.full((1,), -1, jnp.int32)])
    normed, query, key, value, probs, mixed, mixed_token = call(
        attend_kernel,
        [((length, feats), BF16)]
        + [((length, cols), BF16)] * 3
        + [((heads, length, length), BF16), ((cols, length), BF16), ((8, 128), F32)],
        [((length, length), F32)],
        tokens, w_query.T, w_key.T, w_value.T, norm1_gain, segment, bucket, bias_table.T,
        weight=7.0, smem=0, fetch=8, far=(0, 1, 2, 3, 4),
    )

    mixed_parts = gather_four(mixed)
    residual, gate, router_probs, params, *row_blocks = call(
        residual_kernel,
        [
            ((length, feats), F32),
            ((length, 1), F32),
            ((length, experts), F32),
            ((experts + 8, feats), F32),
        ]
        + [((share, feats), BF16)] * experts,
        [((4, packed_rows - cols, cols), F32)],
        meta, route, slot, tokens, *mixed_parts, *packed_parts,
        weight=5.8, fetch=3, far=(0, 1, 2),
    )
    cot_arrived, _ = hyper_exchange(
        cot_blocks, {2: (mixed_token,), -4: (residual,)}
    )
    if direct:
        cot_arrived = cot_arrived + [cot_own]
    else:
        cot_turned = lax.all_gather(cotangent.T, "tensor", axis=0, tiled=True)
    cot_rows = gather_four(jnp.concatenate(cot_arrived, axis=0))
    arrived = exchange(row_blocks)
    groups = GROUPS if direct else 1
    group_size = experts // groups
    row_groups = []
    for g in range(groups):
        blocks = arrived[g * group_size : (g + 1) * group_size]
        if direct:
            (packed,) = call(
                functools.partial(assemble_kernel, count=group_size),
                [((group_size * share, feats), BF16)],
                [],
                *blocks,
                weight=1.0, smem=0, after=(cot_rows[2],),
            )
        else:
            packed = jnp.concatenate(blocks, axis=0)
        row_groups.append(gather_four(packed))

    if not direct:
        def assemble(parts, shape, turn):
            stacked = jnp.stack(parts).reshape(4, experts, *shape)
            stacked = stacked[rank ^ jnp.arange(4, dtype=jnp.int32)]
            return [jnp.transpose(stacked, turn).reshape(total, feats)]

        one = jnp.zeros((16, 128), BF16)
        row_groups = [assemble(row_groups[0], (share, feats), (1, 0, 2, 3)) + [one] * 3]
        cot_rows = assemble(cot_rows, (cols, cap), (1, 3, 0, 2)) + [one] * 3
    w_in, w_out = expert_in[0], expert_out[0]
    hidden_count = w_in.shape[1]
    part_rows = cols + 16
    count = total // groups
    x_shape = (group_size, 4, share, feats) if direct else (1, 1, 16, 128)
    c_shape = (4, cols, count) if direct else (1, 16, 128)
    acts, returning, kept = [], [], []
    for g in range(groups):
        rows_all, act, cots, d_hidden, keep, send, turned = call(
            functools.partial(expert_kernel, first=g * group_size, direct=direct),
            [((count, feats), BF16), ((count, hidden_count), BF16), ((count, feats), BF16),
             ((count, hidden_count), BF16), ((2, part_rows, count), BF16),
             ((2, part_rows, count), BF16), ((4, cols, length) if direct else (1, 16, 128), BF16)],
            [(x_shape, BF16), (c_shape, BF16), ((4, part_rows, count), BF16)],
            meta, *row_groups[g], *cot_rows, w_in, w_out, params[:experts],
            weight=10.0, far=(0, 1, 2, 3, 6) if direct else (),
        )
        if direct:
            cot_turned = turned.reshape(feats, length)
        near, far, met = reduce_four(keep, send)
        whole = add_low(near, far)
        returning += [whole[:, k * cap : (k + 1) * cap] for k in range(group_size)]
        acts.append(act)
        kept += [act, cots, rows_all, d_hidden]

    kept = fence(kept, (met,))
    expert_out_grad = sum(dot_tn(kept[4 * g], kept[4 * g + 1]) for g in range(groups))
    expert_in_grad = sum(dot_tn(kept[4 * g + 2], kept[4 * g + 3]) for g in range(groups))

    def unite(blocks):
        return blocks if cap % 128 == 0 else [jnp.concatenate(blocks, axis=1)]

    keep_fwd, send_fwd = call(
        functools.partial(expert_out_kernel, groups=groups),
        [((2, cols, total), BF16)] * 2,
        [((4, cols, total), BF16)],
        meta, w_out, *acts,
        weight=2.9, after=(whole, expert_out_grad, expert_in_grad),
    )
    (d_routed,) = call(
        functools.partial(combine_kernel, cap=cap),
        [((part_rows, length), BF16)],
        [((part_rows, total), BF16)],
        meta, route, slot, *unite(exchange(returning)), after=(keep_fwd,),
        weight=1.0,
    )
    routed_parts = gather_four(d_routed)

    near_fwd, far_fwd, met_fwd = reduce_four(keep_fwd, send_fwd)
    whole_fwd = add_low(near_fwd, far_fwd)
    fwd_arrived, fwd_steps = hyper_exchange(
        [whole_fwd[:, k * cap : (k + 1) * cap] for k in range(experts)]
    )
    came_fwd = unite(fwd_arrived)
    (block_out,) = call(
        functools.partial(block_out_kernel, cap=cap),
        [((length, cols), BF16)],
        [((cols, total), BF16), ((4, length, cols), F32)],
        meta, route, slot, residual, gate, *came_fwd,
        weight=1.2,
    )

    if chunked:
        size = 2 * cols // experts
        grad_outs = [((experts // 2 * size + 16, feats), BF16)] * 2
        chunk_scratch = ((experts, size, feats), BF16)
    else:
        grad_outs = [((cols, feats), BF16)] * 2
        chunk_scratch = ((16, 128), BF16)
    d_attn_cols, d_mixed, d_value, router_grad, gain2_grad, *first_grads = call(
        functools.partial(residual_back_kernel, chunked=chunked),
        [((length, cols), F32), ((length, cols), BF16), ((length, cols), BF16),
         ((experts, cols), F32), ((1, cols), F32)]
        + [((cols, feats), BF16)] * 2,
        [((4, cols, length), BF16), ((4, length, cols), F32), chunk_scratch],
        meta, *routed_parts, residual, gate, router_probs, route, params, cot_turned, mixed,
        w_attn_out, probs, normed, after=(met_fwd,),
        weight=8.0, far=(0,),
    )
    d_query, d_key, table_grad = call(
        functools.partial(attend_back_kernel, buckets=buckets),
        [((length, cols), BF16)] * 2 + [((8, 128), F32)],
        [],
        query, key, value, probs, d_mixed, bucket, smem=0,
        weight=7.0,
    )
    wide = -(-(cols + 2) // 128) * 128
    first_got = swap(first_grads[1], "expert", 1) if chunked else d_query
    keep_in, send_in, gain1_grad, *second_grads = call(
        functools.partial(query_back_kernel, chunked=chunked, heads=heads, buckets=buckets),
        [((2, length, wide), BF16)] * 2 + [((8, feats), F32)] + grad_outs,
        [((4, length, wide), BF16), chunk_scratch, ((16, feats), F32)],
        meta, tokens, norm1_gain, normed, d_query, d_key, d_value, w_query_t, w_key_t,
        w_value_t, gain2_grad, table_grad, router_grad, after=(whole_fwd, first_got),
        weight=4.0,
    )
    near_in, far_in, _ = reduce_four(keep_in, send_in)
    (input_grad,) = call(
        input_kernel,
        [((length, cols), F32)],
        [((4, length, cols), F32), ((4, 1, cols), F32)],
        meta, tokens, norm1_gain, d_attn_cols, near_in, far_in,
        weight=1.0,
    )

    if chunked:
        (mine, small, gain1_grad), steps = halve(*second_grads)
        second_chunks = gather_chunks(mine)
        attn_grad, value_grad = call(
            functools.partial(spread_kernel, order=ORDER),
            [((cols, feats), F32)] * 2,
            [chunk_scratch],
            meta,
            *gather_chunks(
                halve_plain(first_grads[0], *fence([first_got], steps[:1]), (steps[1], small)),
                (second_chunks[0][:16, :128], second_chunks[1][:16, :128]),
            ),
            weight=1.6,
        )
        for bit in (1, 2):
            gain1_grad = gain1_grad + swap(gain1_grad, "tensor", bit)
        query_grad, key_grad, gain2_grad, table_grad, router_grad = call(
            functools.partial(finish_kernel, order=ORDER, heads=heads),
            [((cols, feats), F32)] * 2
            + [((1, cols), F32), ((heads, buckets), F32), ((experts, cols), F32)],
            [chunk_scratch],
            meta, *second_chunks, small,
            weight=1.6, after=(input_grad, block_out, gain1_grad, attn_grad),
        )
    else:
        query_grad, key_grad, gain2_grad, table_grad, router_grad = lax.psum(
            (*second_grads, gain2_grad, table_grad[:heads, :buckets], router_grad), "expert"
        )
        gain1_grad = lax.psum(gain1_grad, ("expert", "tensor"))
        attn_grad, value_grad = lax.psum(tuple(first_grads), "expert")
    return (
        block_out,
        input_grad,
        gain1_grad[0],
        query_grad.astype(F32).T,
        key_grad.astype(F32).T,
        value_grad.astype(F32).T,
        attn_grad.astype(F32),
        table_grad.T,
        gain2_grad[0],
        router_grad.T,
        expert_in_grad[None],
        expert_out_grad[None],
    )


def solution(mesh):
    return jax.shard_map(
        on_device,
        mesh=mesh,
        in_specs=(
            P("expert", None),
            P("expert", "tensor"),
            P(),
            P(None, "tensor"),
            P(None, "tensor"),
            P(None, "tensor"),
            P("tensor", None),
            P(None, "tensor"),
            P("tensor"),
            P("tensor", None),
            P("expert", None, "tensor"),
            P("expert", "tensor", None),
            P("expert"),
            P("expert"),
            P("expert"),
            P(),
        ),
        out_specs=(
            P("expert", "tensor"),
            P("expert", "tensor"),
            P(),
            P(None, "tensor"),
            P(None, "tensor"),
            P(None, "tensor"),
            P("tensor", None),
            P(None, "tensor"),
            P("tensor"),
            P("tensor", None),
            P("expert", None, "tensor"),
            P("expert", "tensor", None),
        ),
        check_vma=False,
    )
```

```python
import functools

import jax
import jax.numpy as jnp
from jax import lax
from jax.experimental import pallas as pl
from jax.experimental.pallas import tpu as pltpu
from jax.sharding import PartitionSpec as P

HDIM = 64
EPSILON = 1e-06
MASKED_SCORE = -1e30
SCORE_SCALE = 0.125
PRECISE = lax.Precision.HIGHEST
F32 = jnp.float32
BF16 = jnp.bfloat16
GELU_C = 0.7978845608028654
GELU_A = 0.044715
CHUNK = 128
GROUPS = 1


def dot_nn(a, b, precision=None):
    return lax.dot_general(
        a, b, (((1,), (0,)), ((), ())), precision=precision, preferred_element_type=F32
    )


def dot_nt(a, b, precision=None):
    return lax.dot_general(
        a, b, (((1,), (1,)), ((), ())), precision=precision, preferred_element_type=F32
    )


def dot_tn(a, b, precision=None):
    return lax.dot_general(
        a, b, (((0,), (0,)), ((), ())), precision=precision, preferred_element_type=F32
    )


def row_scale(rows):
    return lax.rsqrt(jnp.mean(rows * rows, axis=1, keepdims=True) + EPSILON)


def bucket_marks(bucket, count):
    width = bucket.shape[0]
    return lax.broadcasted_iota(jnp.int32, (count, width), 0) == bucket[...].reshape(1, width)


def in_order(blocks, rank, place, axis):
    for j, block in enumerate(blocks):
        place[rank ^ j] = block[...]
    return jnp.concatenate([place[r] for r in range(len(blocks))], axis=axis)


def as_column(row):
    return jnp.broadcast_to(row, (128, row.shape[1])).T[:, 0:1]


def softmax_rows(logits):
    shifted = jnp.exp(logits - jnp.max(logits, axis=1, keepdims=True))
    return shifted / jnp.sum(shifted, axis=1, keepdims=True)


def attend_kernel(
    tokens, w_query, w_key, w_value, gain, segment, bucket, table,
    normed_out, query_out, key_out, value_out, probs_out, mixed_out, token_out,
    band,
):
    length = tokens.shape[0]
    width = 2 * length
    heads = query_out.shape[1] // HDIM
    marks = bucket_marks(bucket, table.shape[1])
    table_rows = jnp.broadcast_to(table[...][:, None, :], (heads, 128, table.shape[1]))
    bases = []
    for h in range(heads):
        offsets = jnp.sum(
            jnp.where(marks, table_rows[h].T[:, 0:1], 0.0), axis=0, keepdims=True
        )
        bases.append(
            jnp.concatenate(
                [offsets] + [pltpu.roll(offsets, r, 1) for r in range(1, 8)], axis=0
            )
        )
    token_out[...] = jnp.zeros(token_out.shape, F32)
    seg_row = segment[...].reshape(1, length)
    seg_col = as_column(seg_row)
    rows = tokens[...].astype(F32)
    normed = (rows * row_scale(rows) * gain[...].reshape(1, rows.shape[1])).astype(BF16)
    normed_out[...] = normed
    query = dot_nt(normed, w_query[...]).astype(BF16)
    key = dot_nt(normed, w_key[...]).astype(BF16)
    query_out[...] = query
    key_out[...] = key
    value_out[...] = dot_nt(normed, w_value[...]).astype(BF16)
    value_turned = dot_nt(w_value[...], normed).astype(BF16)
    for h in range(heads):
        cols = slice(h * HDIM, (h + 1) * HDIM)
        for b in range(length // 8):
            turned = pltpu.roll(bases[h], (length + 1 + 8 * b) % width, 1)
            band[8 * b : 8 * b + 8, :] = turned[:, :length]
        for c in range(0, length, CHUNK):
            span = slice(c, c + CHUNK)
            scores = dot_nt(query[span, cols], key[:, cols]) * SCORE_SCALE + band[span, :]
            scores = jnp.where(seg_col[span, :] == seg_row, scores, MASKED_SCORE)
            probs = softmax_rows(scores)
            probs = probs.astype(BF16)
            probs_out[h, span, :] = probs
            mixed_out[cols, span] = dot_nt(value_turned[cols, :], probs).astype(BF16)


def dispatch(code, rows, outs, transposed=False):
    share = outs[0].shape[0]
    for k, out in enumerate(outs):
        ids = lax.broadcasted_iota(jnp.int32, (share, code.shape[1]), 0) + k * share
        marks = jnp.where(ids == code[...], 1.0, 0.0).astype(BF16)
        product = dot_nt if transposed else dot_nn
        out[...] = product(marks, rows).astype(BF16)


def slot_codes(meta, route, slot, size):
    count = route.shape[0]
    return ((route[...] ^ meta[1]) * size + slot[...]).reshape(1, count)


def first_kernel(
    meta, route, slot, cotangent, w_attn_out, w_router, gain, packed_out, own_out, *outs
):
    cap = outs[0].shape[1]
    count = len(outs) * cap
    code = slot_codes(meta, route, slot, cap)
    ids = lax.broadcasted_iota(jnp.int32, (count, code.shape[1]), 0)
    marks = jnp.where(ids == code, 1.0, 0.0).astype(BF16)
    placed = dot_nt(cotangent[...], marks).astype(BF16)
    for k, out in enumerate(outs):
        out[...] = placed[:, k * cap : (k + 1) * cap]
    rows, feats = w_attn_out.shape
    for i in range(0, cotangent.shape[1], cap):
        at = i // cap * rows
        own_out[at : at + rows, :] = cotangent[:, i : i + cap]
    experts = w_router.shape[0]
    packed_out[:rows, :] = w_attn_out[...]
    top = packed_out.shape[0]
    line = gain[...].reshape(1, rows)
    high = line.astype(BF16)
    rest = line - high.astype(F32)
    mid = rest.astype(BF16)
    low = (rest - mid.astype(F32)).astype(BF16)
    pad = top - rows - experts - 3
    extra = [w_router[...].astype(F32)] + [p.astype(F32) for p in (high, mid, low)]
    extra = jnp.concatenate(extra + [jnp.zeros((pad, rows), F32)], axis=0)
    wide = jnp.concatenate([extra, jnp.zeros((extra.shape[0], feats - rows), F32)], axis=1)
    packed_out[rows:top, :] = wide.astype(BF16)


def dispatch(code, rows, outs):
    share = outs[0].shape[0]
    for k, out in enumerate(outs):
        ids = lax.broadcasted_iota(jnp.int32, (share, code.shape[1]), 0) + k * share
        marks = jnp.where(ids == code, 1.0, 0.0).astype(BF16)
        out[...] = dot_nn(marks, rows).astype(BF16)


def residual_kernel(
    meta, route, slot, tokens, m0, m1, m2, m3, w0, w1, w2, w3,
    residual_out, gate_out, probs_out, params_out, *rest,
):
    outs, place = rest[:-1], rest[-1]
    share = outs[0].shape[0]
    experts = probs_out.shape[1]
    cols = m0.shape[0]
    for j, w in enumerate((w0, w1, w2, w3)):
        place[meta[0] ^ j] = w[cols:, :cols].astype(F32)
    params = jnp.concatenate([place[r] for r in range(4)], axis=1)
    router = params[:experts]
    gain = params[experts : experts + 1]
    for i in (1, 2):
        gain = gain + params[experts + i : experts + i + 1]
    params_out[...] = jnp.concatenate([router, jnp.broadcast_to(gain, (8, gain.shape[1]))], axis=0)
    residual = tokens[...].astype(F32)
    for m, w in ((m0, w0), (m1, w1), (m2, w2), (m3, w3)):
        residual = residual + dot_tn(m[...], w[:cols, :])
    residual_out[...] = residual
    normed = residual * row_scale(residual) * gain
    part = slot[...] - meta[0] * share
    code = jnp.where(
        (part >= 0) & (part < share), (route[...] ^ meta[1]) * share + part, -1
    ).reshape(1, part.shape[0])
    dispatch(code, normed.astype(BF16), outs)
    probs = softmax_rows(dot_nt(normed, router, PRECISE))
    probs_out[...] = probs
    lanes = lax.broadcasted_iota(jnp.int32, probs.shape, 1)
    where = as_column(route[...].reshape(1, part.shape[0]))
    gate_out[...] = jnp.sum(jnp.where(lanes == where, probs, 0.0), axis=1, keepdims=True)


def assemble_kernel(*refs, count):
    out = refs[-1]
    size = refs[0].shape[0]
    for i, block in enumerate(refs[:count]):
        out[i * size : (i + 1) * size, :] = block[...]


def expert_kernel(
    meta, x0, x1, x2, x3, c0, c1, c2, c3, w_in, w_out, router,
    rows_out, act_out, cots_out, d_hidden_out, keep_out, send_out, turned_out,
    x_all, c_all, part_all, *, first, direct,
):
    rank, expert = meta[0], meta[1]
    ranks = 4
    total = rows_out.shape[0]
    feats = rows_out.shape[1]
    cols = feats // ranks
    if direct:
        sources, _, share, _ = x_all.shape
        cap = ranks * share
        for j, (x, c) in enumerate(((x0, c0), (x1, c1), (x2, c2), (x3, c3))):
            for s in range(sources):
                x_all[s, rank ^ j] = x[s * share : (s + 1) * share, :]
                at = (first + s) * cols
                c_all[rank ^ j, :, s * cap : (s + 1) * cap] = c[at : at + cols, :]
            at = c.shape[0] - turned_out.shape[2] // cap * cols
            for i in range(turned_out.shape[2] // cap):
                turned_out[rank ^ j, :, i * cap : (i + 1) * cap] = c[
                    at + i * cols : at + (i + 1) * cols, :
                ]
        step = 256 // cap
    for i in range(total // 256):
        span = slice(i * 256, (i + 1) * 256)
        if direct:
            rows = x_all[i * step : (i + 1) * step].reshape(256, feats)
            turned = jnp.concatenate([c_all[r, :, span] for r in range(ranks)], axis=0)
            cots = turned.astype(F32).T.astype(BF16)
        else:
            rows = x0[span, :]
            cots = c0[span, :]
        rows_out[span, :] = rows
        probs = softmax_rows(dot_nt(rows, router[...].astype(BF16)))
        lanes = lax.broadcasted_iota(jnp.int32, probs.shape, 1)
        gate = jnp.sum(jnp.where(lanes == expert, probs, 0.0), axis=1, keepdims=True)
        cots_out[span, :] = (gate * cots.astype(F32)).astype(BF16)
        hidden = dot_nn(rows, w_in[...])
        pull = dot_nt(cots, w_out[...])
        bent = jnp.tanh(GELU_C * (hidden + GELU_A * hidden * hidden * hidden))
        act = (0.5 * hidden * (1.0 + bent)).astype(BF16)
        act_out[span, :] = act
        slope = 0.5 * (1.0 + bent) + 0.5 * hidden * (1.0 - bent * bent) * (
            GELU_C * (1.0 + 3.0 * GELU_A * hidden * hidden)
        )
        d_hidden = (gate * pull * slope).astype(BF16)
        d_hidden_out[span, :] = d_hidden
        d_gate = jnp.sum(pull * act.astype(F32), axis=1, keepdims=True)
        d_part = dot_nt(w_in[...], d_hidden).astype(BF16)
        tail = jnp.broadcast_to(d_gate, (256, 128)).T[: part_all.shape[1] - cols].astype(BF16)
        for r in range(ranks):
            j = rank ^ r
            place = (j % 2) * 2 + j // 2
            part_all[place, :cols, span] = d_part[r * cols : (r + 1) * cols, :]
            part_all[place, cols:, span] = tail
    keep_out[...] = part_all[0:2]
    send_out[...] = part_all[2:4]


def expert_out_kernel(meta, w_out, *refs, groups):
    acts, (keep_out, send_out, part_all) = refs[:groups], refs[-3:]
    rank = meta[0]
    ranks = 4
    cols = part_all.shape[1]
    at = 0
    for act in acts:
        for i in range(0, act.shape[0], 256):
            part = dot_nn(act[i : i + 256, :], w_out[...]).T.astype(BF16)
            for r in range(ranks):
                j = rank ^ r
                part_all[(j % 2) * 2 + j // 2, :, at : at + 256] = part[r * cols : (r + 1) * cols]
            at += 256
    keep_out[...] = part_all[0:2]
    send_out[...] = part_all[2:4]


def slot_marks(meta, route, slot, cap, count):
    code = slot_codes(meta, route, slot, cap)
    ids = lax.broadcasted_iota(jnp.int32, (code.shape[1], count), 1)
    return jnp.where(ids == as_column(code), 1.0, 0.0).astype(BF16)


def fence_kernel(*refs):
    del refs


def side_by_side(blocks, came):
    size = blocks[0].shape[1]
    for k, block in enumerate(blocks):
        came[:, k * size : (k + 1) * size] = block[...]
    return came[...]


def combine_kernel(meta, route, slot, *rest, cap):
    *blocks, _, out, came = rest
    marks = slot_marks(meta, route, slot, cap, came.shape[1])
    out[...] = dot_nt(side_by_side(blocks, came), marks).astype(BF16)


def block_out_kernel(meta, route, slot, residual, gate, *rest, cap):
    *blocks, block_out, came, place = rest
    rank = meta[0]
    cols = block_out.shape[1]
    marks = slot_marks(meta, route, slot, cap, came.shape[1])
    returned = dot_nt(marks, side_by_side(blocks, came))
    for r in range(4):
        place[r] = residual[:, r * cols : (r + 1) * cols]
    block_out[...] = (place[rank] + gate[...] * returned).astype(BF16)


def put_chunks(grads, keep, send, place, expert, order):
    count = len(order)
    size = grads.shape[0] // count
    for c in range(count):
        place[c ^ expert] = grads[c * size : (c + 1) * size, :]
    for i, k in enumerate(order):
        out = keep if i < count // 2 else send
        at = (i % (count // 2)) * size
        out[at : at + size, :] = place[k]


def residual_back_kernel(
    meta, r0, r1, r2, r3, residual, gate, probs, route, params, cotangent, mixed, w_attn_out,
    attn_probs, normed_one, _, d_attn_cols_out, d_mixed_out, d_value_out, router_grad_out,
    gain_grad_out, first_out, second_out, place, place_f32, chunk_place, *, chunked,
):
    rank, expert = meta[0], meta[1]
    experts = probs.shape[1]
    feats = residual.shape[1]
    cols = feats // 4
    length = residual.shape[0]
    router = params[:experts, :]
    gain = params[experts : experts + 1, :]
    for j, r in enumerate((r0, r1, r2, r3)):
        place[rank ^ j] = r[:cols, :]
    d_gate = as_column(r0[cols : cols + 1, :].astype(F32))
    d_routed = jnp.concatenate([place[r] for r in range(4)], axis=0).astype(F32).T
    res = residual[...]
    scale = row_scale(res)
    lanes = lax.broadcasted_iota(jnp.int32, probs.shape, 1)
    onehot = jnp.where(lanes == as_column(route[...].reshape(1, length)), 1.0, 0.0)
    d_logits = d_gate * probs[...] * (onehot - gate[...])
    d_normed = d_routed + dot_nn(d_logits, router, PRECISE)
    normed = res * scale * gain
    router_grad = dot_tn(d_logits, normed, PRECISE)
    gain_grad = jnp.sum(d_normed * res * scale, axis=0, keepdims=True)
    cross = jnp.sum(gain * res * d_normed, axis=1, keepdims=True)
    d_residual = (
        cotangent[...].astype(F32).T
        + scale * gain * d_normed
        - res * (scale * scale * scale * cross * (1.0 / feats))
    )
    for r in range(4):
        own = slice(r * cols, (r + 1) * cols)
        place_f32[r] = d_residual[:, own]

        @pl.when(rank == r)
        def _():
            router_grad_out[...] = router_grad[:, own]
            gain_grad_out[...] = gain_grad[:, own]

    d_attn_cols_out[...] = place_f32[rank]
    d_attn = d_residual.astype(BF16)
    attn_grad = dot_nn(mixed[...], d_attn).astype(BF16)
    d_mixed = dot_nt(d_attn, w_attn_out[...]).astype(BF16)
    d_mixed_out[...] = d_mixed
    for h in range(cols // HDIM):
        own = slice(h * HDIM, (h + 1) * HDIM)
        total = jnp.zeros((length, HDIM), F32)
        for c in range(0, length, CHUNK):
            span = slice(c, c + CHUNK)
            total = total + dot_tn(attn_probs[h, span, :], d_mixed[span, own])
        d_value_out[:, own] = total.astype(BF16)
    value_grad = dot_tn(d_value_out[...], normed_one[...]).astype(BF16)
    if chunked:
        both = jnp.concatenate([attn_grad, value_grad], axis=0)
        put_chunks(both, first_out, second_out, chunk_place, expert, chunked)
    else:
        first_out[...] = attn_grad
        second_out[...] = value_grad


def attend_back_kernel(
    query, key, value, probs, d_mixed, bucket, d_query, d_key, table_out, *, buckets
):
    length = query.shape[0]
    width = 2 * length
    heads = query.shape[1] // HDIM
    marks = bucket_marks(bucket, buckets)
    zeros = jnp.zeros((8, width - length), F32)
    table_out[...] = jnp.zeros(table_out.shape, F32)
    for h in range(heads):
        own = slice(h * HDIM, (h + 1) * HDIM)
        dk = jnp.zeros((length, HDIM), F32)
        diagonals = jnp.zeros((8, width), F32)
        for c in range(0, length, CHUNK):
            span = slice(c, c + CHUNK)
            weights = probs[h, span, :].astype(F32)
            d_probs = dot_nt(d_mixed[span, own], value[:, own])
            inner = jnp.sum(d_probs * weights, axis=1, keepdims=True)
            d_scores = weights * (d_probs - inner)
            for b in range(CHUNK // 8):
                piece = jnp.concatenate([d_scores[8 * b : 8 * b + 8, :], zeros], axis=1)
                diagonals = diagonals + pltpu.roll(piece, (length - 1 - c - 8 * b) % width, 1)
            low = d_scores.astype(BF16)
            d_query[span, own] = (dot_nn(low, key[:, own]) * SCORE_SCALE).astype(BF16)
            dk = dk + dot_tn(low, query[span, own])
        d_key[:, own] = (dk * SCORE_SCALE).astype(BF16)
        line = diagonals[0:1]
        for r in range(1, 8):
            line = line + pltpu.roll(diagonals[r : r + 1], width - r, 1)
        table_col = jnp.sum(jnp.where(marks, line, 0.0), axis=1, keepdims=True)
        table_out[h : h + 1, :buckets] = jnp.broadcast_to(table_col, (buckets, 128)).T[0:1, :]


def put_split(out, at, row, value):
    high = value.astype(BF16).astype(F32)
    out[row : row + 1, at : at + value.shape[1]] = high
    out[row + 8 : row + 9, at : at + value.shape[1]] = value - high


def query_back_kernel(
    meta, tokens, gain, normed, d_query, d_key, d_value, w_query, w_key, w_value, gain2_grad,
    table_grad, router_grad, _, _got, *rest, chunked, heads, buckets,
):
    keep_in, send_in, gain1_out, first_out, second_out, place, chunk_place, pack = rest
    rank, expert = meta[0], meta[1]
    length, feats = tokens.shape
    cols = feats // 4
    normed_rows = normed[...]
    query_grad = dot_tn(d_query[...], normed_rows).astype(BF16)
    key_grad = dot_tn(d_key[...], normed_rows).astype(BF16)
    d_normed = (
        dot_nn(d_query[...], w_query[...])
        + dot_nn(d_key[...], w_key[...])
        + dot_nn(d_value[...], w_value[...])
    )
    rows = tokens[...].astype(F32)
    product = d_normed * rows
    gain1_grad = jnp.sum(product * row_scale(rows), axis=0, keepdims=True)
    gain1_out[...] = jnp.broadcast_to(gain1_grad, gain1_out.shape)
    if chunked:
        pack[...] = jnp.zeros(pack.shape, F32)
        put_split(pack, 0, 0, gain1_grad)
        put_split(pack, 0, 1, gain2_grad[...])
        for h in range(heads):
            put_split(pack, 256 * h, 2, table_grad[h : h + 1, :])
        for e in range(router_grad.shape[0]):
            put_split(pack, 256 * (e % 3), 3 + e // 3, router_grad[e : e + 1, :])
        small = pack[...].astype(BF16)
        both = jnp.concatenate([query_grad, key_grad], axis=0)
        put_chunks(both, first_out, second_out, chunk_place, expert, chunked)
        for out in (first_out, second_out):
            out[out.shape[0] - 16 :, :] = small
    else:
        first_out[...] = query_grad
        second_out[...] = key_grad
    cross = jnp.sum(product * gain[...].reshape(1, feats), axis=1, keepdims=True)
    high = cross.astype(BF16).astype(F32)
    low = cross - high
    lanes = lax.broadcasted_iota(jnp.int32, (length, place.shape[2] - cols), 1)
    extra = jnp.where(lanes == 0, high, jnp.where(lanes == 1, low, 0.0)).astype(BF16)
    for r in range(4):
        j = rank ^ r
        own = d_normed[:, r * cols : (r + 1) * cols].astype(BF16)
        place[(j % 2) * 2 + j // 2] = jnp.concatenate([own, extra], axis=1)
    keep_in[...] = place[0:2]
    send_in[...] = place[2:4]


def input_kernel(
    meta, tokens, gain, d_attn_cols, first, second, *rest
):
    *_, out, place, gain_place = rest
    rank = meta[0]
    feats = tokens.shape[1]
    cols = feats // 4
    rows = tokens[...].astype(F32)
    scale = row_scale(rows)
    both = first[...].astype(F32) + second[...].astype(F32)
    cross = both[:, cols : cols + 1] + both[:, cols + 1 : cols + 2]
    gain_row = gain[...].reshape(1, feats)
    for r in range(4):
        place[r] = rows[:, r * cols : (r + 1) * cols]
        gain_place[r] = gain_row[:, r * cols : (r + 1) * cols]
    own = both[:, :cols]
    own_rows = place[rank]
    out[...] = (
        d_attn_cols[...]
        + scale * gain_place[rank] * own
        - own_rows * (scale * scale * scale * cross * (1.0 / feats))
    )


def add_small(a, b):
    at = a.shape[0] - 16
    total = (
        a[at : at + 8, :].astype(F32)
        + b[at : at + 8, :].astype(F32)
        + a[at + 8 :, :].astype(F32)
        + b[at + 8 :, :].astype(F32)
    )
    high = total.astype(BF16).astype(F32)
    return total, jnp.concatenate([high, total - high], axis=0).astype(BF16)


def sum_kernel(keep, got, keep_out, send_out, token_out):
    token_out[...] = jnp.zeros(token_out.shape, F32)
    half = (keep.shape[0] - 16) // 2
    total = (keep[: 2 * half, :].astype(F32) + got[: 2 * half, :].astype(F32)).astype(BF16)
    _, small = add_small(keep, got)
    keep_out[:half, :] = total[:half]
    send_out[:half, :] = total[half:]
    keep_out[half:, :] = small
    send_out[half:, :] = small


def last_sum_kernel(keep, got, mine_out, small_out, gain1_out):
    size = mine_out.shape[0]
    mine_out[...] = (keep[:size, :].astype(F32) + got[:size, :].astype(F32)).astype(BF16)
    total, _ = add_small(keep, got)
    small_out[...] = total
    gain1_out[...] = jnp.broadcast_to(total[0:1], gain1_out.shape)


def spread_kernel(
    meta, mine, second, third, fourth, first_out, second_out, token_out, place, *, order
):
    expert = meta[1]
    count = len(order)
    size = mine.shape[0] // 2
    quarter = count // 4
    token_out[...] = jnp.zeros(token_out.shape, F32)
    for i in range(count):
        block = (mine, second, third, fourth)[i // quarter]
        at = i % quarter
        place[order[i]] = block[at * size : (at + 1) * size, :]
    rows = first_out.shape[0]
    for c in range(count):
        chunk = place[c ^ expert].astype(F32)
        start = c * size
        if start < rows:
            first_out[start : start + size, :] = chunk
        else:
            second_out[start - rows : start - rows + size, :] = chunk


def finish_kernel(
    meta, mine, second, third, fourth, small, *rest, order, heads
):
    first_out, second_out, token_out, gain2_out, table_out, router_out, place = rest[-7:]
    blocks = (mine, second, third, fourth)
    spread_kernel(meta, *blocks, first_out, second_out, token_out, place, order=order)
    cols = gain2_out.shape[1]
    gain2_out[...] = small[1:2, :cols]
    for h in range(heads):
        table_out[h : h + 1, :] = small[2:3, 256 * h : 256 * h + table_out.shape[1]]
    for e in range(router_out.shape[0]):
        at = 256 * (e % 3)
        router_out[e : e + 1, :] = small[3 + e // 3 : 4 + e // 3, at : at + cols]


def moving(kernel, smem, fetch, total, far):
    def run(*refs):
        rest = list(refs[: len(refs) - 1])
        sems = refs[-1]
        near_out = rest[len(rest) - len(far) :] if far else []
        rest = rest[: len(rest) - len(far)]
        near_in = rest[len(rest) - fetch :] if fetch else []
        rest = rest[: len(rest) - fetch]
        copies = [
            pltpu.make_async_copy(rest[smem + i], b, sems.at[i]) for i, b in enumerate(near_in)
        ]
        for copy in copies:
            copy.start()
        for copy in copies:
            copy.wait()
        inner = list(rest)
        for i, b in enumerate(near_in):
            inner[smem + i] = b
        for b, at in zip(near_out, far):
            inner[total + at] = b
        kernel(*inner)
        copies = [
            pltpu.make_async_copy(b, rest[total + at], sems.at[fetch + i])
            for i, (b, at) in enumerate(zip(near_out, far))
        ]
        for copy in copies:
            copy.start()
        for copy in copies:
            copy.wait()

    return run


def call(kernel, outs, scratch, *operands, weight=1.0, smem=1, fetch=0, far=(), after=()):
    specs, given = [], []
    for i, operand in enumerate(operands):
        if i < smem:
            specs.append(pl.BlockSpec(memory_space=pltpu.SMEM))
        elif i < smem + fetch:
            specs.append(pl.BlockSpec(memory_space=pltpu.HBM))
            operand = pltpu.with_memory_space_constraint(operand, pltpu.HBM)
        else:
            specs.append(pl.BlockSpec(memory_space=pltpu.VMEM))
        given.append(operand)
    specs += [pl.BlockSpec(memory_space=pl.ANY)] * len(after)
    scratch_shapes = [pltpu.VMEM(shape, kind) for shape, kind in scratch]
    shapes, out_specs = [], []
    for i, (shape, kind) in enumerate(outs):
        shapes.append(pltpu.HBM(shape, kind) if i in far else jax.ShapeDtypeStruct(shape, kind))
        out_specs.append(pl.BlockSpec(memory_space=pltpu.HBM if i in far else pltpu.VMEM))
    if fetch or far:
        kernel = moving(kernel, smem, fetch, len(operands) + len(after), far)
        scratch_shapes += [pltpu.VMEM(a.shape, a.dtype) for a in operands[smem : smem + fetch]]
        scratch_shapes += [pltpu.VMEM(*outs[i]) for i in far]
        scratch_shapes.append(pltpu.SemaphoreType.DMA((fetch + len(far),)))
    return pl.pallas_call(
        kernel,
        out_shape=shapes,
        in_specs=specs,
        out_specs=out_specs,
        scratch_shapes=scratch_shapes,
        compiler_params=pltpu.CompilerParams(vmem_limit_bytes=32 * 1024 * 1024),
        cost_estimate=pl.CostEstimate(
            flops=int(weight * 1.1e9), bytes_accessed=1 << 16, transcendentals=0
        ),
    )(*given, *after)


def swap(array, axis, bit):
    size = lax.axis_size(axis)
    return lax.ppermute(array, axis, [(i, i ^ bit) for i in range(size)])


def add_low(a, b):
    return (a.astype(F32) + b.astype(F32)).astype(BF16)


def gather_four(array):
    across = swap(array, "tensor", 2)
    beside = swap(array, "tensor", 1)
    return [array, beside, across, swap(across, "tensor", 1)]


def reduce_four(keep, send):
    got = swap(send, "tensor", 1)
    far = add_low(keep[1], got[1])
    return add_low(keep[0], got[0]), swap(far, "tensor", 2), far


def exchange(blocks):
    if len(blocks) > 8:
        return hyper_exchange(blocks)[0]
    return [blocks[0]] + [swap(b, "expert", k) for k, b in enumerate(blocks) if k]


def hyper_exchange(blocks, gates=None):
    count = len(blocks)
    held = {k: [b] for k, b in enumerate(blocks)}
    steps = []
    bit = 1
    while bit < count:
        away = [k for k in sorted(held) if k & bit]
        sent = jnp.concatenate([b for k in away for b in held[k]], axis=0)
        if gates and bit in gates:
            (sent,) = fence([sent], gates[bit])
        got = swap(sent, "expert", bit)
        if gates and -bit in gates:
            (got,) = fence([got], gates[-bit])
        steps.append(got)
        size = blocks[0].shape[0]
        at = 0
        fresh = {}
        for k in away:
            pieces = [got[at + i * size : at + (i + 1) * size] for i in range(len(held[k]))]
            at += len(held[k]) * size
            fresh[k ^ bit] = held[k ^ bit] + pieces
        held = fresh
        bit *= 2
    return held[0], steps


ORDER = (0, 4, 2, 6, 1, 5, 3, 7)


def gather_chunks(mine, gates=None):
    held = swap(mine, "expert", 4)
    if gates:
        (held,) = fence([held], (gates[0],))
    held = jnp.concatenate([mine, held], axis=0)
    beside = swap(held, "expert", 2)
    if gates:
        (beside,) = fence([beside], (gates[1],))
    return held, beside, swap(held, "expert", 1), swap(beside, "expert", 1)


def halve_plain(keep, got, gates):
    for bit, gate in zip((2, 4), gates):
        half = keep.shape[0] // 2
        sent = add_low(keep[half:], got[half:])
        keep = add_low(keep[:half], got[:half])
        (got,) = fence([swap(sent, "expert", bit)], (gate,))
    return add_low(keep, got)


def halve(keep, send):
    feats = keep.shape[1]
    steps = []
    for bit in (1, 2):
        rows = (keep.shape[0] - 16) // 2 + 16
        keep, send, token = call(
            sum_kernel, [((rows, feats), BF16)] * 2 + [((8, 128), F32)], [], keep, swap(send, "expert", bit), smem=0
        )
        steps.append(token)
    last = call(
        last_sum_kernel,
        [((keep.shape[0] - 16, feats), BF16), ((8, feats), F32), ((8, feats), F32)],
        [],
        keep, swap(send, "expert", 4), smem=0,
    )
    return last, steps


def fence(arrays, after):
    count = len(arrays)
    return pl.pallas_call(
        fence_kernel,
        out_shape=[jax.ShapeDtypeStruct(a.shape, a.dtype) for a in arrays],
        in_specs=[pl.BlockSpec(memory_space=pl.ANY)] * (count + len(after)),
        out_specs=[pl.BlockSpec(memory_space=pl.ANY)] * count,
        input_output_aliases={i: i for i in range(count)},
    )(*arrays, *after)


def on_device(
    tokens, cotangent, norm1_gain, w_query, w_key, w_value, w_attn_out, bias_table, norm2_gain,
    w_router, expert_in, expert_out, route, slot, segment, rel_bucket,
):
    length, feats = tokens.shape
    cols = cotangent.shape[1]
    heads = cols // HDIM
    experts = lax.axis_size("expert")
    cap = 2 * length // experts
    share = cap // 4
    rank = lax.axis_index("tensor").astype(jnp.int32)
    expert = lax.axis_index("expert").astype(jnp.int32)
    meta = jnp.stack([rank, expert])
    total = experts * cap
    direct = share % 16 == 0
    buckets = bias_table.shape[0]
    chunked = ORDER if experts == len(ORDER) else None

    w_query_t, w_key_t, w_value_t = w_query.T, w_key.T, w_value.T
    packed_rows = cols + -(-(experts + 3) // 16) * 16
    packed, cot_own, *cot_blocks = call(
        first_kernel,
        [((packed_rows, feats), BF16), ((length // cap * cols, cap), BF16)] + [((cols, cap), BF16)] * experts,
        [],
        meta, route, slot, cotangent.T, w_attn_out, w_router.T, norm2_gain,
        weight=2.0, fetch=6,
    )
    packed_parts = gather_four(packed)
    bucket = jnp.concatenate([rel_bucket, jnp.full((1,), -1, jnp.int32)])
    normed, query, key, value, probs, mixed, mixed_token = call(
        attend_kernel,
        [((length, feats), BF16)]
        + [((length, cols), BF16)] * 3
        + [((heads, length, length), BF16), ((cols, length), BF16), ((8, 128), F32)],
        [((length, length), F32)],
        tokens, w_query.T, w_key.T, w_value.T, norm1_gain, segment, bucket, bias_table.T,
        weight=7.0, smem=0, fetch=8, far=(0, 1, 2, 3, 4),
    )

    mixed_parts = gather_four(mixed)
    residual, gate, router_probs, params, *row_blocks = call(
        residual_kernel,
        [
            ((length, feats), F32),
            ((length, 1), F32),
            ((length, experts), F32),
            ((experts + 8, feats), F32),
        ]
        + [((share, feats), BF16)] * experts,
        [((4, packed_rows - cols, cols), F32)],
        meta, route, slot, tokens, *mixed_parts, *packed_parts,
        weight=5.8, fetch=3, far=(0, 1, 2),
    )
    cot_arrived, _ = hyper_exchange(
        cot_blocks, {2: (mixed_token,), -4: (residual,)}
    )
    if direct:
        cot_arrived = cot_arrived + [cot_own]
    else:
        cot_turned = lax.all_gather(cotangent.T, "tensor", axis=0, tiled=True)
    cot_rows = gather_four(jnp.concatenate(cot_arrived, axis=0))
    arrived = exchange(row_blocks)
    groups = GROUPS if direct else 1
    group_size = experts // groups
    row_groups = []
    for g in range(groups):
        blocks = arrived[g * group_size : (g + 1) * group_size]
        if direct:
            (packed,) = call(
                functools.partial(assemble_kernel, count=group_size),
                [((group_size * share, feats), BF16)],
                [],
                *blocks,
                weight=1.0, smem=0, after=(cot_rows[2],),
            )
        else:
            packed = jnp.concatenate(blocks, axis=0)
        row_groups.append(gather_four(packed))

    if not direct:
        def assemble(parts, shape, turn):
            stacked = jnp.stack(parts).reshape(4, experts, *shape)
            stacked = stacked[rank ^ jnp.arange(4, dtype=jnp.int32)]
            return [jnp.transpose(stacked, turn).reshape(total, feats)]

        one = jnp.zeros((16, 128), BF16)
        row_groups = [assemble(row_groups[0], (share, feats), (1, 0, 2, 3)) + [one] * 3]
        cot_rows = assemble(cot_rows, (cols, cap), (1, 3, 0, 2)) + [one] * 3
    w_in, w_out = expert_in[0], expert_out[0]
    hidden_count = w_in.shape[1]
    part_rows = cols + 16
    count = total // groups
    x_shape = (group_size, 4, share, feats) if direct else (1, 1, 16, 128)
    c_shape = (4, cols, count) if direct else (1, 16, 128)
    acts, returning, kept = [], [], []
    for g in range(groups):
        rows_all, act, cots, d_hidden, keep, send, turned = call(
            functools.partial(expert_kernel, first=g * group_size, direct=direct),
            [((count, feats), BF16), ((count, hidden_count), BF16), ((count, feats), BF16),
             ((count, hidden_count), BF16), ((2, part_rows, count), BF16),
             ((2, part_rows, count), BF16), ((4, cols, length) if direct else (1, 16, 128), BF16)],
            [(x_shape, BF16), (c_shape, BF16), ((4, part_rows, count), BF16)],
            meta, *row_groups[g], *cot_rows, w_in, w_out, params[:experts],
            weight=10.0, far=(0, 1, 2, 3, 6) if direct else (),
        )
        if direct:
            cot_turned = turned.reshape(feats, length)
        near, far, met = reduce_four(keep, send)
        whole = add_low(near, far)
        returning += [whole[:, k * cap : (k + 1) * cap] for k in range(group_size)]
        acts.append(act)
        kept += [act, cots, rows_all, d_hidden]

    kept = fence(kept, (met,))
    expert_out_grad = sum(dot_tn(kept[4 * g], kept[4 * g + 1]) for g in range(groups))
    expert_in_grad = sum(dot_tn(kept[4 * g + 2], kept[4 * g + 3]) for g in range(groups))

    def unite(blocks):
        return blocks if cap % 128 == 0 else [jnp.concatenate(blocks, axis=1)]

    keep_fwd, send_fwd = call(
        functools.partial(expert_out_kernel, groups=groups),
        [((2, cols, total), BF16)] * 2,
        [((4, cols, total), BF16)],
        meta, w_out, *[kept[4 * g] for g in range(groups)],
        weight=2.9, after=(whole, expert_out_grad, expert_in_grad),
    )
    (d_routed,) = call(
        functools.partial(combine_kernel, cap=cap),
        [((part_rows, length), BF16)],
        [((part_rows, total), BF16)],
        meta, route, slot, *unite(exchange(returning)), after=(keep_fwd,),
        weight=1.0,
    )
    routed_parts = gather_four(d_routed)

    near_fwd, far_fwd, met_fwd = reduce_four(keep_fwd, send_fwd)
    whole_fwd = add_low(near_fwd, far_fwd)
    fwd_arrived, fwd_steps = hyper_exchange(
        [whole_fwd[:, k * cap : (k + 1) * cap] for k in range(experts)]
    )
    came_fwd = unite(fwd_arrived)
    (block_out,) = call(
        functools.partial(block_out_kernel, cap=cap),
        [((length, cols), BF16)],
        [((cols, total), BF16), ((4, length, cols), F32)],
        meta, route, slot, residual, gate, *came_fwd,
        weight=1.2,
    )

    if chunked:
        size = 2 * cols // experts
        grad_outs = [((experts // 2 * size + 16, feats), BF16)] * 2
        chunk_scratch = ((experts, size, feats), BF16)
    else:
        grad_outs = [((cols, feats), BF16)] * 2
        chunk_scratch = ((16, 128), BF16)
    d_attn_cols, d_mixed, d_value, router_grad, gain2_grad, *first_grads = call(
        functools.partial(residual_back_kernel, chunked=chunked),
        [((length, cols), F32), ((length, cols), BF16), ((length, cols), BF16),
         ((experts, cols), F32), ((1, cols), F32)]
        + [((cols, feats), BF16)] * 2,
        [((4, cols, length), BF16), ((4, length, cols), F32), chunk_scratch],
        meta, *routed_parts, residual, gate, router_probs, route, params, cot_turned, mixed,
        w_attn_out, probs, normed, after=(met_fwd,),
        weight=8.0, far=(0,),
    )
    d_query, d_key, table_grad = call(
        functools.partial(attend_back_kernel, buckets=buckets),
        [((length, cols), BF16)] * 2 + [((8, 128), F32)],
        [],
        query, key, value, probs, d_mixed, bucket, smem=0,
        weight=7.0,
    )
    wide = -(-(cols + 2) // 128) * 128
    first_got = swap(first_grads[1], "expert", 1) if chunked else d_query
    keep_in, send_in, gain1_grad, *second_grads = call(
        functools.partial(query_back_kernel, chunked=chunked, heads=heads, buckets=buckets),
        [((2, length, wide), BF16)] * 2 + [((8, feats), F32)] + grad_outs,
        [((4, length, wide), BF16), chunk_scratch, ((16, feats), F32)],
        meta, tokens, norm1_gain, normed, d_query, d_key, d_value, w_query_t, w_key_t,
        w_value_t, gain2_grad, table_grad, router_grad, after=(whole_fwd, first_got),
        weight=4.0,
    )
    near_in, far_in, _ = reduce_four(keep_in, send_in)
    (input_grad,) = call(
        input_kernel,
        [((length, cols), F32)],
        [((4, length, cols), F32), ((4, 1, cols), F32)],
        meta, tokens, norm1_gain, d_attn_cols, near_in, far_in,
        weight=1.0,
    )

    if chunked:
        (mine, small, gain1_grad), steps = halve(*second_grads)
        second_chunks = gather_chunks(mine)
        attn_grad, value_grad, spread_token = call(
            functools.partial(spread_kernel, order=ORDER),
            [((cols, feats), F32)] * 2 + [((8, 128), F32)],
            [chunk_scratch],
            meta,
            *gather_chunks(
                halve_plain(first_grads[0], *fence([first_got], steps[:1]), (steps[1], small)),
                (second_chunks[0][:16, :128], second_chunks[1][:16, :128]),
            ),
            weight=1.6,
        )
        for bit in (1, 2):
            gain1_grad = gain1_grad + swap(gain1_grad, "tensor", bit)
        query_grad, key_grad, _, gain2_grad, table_grad, router_grad = call(
            functools.partial(finish_kernel, order=ORDER, heads=heads),
            [((cols, feats), F32)] * 2
            + [((8, 128), F32), ((1, cols), F32), ((heads, buckets), F32), ((experts, cols), F32)],
            [chunk_scratch],
            meta, *second_chunks, small,
            weight=1.6, after=(input_grad, block_out, gain1_grad, spread_token),
        )
    else:
        query_grad, key_grad, gain2_grad, table_grad, router_grad = lax.psum(
            (*second_grads, gain2_grad, table_grad[:heads, :buckets], router_grad), "expert"
        )
        gain1_grad = lax.psum(gain1_grad, ("expert", "tensor"))
        attn_grad, value_grad = lax.psum(tuple(first_grads), "expert")
    return (
        block_out,
        input_grad,
        gain1_grad[0],
        query_grad.astype(F32).T,
        key_grad.astype(F32).T,
        value_grad.astype(F32).T,
        attn_grad.astype(F32),
        table_grad.T,
        gain2_grad[0],
        router_grad.T,
        expert_in_grad[None],
        expert_out_grad[None],
    )


def solution(mesh):
    return jax.shard_map(
        on_device,
        mesh=mesh,
        in_specs=(
            P("expert", None),
            P("expert", "tensor"),
            P(),
            P(None, "tensor"),
            P(None, "tensor"),
            P(None, "tensor"),
            P("tensor", None),
            P(None, "tensor"),
            P("tensor"),
            P("tensor", None),
            P("expert", None, "tensor"),
            P("expert", "tensor", None),
            P("expert"),
            P("expert"),
            P("expert"),
            P(),
        ),
        out_specs=(
            P("expert", "tensor"),
            P("expert", "tensor"),
            P(),
            P(None, "tensor"),
            P(None, "tensor"),
            P(None, "tensor"),
            P("tensor", None),
            P(None, "tensor"),
            P("tensor"),
            P("tensor", None),
            P("expert", None, "tensor"),
            P("expert", "tensor", None),
        ),
        check_vma=False,
    )
```

```python
import functools

import jax
import jax.numpy as jnp
from jax import lax
from jax.experimental import pallas as pl
from jax.experimental.pallas import tpu as pltpu
from jax.sharding import PartitionSpec as P

HDIM = 64
EPSILON = 1e-06
MASKED_SCORE = -1e30
SCORE_SCALE = 0.125
PRECISE = lax.Precision.HIGHEST
F32 = jnp.float32
BF16 = jnp.bfloat16
GELU_C = 0.7978845608028654
GELU_A = 0.044715
CHUNK = 128
GROUPS = 1


def dot_nn(a, b, precision=None):
    return lax.dot_general(
        a, b, (((1,), (0,)), ((), ())), precision=precision, preferred_element_type=F32
    )


def dot_nt(a, b, precision=None):
    return lax.dot_general(
        a, b, (((1,), (1,)), ((), ())), precision=precision, preferred_element_type=F32
    )


def dot_tn(a, b, precision=None):
    return lax.dot_general(
        a, b, (((0,), (0,)), ((), ())), precision=precision, preferred_element_type=F32
    )


def row_scale(rows):
    return lax.rsqrt(jnp.mean(rows * rows, axis=1, keepdims=True) + EPSILON)


def bucket_marks(bucket, count):
    width = bucket.shape[0]
    return lax.broadcasted_iota(jnp.int32, (count, width), 0) == bucket[...].reshape(1, width)


def in_order(blocks, rank, place, axis):
    for j, block in enumerate(blocks):
        place[rank ^ j] = block[...]
    return jnp.concatenate([place[r] for r in range(len(blocks))], axis=axis)


def as_column(row):
    return jnp.broadcast_to(row, (128, row.shape[1])).T[:, 0:1]


def softmax_rows(logits):
    shifted = jnp.exp(logits - jnp.max(logits, axis=1, keepdims=True))
    return shifted / jnp.sum(shifted, axis=1, keepdims=True)


def attend_kernel(
    tokens, w_query, w_key, w_value, gain, segment, bucket, table,
    normed_out, query_out, key_out, value_out, probs_out, mixed_out, token_out,
    band,
):
    length = tokens.shape[0]
    width = 2 * length
    heads = query_out.shape[1] // HDIM
    marks = bucket_marks(bucket, table.shape[1])
    table_rows = jnp.broadcast_to(table[...][:, None, :], (heads, 128, table.shape[1]))
    bases = []
    for h in range(heads):
        offsets = jnp.sum(
            jnp.where(marks, table_rows[h].T[:, 0:1], 0.0), axis=0, keepdims=True
        )
        bases.append(
            jnp.concatenate(
                [offsets] + [pltpu.roll(offsets, r, 1) for r in range(1, 8)], axis=0
            )
        )
    token_out[...] = jnp.zeros(token_out.shape, F32)
    seg_row = segment[...].reshape(1, length)
    seg_col = as_column(seg_row)
    rows = tokens[...].astype(F32)
    normed = (rows * row_scale(rows) * gain[...].reshape(1, rows.shape[1])).astype(BF16)
    normed_out[...] = normed
    query = dot_nt(normed, w_query[...]).astype(BF16)
    key = dot_nt(normed, w_key[...]).astype(BF16)
    query_out[...] = query
    key_out[...] = key
    value_out[...] = dot_nt(normed, w_value[...]).astype(BF16)
    value_turned = dot_nt(w_value[...], normed).astype(BF16)
    for h in range(heads):
        cols = slice(h * HDIM, (h + 1) * HDIM)
        for b in range(length // 8):
            turned = pltpu.roll(bases[h], (length + 1 + 8 * b) % width, 1)
            band[8 * b : 8 * b + 8, :] = turned[:, :length]
        for c in range(0, length, CHUNK):
            span = slice(c, c + CHUNK)
            scores = dot_nt(query[span, cols], key[:, cols]) * SCORE_SCALE + band[span, :]
            scores = jnp.where(seg_col[span, :] == seg_row, scores, MASKED_SCORE)
            probs = softmax_rows(scores)
            probs = probs.astype(BF16)
            probs_out[h, span, :] = probs
            mixed_out[cols, span] = dot_nt(value_turned[cols, :], probs).astype(BF16)


def dispatch(code, rows, outs, transposed=False):
    share = outs[0].shape[0]
    for k, out in enumerate(outs):
        ids = lax.broadcasted_iota(jnp.int32, (share, code.shape[1]), 0) + k * share
        marks = jnp.where(ids == code[...], 1.0, 0.0).astype(BF16)
        product = dot_nt if transposed else dot_nn
        out[...] = product(marks, rows).astype(BF16)


def slot_codes(meta, route, slot, size):
    count = route.shape[0]
    return ((route[...] ^ meta[1]) * size + slot[...]).reshape(1, count)


def first_kernel(
    meta, route, slot, cotangent, w_attn_out, w_router, gain, packed_out, own_out, *outs
):
    cap = outs[0].shape[1]
    count = len(outs) * cap
    code = slot_codes(meta, route, slot, cap)
    ids = lax.broadcasted_iota(jnp.int32, (count, code.shape[1]), 0)
    marks = jnp.where(ids == code, 1.0, 0.0).astype(BF16)
    placed = dot_nt(cotangent[...], marks).astype(BF16)
    for k, out in enumerate(outs):
        out[...] = placed[:, k * cap : (k + 1) * cap]
    rows, feats = w_attn_out.shape
    for i in range(0, cotangent.shape[1], cap):
        at = i // cap * rows
        own_out[at : at + rows, :] = cotangent[:, i : i + cap]
    experts = w_router.shape[0]
    packed_out[:rows, :] = w_attn_out[...]
    top = packed_out.shape[0]
    line = gain[...].reshape(1, rows)
    high = line.astype(BF16)
    rest = line - high.astype(F32)
    mid = rest.astype(BF16)
    low = (rest - mid.astype(F32)).astype(BF16)
    pad = top - rows - experts - 3
    extra = [w_router[...].astype(F32)] + [p.astype(F32) for p in (high, mid, low)]
    extra = jnp.concatenate(extra + [jnp.zeros((pad, rows), F32)], axis=0)
    wide = jnp.concatenate([extra, jnp.zeros((extra.shape[0], feats - rows), F32)], axis=1)
    packed_out[rows:top, :] = wide.astype(BF16)


def dispatch(code, rows, outs):
    share = outs[0].shape[0]
    for k, out in enumerate(outs):
        ids = lax.broadcasted_iota(jnp.int32, (share, code.shape[1]), 0) + k * share
        marks = jnp.where(ids == code, 1.0, 0.0).astype(BF16)
        out[...] = dot_nn(marks, rows).astype(BF16)


def residual_kernel(
    meta, route, slot, tokens, m0, m1, m2, m3, w0, w1, w2, w3,
    residual_out, gate_out, probs_out, params_out, *rest,
):
    outs, place = rest[:-1], rest[-1]
    share = outs[0].shape[0]
    experts = probs_out.shape[1]
    cols = m0.shape[0]
    for j, w in enumerate((w0, w1, w2, w3)):
        place[meta[0] ^ j] = w[cols:, :cols].astype(F32)
    params = jnp.concatenate([place[r] for r in range(4)], axis=1)
    router = params[:experts]
    gain = params[experts : experts + 1]
    for i in (1, 2):
        gain = gain + params[experts + i : experts + i + 1]
    params_out[...] = jnp.concatenate([router, jnp.broadcast_to(gain, (8, gain.shape[1]))], axis=0)
    residual = tokens[...].astype(F32)
    for m, w in ((m0, w0), (m1, w1), (m2, w2), (m3, w3)):
        residual = residual + dot_tn(m[...], w[:cols, :])
    residual_out[...] = residual
    normed = residual * row_scale(residual) * gain
    part = slot[...] - meta[0] * share
    code = jnp.where(
        (part >= 0) & (part < share), (route[...] ^ meta[1]) * share + part, -1
    ).reshape(1, part.shape[0])
    dispatch(code, normed.astype(BF16), outs)
    probs = softmax_rows(dot_nt(normed, router, PRECISE))
    probs_out[...] = probs
    lanes = lax.broadcasted_iota(jnp.int32, probs.shape, 1)
    where = as_column(route[...].reshape(1, part.shape[0]))
    gate_out[...] = jnp.sum(jnp.where(lanes == where, probs, 0.0), axis=1, keepdims=True)


def assemble_kernel(*refs, count):
    out = refs[-1]
    size = refs[0].shape[0]
    for i, block in enumerate(refs[:count]):
        out[i * size : (i + 1) * size, :] = block[...]


def expert_kernel(
    meta, x0, x1, x2, x3, c0, c1, c2, c3, w_in, w_out, router,
    rows_out, act_out, cots_out, d_hidden_out, keep_out, send_out, turned_out,
    x_all, c_all, part_all, *, first, direct,
):
    rank, expert = meta[0], meta[1]
    ranks = 4
    total = rows_out.shape[0]
    feats = rows_out.shape[1]
    cols = feats // ranks
    if direct:
        sources, _, share, _ = x_all.shape
        cap = ranks * share
        for j, (x, c) in enumerate(((x0, c0), (x1, c1), (x2, c2), (x3, c3))):
            for s in range(sources):
                x_all[s, rank ^ j] = x[s * share : (s + 1) * share, :]
                at = (first + s) * cols
                c_all[rank ^ j, :, s * cap : (s + 1) * cap] = c[at : at + cols, :]
            at = c.shape[0] - turned_out.shape[2] // cap * cols
            for i in range(turned_out.shape[2] // cap):
                turned_out[rank ^ j, :, i * cap : (i + 1) * cap] = c[
                    at + i * cols : at + (i + 1) * cols, :
                ]
        step = 256 // cap
    for i in range(total // 256):
        span = slice(i * 256, (i + 1) * 256)
        if direct:
            rows = x_all[i * step : (i + 1) * step].reshape(256, feats)
            turned = jnp.concatenate([c_all[r, :, span] for r in range(ranks)], axis=0)
            cots = turned.astype(F32).T.astype(BF16)
        else:
            rows = x0[span, :]
            cots = c0[span, :]
        rows_out[span, :] = rows
        probs = softmax_rows(dot_nt(rows, router[...].astype(BF16)))
        lanes = lax.broadcasted_iota(jnp.int32, probs.shape, 1)
        gate = jnp.sum(jnp.where(lanes == expert, probs, 0.0), axis=1, keepdims=True)
        cots_out[span, :] = (gate * cots.astype(F32)).astype(BF16)
        hidden = dot_nn(rows, w_in[...])
        pull = dot_nt(cots, w_out[...])
        bent = jnp.tanh(GELU_C * (hidden + GELU_A * hidden * hidden * hidden))
        act = (0.5 * hidden * (1.0 + bent)).astype(BF16)
        act_out[span, :] = act
        slope = 0.5 * (1.0 + bent) + 0.5 * hidden * (1.0 - bent * bent) * (
            GELU_C * (1.0 + 3.0 * GELU_A * hidden * hidden)
        )
        d_hidden = (gate * pull * slope).astype(BF16)
        d_hidden_out[span, :] = d_hidden
        d_gate = jnp.sum(pull * act.astype(F32), axis=1, keepdims=True)
        d_part = dot_nt(w_in[...], d_hidden).astype(BF16)
        tail = jnp.broadcast_to(d_gate, (256, 128)).T[: part_all.shape[1] - cols].astype(BF16)
        for r in range(ranks):
            j = rank ^ r
            place = (j % 2) * 2 + j // 2
            part_all[place, :cols, span] = d_part[r * cols : (r + 1) * cols, :]
            part_all[place, cols:, span] = tail
    keep_out[...] = part_all[0:2]
    send_out[...] = part_all[2:4]


def expert_out_kernel(meta, w_out, *refs, groups):
    acts, (keep_out, send_out, part_all) = refs[:groups], refs[-3:]
    rank = meta[0]
    ranks = 4
    cols = part_all.shape[1]
    at = 0
    for act in acts:
        for i in range(0, act.shape[0], 256):
            part = dot_nn(act[i : i + 256, :], w_out[...]).T.astype(BF16)
            for r in range(ranks):
                j = rank ^ r
                part_all[(j % 2) * 2 + j // 2, :, at : at + 256] = part[r * cols : (r + 1) * cols]
            at += 256
    keep_out[...] = part_all[0:2]
    send_out[...] = part_all[2:4]


def slot_marks(meta, route, slot, cap, count):
    code = slot_codes(meta, route, slot, cap)
    ids = lax.broadcasted_iota(jnp.int32, (code.shape[1], count), 1)
    return jnp.where(ids == as_column(code), 1.0, 0.0).astype(BF16)


def fence_kernel(*refs):
    del refs


def side_by_side(blocks, came):
    size = blocks[0].shape[1]
    for k, block in enumerate(blocks):
        came[:, k * size : (k + 1) * size] = block[...]
    return came[...]


def combine_kernel(meta, route, slot, *rest, cap):
    *blocks, _, out, came = rest
    marks = slot_marks(meta, route, slot, cap, came.shape[1])
    out[...] = dot_nt(side_by_side(blocks, came), marks).astype(BF16)


def block_out_kernel(meta, route, slot, residual, gate, *rest, cap):
    *blocks, block_out, came, place = rest
    rank = meta[0]
    cols = block_out.shape[1]
    marks = slot_marks(meta, route, slot, cap, came.shape[1])
    returned = dot_nt(marks, side_by_side(blocks, came))
    for r in range(4):
        place[r] = residual[:, r * cols : (r + 1) * cols]
    block_out[...] = (place[rank] + gate[...] * returned).astype(BF16)


def put_chunks(grads, keep, send, place, expert, order):
    count = len(order)
    size = grads.shape[0] // count
    for c in range(count):
        place[c ^ expert] = grads[c * size : (c + 1) * size, :]
    for i, k in enumerate(order):
        out = keep if i < count // 2 else send
        at = (i % (count // 2)) * size
        out[at : at + size, :] = place[k]


def residual_back_kernel(
    meta, r0, r1, r2, r3, residual, gate, probs, route, params, cotangent, mixed, w_attn_out,
    attn_probs, normed_one, _, d_attn_cols_out, d_mixed_out, d_value_out, router_grad_out,
    gain_grad_out, first_out, second_out, place, place_f32, chunk_place, *, chunked,
):
    rank, expert = meta[0], meta[1]
    experts = probs.shape[1]
    feats = residual.shape[1]
    cols = feats // 4
    length = residual.shape[0]
    router = params[:experts, :]
    gain = params[experts : experts + 1, :]
    for j, r in enumerate((r0, r1, r2, r3)):
        place[rank ^ j] = r[:cols, :]
    d_gate = as_column(r0[cols : cols + 1, :].astype(F32))
    d_routed = jnp.concatenate([place[r] for r in range(4)], axis=0).astype(F32).T
    res = residual[...]
    scale = row_scale(res)
    lanes = lax.broadcasted_iota(jnp.int32, probs.shape, 1)
    onehot = jnp.where(lanes == as_column(route[...].reshape(1, length)), 1.0, 0.0)
    d_logits = d_gate * probs[...] * (onehot - gate[...])
    d_normed = d_routed + dot_nn(d_logits, router, PRECISE)
    normed = res * scale * gain
    router_grad = dot_tn(d_logits, normed, PRECISE)
    gain_grad = jnp.sum(d_normed * res * scale, axis=0, keepdims=True)
    cross = jnp.sum(gain * res * d_normed, axis=1, keepdims=True)
    d_residual = (
        cotangent[...].astype(F32).T
        + scale * gain * d_normed
        - res * (scale * scale * scale * cross * (1.0 / feats))
    )
    for r in range(4):
        own = slice(r * cols, (r + 1) * cols)
        place_f32[r] = d_residual[:, own]

        @pl.when(rank == r)
        def _():
            router_grad_out[...] = router_grad[:, own]
            gain_grad_out[...] = gain_grad[:, own]

    d_attn_cols_out[...] = place_f32[rank]
    d_attn = d_residual.astype(BF16)
    attn_grad = dot_nn(mixed[...], d_attn).astype(BF16)
    d_mixed = dot_nt(d_attn, w_attn_out[...]).astype(BF16)
    d_mixed_out[...] = d_mixed
    for h in range(cols // HDIM):
        own = slice(h * HDIM, (h + 1) * HDIM)
        total = jnp.zeros((length, HDIM), F32)
        for c in range(0, length, CHUNK):
            span = slice(c, c + CHUNK)
            total = total + dot_tn(attn_probs[h, span, :], d_mixed[span, own])
        d_value_out[:, own] = total.astype(BF16)
    value_grad = dot_tn(d_value_out[...], normed_one[...]).astype(BF16)
    if chunked:
        both = jnp.concatenate([attn_grad, value_grad], axis=0)
        put_chunks(both, first_out, second_out, chunk_place, expert, chunked)
    else:
        first_out[...] = attn_grad
        second_out[...] = value_grad


def attend_back_kernel(
    query, key, value, probs, d_mixed, bucket, d_query, d_key, table_out, *, buckets
):
    length = query.shape[0]
    width = 2 * length
    heads = query.shape[1] // HDIM
    marks = bucket_marks(bucket, buckets)
    zeros = jnp.zeros((8, width - length), F32)
    table_out[...] = jnp.zeros(table_out.shape, F32)
    for h in range(heads):
        own = slice(h * HDIM, (h + 1) * HDIM)
        dk = jnp.zeros((length, HDIM), F32)
        diagonals = jnp.zeros((8, width), F32)
        for c in range(0, length, CHUNK):
            span = slice(c, c + CHUNK)
            weights = probs[h, span, :].astype(F32)
            d_probs = dot_nt(d_mixed[span, own], value[:, own])
            inner = jnp.sum(d_probs * weights, axis=1, keepdims=True)
            d_scores = weights * (d_probs - inner)
            for b in range(CHUNK // 8):
                piece = jnp.concatenate([d_scores[8 * b : 8 * b + 8, :], zeros], axis=1)
                diagonals = diagonals + pltpu.roll(piece, (length - 1 - c - 8 * b) % width, 1)
            low = d_scores.astype(BF16)
            d_query[span, own] = (dot_nn(low, key[:, own]) * SCORE_SCALE).astype(BF16)
            dk = dk + dot_tn(low, query[span, own])
        d_key[:, own] = (dk * SCORE_SCALE).astype(BF16)
        line = diagonals[0:1]
        for r in range(1, 8):
            line = line + pltpu.roll(diagonals[r : r + 1], width - r, 1)
        table_col = jnp.sum(jnp.where(marks, line, 0.0), axis=1, keepdims=True)
        table_out[h : h + 1, :buckets] = jnp.broadcast_to(table_col, (buckets, 128)).T[0:1, :]


def put_split(out, at, row, value):
    high = value.astype(BF16).astype(F32)
    out[row : row + 1, at : at + value.shape[1]] = high
    out[row + 8 : row + 9, at : at + value.shape[1]] = value - high


def query_back_kernel(
    meta, tokens, gain, normed, d_query, d_key, d_value, w_query, w_key, w_value, gain2_grad,
    table_grad, router_grad, _, _got, *rest, chunked, heads, buckets,
):
    keep_in, send_in, gain1_out, first_out, second_out, place, chunk_place, pack = rest
    rank, expert = meta[0], meta[1]
    length, feats = tokens.shape
    cols = feats // 4
    normed_rows = normed[...]
    query_grad = dot_tn(d_query[...], normed_rows).astype(BF16)
    key_grad = dot_tn(d_key[...], normed_rows).astype(BF16)
    d_normed = (
        dot_nn(d_query[...], w_query[...])
        + dot_nn(d_key[...], w_key[...])
        + dot_nn(d_value[...], w_value[...])
    )
    rows = tokens[...].astype(F32)
    product = d_normed * rows
    gain1_grad = jnp.sum(product * row_scale(rows), axis=0, keepdims=True)
    gain1_out[...] = jnp.broadcast_to(gain1_grad, gain1_out.shape)
    if chunked:
        pack[...] = jnp.zeros(pack.shape, F32)
        put_split(pack, 0, 0, gain1_grad)
        put_split(pack, 0, 1, gain2_grad[...])
        for h in range(heads):
            put_split(pack, 256 * h, 2, table_grad[h : h + 1, :])
        for e in range(router_grad.shape[0]):
            put_split(pack, 256 * (e % 3), 3 + e // 3, router_grad[e : e + 1, :])
        small = pack[...].astype(BF16)
        both = jnp.concatenate([query_grad, key_grad], axis=0)
        put_chunks(both, first_out, second_out, chunk_place, expert, chunked)
        for out in (first_out, second_out):
            out[out.shape[0] - 16 :, :] = small
    else:
        first_out[...] = query_grad
        second_out[...] = key_grad
    cross = jnp.sum(product * gain[...].reshape(1, feats), axis=1, keepdims=True)
    high = cross.astype(BF16).astype(F32)
    low = cross - high
    lanes = lax.broadcasted_iota(jnp.int32, (length, place.shape[2] - cols), 1)
    extra = jnp.where(lanes == 0, high, jnp.where(lanes == 1, low, 0.0)).astype(BF16)
    for r in range(4):
        j = rank ^ r
        own = d_normed[:, r * cols : (r + 1) * cols].astype(BF16)
        place[(j % 2) * 2 + j // 2] = jnp.concatenate([own, extra], axis=1)
    keep_in[...] = place[0:2]
    send_in[...] = place[2:4]


def input_kernel(
    meta, tokens, gain, d_attn_cols, first, second, *rest
):
    *_, out, place, gain_place = rest
    rank = meta[0]
    feats = tokens.shape[1]
    cols = feats // 4
    rows = tokens[...].astype(F32)
    scale = row_scale(rows)
    both = first[...].astype(F32) + second[...].astype(F32)
    cross = both[:, cols : cols + 1] + both[:, cols + 1 : cols + 2]
    gain_row = gain[...].reshape(1, feats)
    for r in range(4):
        place[r] = rows[:, r * cols : (r + 1) * cols]
        gain_place[r] = gain_row[:, r * cols : (r + 1) * cols]
    own = both[:, :cols]
    own_rows = place[rank]
    out[...] = (
        d_attn_cols[...]
        + scale * gain_place[rank] * own
        - own_rows * (scale * scale * scale * cross * (1.0 / feats))
    )


def add_small(a, b):
    at = a.shape[0] - 16
    total = (
        a[at : at + 8, :].astype(F32)
        + b[at : at + 8, :].astype(F32)
        + a[at + 8 :, :].astype(F32)
        + b[at + 8 :, :].astype(F32)
    )
    high = total.astype(BF16).astype(F32)
    return total, jnp.concatenate([high, total - high], axis=0).astype(BF16)


def sum_kernel(keep, got, keep_out, send_out, token_out):
    token_out[...] = jnp.zeros(token_out.shape, F32)
    half = (keep.shape[0] - 16) // 2
    total = (keep[: 2 * half, :].astype(F32) + got[: 2 * half, :].astype(F32)).astype(BF16)
    _, small = add_small(keep, got)
    keep_out[:half, :] = total[:half]
    send_out[:half, :] = total[half:]
    keep_out[half:, :] = small
    send_out[half:, :] = small


def last_sum_kernel(keep, got, mine_out, small_out, gain1_out):
    size = mine_out.shape[0]
    mine_out[...] = (keep[:size, :].astype(F32) + got[:size, :].astype(F32)).astype(BF16)
    total, _ = add_small(keep, got)
    small_out[...] = total
    gain1_out[...] = jnp.broadcast_to(total[0:1], gain1_out.shape)


def spread_kernel(
    meta, mine, second, third, fourth, first_out, second_out, token_out, place, *, order
):
    expert = meta[1]
    count = len(order)
    size = mine.shape[0] // 2
    quarter = count // 4
    token_out[...] = jnp.zeros(token_out.shape, F32)
    for i in range(count):
        block = (mine, second, third, fourth)[i // quarter]
        at = i % quarter
        place[order[i]] = block[at * size : (at + 1) * size, :]
    rows = first_out.shape[0]
    for c in range(count):
        chunk = place[c ^ expert].astype(F32)
        start = c * size
        if start < rows:
            first_out[start : start + size, :] = chunk
        else:
            second_out[start - rows : start - rows + size, :] = chunk


def finish_kernel(
    meta, mine, second, third, fourth, small, *rest, order, heads
):
    first_out, second_out, token_out, gain2_out, table_out, router_out, place = rest[-7:]
    blocks = (mine, second, third, fourth)
    spread_kernel(meta, *blocks, first_out, second_out, token_out, place, order=order)
    cols = gain2_out.shape[1]
    gain2_out[...] = small[1:2, :cols]
    for h in range(heads):
        table_out[h : h + 1, :] = small[2:3, 256 * h : 256 * h + table_out.shape[1]]
    for e in range(router_out.shape[0]):
        at = 256 * (e % 3)
        router_out[e : e + 1, :] = small[3 + e // 3 : 4 + e // 3, at : at + cols]


def moving(kernel, smem, fetch, total, far):
    def run(*refs):
        rest = list(refs[: len(refs) - 1])
        sems = refs[-1]
        near_out = rest[len(rest) - len(far) :] if far else []
        rest = rest[: len(rest) - len(far)]
        near_in = rest[len(rest) - fetch :] if fetch else []
        rest = rest[: len(rest) - fetch]
        copies = [
            pltpu.make_async_copy(rest[smem + i], b, sems.at[i]) for i, b in enumerate(near_in)
        ]
        for copy in copies:
            copy.start()
        for copy in copies:
            copy.wait()
        inner = list(rest)
        for i, b in enumerate(near_in):
            inner[smem + i] = b
        for b, at in zip(near_out, far):
            inner[total + at] = b
        kernel(*inner)
        copies = [
            pltpu.make_async_copy(b, rest[total + at], sems.at[fetch + i])
            for i, (b, at) in enumerate(zip(near_out, far))
        ]
        for copy in copies:
            copy.start()
        for copy in copies:
            copy.wait()

    return run


def call(kernel, outs, scratch, *operands, weight=1.0, smem=1, fetch=0, far=(), after=()):
    specs, given = [], []
    for i, operand in enumerate(operands):
        if i < smem:
            specs.append(pl.BlockSpec(memory_space=pltpu.SMEM))
        elif i < smem + fetch:
            specs.append(pl.BlockSpec(memory_space=pltpu.HBM))
            operand = pltpu.with_memory_space_constraint(operand, pltpu.HBM)
        else:
            specs.append(pl.BlockSpec(memory_space=pltpu.VMEM))
        given.append(operand)
    specs += [pl.BlockSpec(memory_space=pl.ANY)] * len(after)
    scratch_shapes = [pltpu.VMEM(shape, kind) for shape, kind in scratch]
    shapes, out_specs = [], []
    for i, (shape, kind) in enumerate(outs):
        shapes.append(pltpu.HBM(shape, kind) if i in far else jax.ShapeDtypeStruct(shape, kind))
        out_specs.append(pl.BlockSpec(memory_space=pltpu.HBM if i in far else pltpu.VMEM))
    if fetch or far:
        kernel = moving(kernel, smem, fetch, len(operands) + len(after), far)
        scratch_shapes += [pltpu.VMEM(a.shape, a.dtype) for a in operands[smem : smem + fetch]]
        scratch_shapes += [pltpu.VMEM(*outs[i]) for i in far]
        scratch_shapes.append(pltpu.SemaphoreType.DMA((fetch + len(far),)))
    return pl.pallas_call(
        kernel,
        out_shape=shapes,
        in_specs=specs,
        out_specs=out_specs,
        scratch_shapes=scratch_shapes,
        compiler_params=pltpu.CompilerParams(vmem_limit_bytes=32 * 1024 * 1024),
        cost_estimate=pl.CostEstimate(
            flops=int(weight * 1.1e9), bytes_accessed=1 << 16, transcendentals=0
        ),
    )(*given, *after)


def swap(array, axis, bit):
    size = lax.axis_size(axis)
    return lax.ppermute(array, axis, [(i, i ^ bit) for i in range(size)])


def add_low(a, b):
    return (a.astype(F32) + b.astype(F32)).astype(BF16)


def gather_four(array):
    across = swap(array, "tensor", 2)
    beside = swap(array, "tensor", 1)
    return [array, beside, across, swap(across, "tensor", 1)]


def reduce_four(keep, send):
    got = swap(send, "tensor", 1)
    far = add_low(keep[1], got[1])
    return add_low(keep[0], got[0]), swap(far, "tensor", 2), far


def exchange(blocks):
    if len(blocks) > 8:
        return hyper_exchange(blocks)[0]
    return [blocks[0]] + [swap(b, "expert", k) for k, b in enumerate(blocks) if k]


def hyper_exchange(blocks, gates=None):
    count = len(blocks)
    held = {k: [b] for k, b in enumerate(blocks)}
    steps = []
    bit = 1
    while bit < count:
        away = [k for k in sorted(held) if k & bit]
        sent = jnp.concatenate([b for k in away for b in held[k]], axis=0)
        if gates and bit in gates:
            (sent,) = fence([sent], gates[bit])
        got = swap(sent, "expert", bit)
        if gates and -bit in gates:
            (got,) = fence([got], gates[-bit])
        steps.append(got)
        size = blocks[0].shape[0]
        at = 0
        fresh = {}
        for k in away:
            pieces = [got[at + i * size : at + (i + 1) * size] for i in range(len(held[k]))]
            at += len(held[k]) * size
            fresh[k ^ bit] = held[k ^ bit] + pieces
        held = fresh
        bit *= 2
    return held[0], steps


ORDER = (0, 4, 2, 6, 1, 5, 3, 7)


def gather_chunks(mine, gates=None):
    held = swap(mine, "expert", 4)
    if gates:
        (held,) = fence([held], (gates[0],))
    held = jnp.concatenate([mine, held], axis=0)
    beside = swap(held, "expert", 2)
    if gates:
        (beside,) = fence([beside], (gates[1],))
    return held, beside, swap(held, "expert", 1), swap(beside, "expert", 1)


def halve_plain(keep, got, gates):
    for bit, gate in zip((2, 4), gates):
        half = keep.shape[0] // 2
        sent = add_low(keep[half:], got[half:])
        keep = add_low(keep[:half], got[:half])
        (got,) = fence([swap(sent, "expert", bit)], (gate,))
    return add_low(keep, got)


def halve(keep, send):
    feats = keep.shape[1]
    steps = []
    for bit in (1, 2):
        rows = (keep.shape[0] - 16) // 2 + 16
        keep, send, token = call(
            sum_kernel, [((rows, feats), BF16)] * 2 + [((8, 128), F32)], [], keep, swap(send, "expert", bit), smem=0
        )
        steps.append(token)
    last = call(
        last_sum_kernel,
        [((keep.shape[0] - 16, feats), BF16), ((8, feats), F32), ((8, feats), F32)],
        [],
        keep, swap(send, "expert", 4), smem=0,
    )
    return last, steps


def fence(arrays, after):
    count = len(arrays)
    return pl.pallas_call(
        fence_kernel,
        out_shape=[jax.ShapeDtypeStruct(a.shape, a.dtype) for a in arrays],
        in_specs=[pl.BlockSpec(memory_space=pl.ANY)] * (count + len(after)),
        out_specs=[pl.BlockSpec(memory_space=pl.ANY)] * count,
        input_output_aliases={i: i for i in range(count)},
    )(*arrays, *after)


def on_device(
    tokens, cotangent, norm1_gain, w_query, w_key, w_value, w_attn_out, bias_table, norm2_gain,
    w_router, expert_in, expert_out, route, slot, segment, rel_bucket,
):
    length, feats = tokens.shape
    cols = cotangent.shape[1]
    heads = cols // HDIM
    experts = lax.axis_size("expert")
    cap = 2 * length // experts
    share = cap // 4
    rank = lax.axis_index("tensor").astype(jnp.int32)
    expert = lax.axis_index("expert").astype(jnp.int32)
    meta = jnp.stack([rank, expert])
    total = experts * cap
    direct = share % 16 == 0
    buckets = bias_table.shape[0]
    chunked = ORDER if experts == len(ORDER) else None

    w_query_t, w_key_t, w_value_t = w_query.T, w_key.T, w_value.T
    packed_rows = cols + -(-(experts + 3) // 16) * 16
    packed, cot_own, *cot_blocks = call(
        first_kernel,
        [((packed_rows, feats), BF16), ((length // cap * cols, cap), BF16)] + [((cols, cap), BF16)] * experts,
        [],
        meta, route, slot, cotangent.T, w_attn_out, w_router.T, norm2_gain,
        weight=2.0, fetch=6,
    )
    packed_parts = gather_four(packed)
    bucket = jnp.concatenate([rel_bucket, jnp.full((1,), -1, jnp.int32)])
    normed, query, key, value, probs, mixed, mixed_token = call(
        attend_kernel,
        [((length, feats), BF16)]
        + [((length, cols), BF16)] * 3
        + [((heads, length, length), BF16), ((cols, length), BF16), ((8, 128), F32)],
        [((length, length), F32)],
        tokens, w_query.T, w_key.T, w_value.T, norm1_gain, segment, bucket, bias_table.T,
        weight=7.0, smem=0, fetch=8, far=(0, 1, 2, 3, 4),
    )

    mixed_parts = gather_four(mixed)
    residual, gate, router_probs, params, *row_blocks = call(
        residual_kernel,
        [
            ((length, feats), F32),
            ((length, 1), F32),
            ((length, experts), F32),
            ((experts + 8, feats), F32),
        ]
        + [((share, feats), BF16)] * experts,
        [((4, packed_rows - cols, cols), F32)],
        meta, route, slot, tokens, *mixed_parts, *packed_parts,
        weight=5.8, fetch=3, far=(0, 1, 2),
    )
    cot_arrived, _ = hyper_exchange(
        cot_blocks, {2: (mixed_token,), -4: (residual,)}
    )
    if direct:
        cot_arrived = cot_arrived + [cot_own]
    else:
        cot_turned = lax.all_gather(cotangent.T, "tensor", axis=0, tiled=True)
    cot_rows = gather_four(jnp.concatenate(cot_arrived, axis=0))
    arrived = exchange(row_blocks)
    groups = GROUPS if direct else 1
    group_size = experts // groups
    row_groups = []
    for g in range(groups):
        blocks = arrived[g * group_size : (g + 1) * group_size]
        if direct:
            (packed,) = call(
                functools.partial(assemble_kernel, count=group_size),
                [((group_size * share, feats), BF16)],
                [],
                *blocks,
                weight=1.0, smem=0, after=(cot_rows[2],),
            )
        else:
            packed = jnp.concatenate(blocks, axis=0)
        row_groups.append(gather_four(packed))

    if not direct:
        def assemble(parts, shape, turn):
            stacked = jnp.stack(parts).reshape(4, experts, *shape)
            stacked = stacked[rank ^ jnp.arange(4, dtype=jnp.int32)]
            return [jnp.transpose(stacked, turn).reshape(total, feats)]

        one = jnp.zeros((16, 128), BF16)
        row_groups = [assemble(row_groups[0], (share, feats), (1, 0, 2, 3)) + [one] * 3]
        cot_rows = assemble(cot_rows, (cols, cap), (1, 3, 0, 2)) + [one] * 3
    w_in, w_out = expert_in[0], expert_out[0]
    hidden_count = w_in.shape[1]
    part_rows = cols + 16
    count = total // groups
    x_shape = (group_size, 4, share, feats) if direct else (1, 1, 16, 128)
    c_shape = (4, cols, count) if direct else (1, 16, 128)
    acts, returning, kept = [], [], []
    for g in range(groups):
        rows_all, act, cots, d_hidden, keep, send, turned = call(
            functools.partial(expert_kernel, first=g * group_size, direct=direct),
            [((count, feats), BF16), ((count, hidden_count), BF16), ((count, feats), BF16),
             ((count, hidden_count), BF16), ((2, part_rows, count), BF16),
             ((2, part_rows, count), BF16), ((4, cols, length) if direct else (1, 16, 128), BF16)],
            [(x_shape, BF16), (c_shape, BF16), ((4, part_rows, count), BF16)],
            meta, *row_groups[g], *cot_rows, w_in, w_out, params[:experts],
            weight=10.0, far=(0, 1, 2, 3, 6) if direct else (),
        )
        if direct:
            cot_turned = turned.reshape(feats, length)
        near, far, met = reduce_four(keep, send)
        whole = add_low(near, far)
        returning += [whole[:, k * cap : (k + 1) * cap] for k in range(group_size)]
        acts.append(act)
        kept += [act, cots, rows_all, d_hidden]

    kept = fence(kept, (met,))
    expert_out_grad = sum(dot_tn(kept[4 * g], kept[4 * g + 1]) for g in range(groups))
    expert_in_grad = sum(dot_tn(kept[4 * g + 2], kept[4 * g + 3]) for g in range(groups))

    def unite(blocks):
        return blocks if cap % 128 == 0 else [jnp.concatenate(blocks, axis=1)]

    keep_fwd, send_fwd = call(
        functools.partial(expert_out_kernel, groups=groups),
        [((2, cols, total), BF16)] * 2,
        [((4, cols, total), BF16)],
        meta, w_out, *[kept[4 * g] for g in range(groups)],
        weight=2.9, after=(whole, expert_out_grad, expert_in_grad),
    )
    (d_routed,) = call(
        functools.partial(combine_kernel, cap=cap),
        [((part_rows, length), BF16)],
        [((part_rows, total), BF16)],
        meta, route, slot, *unite(exchange(returning)), after=(keep_fwd,),
        weight=1.0,
    )
    routed_parts = gather_four(d_routed)

    near_fwd, far_fwd, met_fwd = reduce_four(keep_fwd, send_fwd)
    whole_fwd = add_low(near_fwd, far_fwd)
    fwd_arrived, fwd_steps = hyper_exchange(
        [whole_fwd[:, k * cap : (k + 1) * cap] for k in range(experts)]
    )
    came_fwd = unite(fwd_arrived)
    (block_out,) = call(
        functools.partial(block_out_kernel, cap=cap),
        [((length, cols), BF16)],
        [((cols, total), BF16), ((4, length, cols), F32)],
        meta, route, slot, residual, gate, *came_fwd,
        weight=1.2,
    )

    if chunked:
        size = 2 * cols // experts
        grad_outs = [((experts // 2 * size + 16, feats), BF16)] * 2
        chunk_scratch = ((experts, size, feats), BF16)
    else:
        grad_outs = [((cols, feats), BF16)] * 2
        chunk_scratch = ((16, 128), BF16)
    d_attn_cols, d_mixed, d_value, router_grad, gain2_grad, *first_grads = call(
        functools.partial(residual_back_kernel, chunked=chunked),
        [((length, cols), F32), ((length, cols), BF16), ((length, cols), BF16),
         ((experts, cols), F32), ((1, cols), F32)]
        + [((cols, feats), BF16)] * 2,
        [((4, cols, length), BF16), ((4, length, cols), F32), chunk_scratch],
        meta, *routed_parts, residual, gate, router_probs, route, params, cot_turned, mixed,
        w_attn_out, probs, normed, after=(met_fwd,),
        weight=8.0, far=(0,),
    )
    d_query, d_key, table_grad = call(
        functools.partial(attend_back_kernel, buckets=buckets),
        [((length, cols), BF16)] * 2 + [((8, 128), F32)],
        [],
        query, key, value, probs, d_mixed, bucket, smem=0,
        weight=7.0,
    )
    wide = -(-(cols + 2) // 128) * 128
    first_got = swap(first_grads[1], "expert", 1) if chunked else d_query
    keep_in, send_in, gain1_grad, *second_grads = call(
        functools.partial(query_back_kernel, chunked=chunked, heads=heads, buckets=buckets),
        [((2, length, wide), BF16)] * 2 + [((8, feats), F32)] + grad_outs,
        [((4, length, wide), BF16), chunk_scratch, ((16, feats), F32)],
        meta, tokens, norm1_gain, normed, d_query, d_key, d_value, w_query_t, w_key_t,
        w_value_t, gain2_grad, table_grad, router_grad, after=(whole_fwd, first_got),
        weight=4.0,
    )
    near_in, far_in, _ = reduce_four(keep_in, send_in)
    (input_grad,) = call(
        input_kernel,
        [((length, cols), F32)],
        [((4, length, cols), F32), ((4, 1, cols), F32)],
        meta, tokens, norm1_gain, d_attn_cols, near_in, far_in,
        weight=1.0,
    )

    if chunked:
        (mine, small, gain1_grad), steps = halve(*second_grads)
        second_chunks = gather_chunks(mine)
        attn_grad, value_grad, spread_token = call(
            functools.partial(spread_kernel, order=ORDER),
            [((cols, feats), F32)] * 2 + [((8, 128), F32)],
            [chunk_scratch],
            meta,
            *gather_chunks(
                halve_plain(
                    first_grads[0], *fence([first_got], (fwd_steps[0][:16, :128],)), steps
                ),
                (small, second_chunks[0][:16, :128]),
            ),
            weight=1.6,
        )
        for bit in (1, 2):
            gain1_grad = gain1_grad + swap(gain1_grad, "tensor", bit)
        query_grad, key_grad, _, gain2_grad, table_grad, router_grad = call(
            functools.partial(finish_kernel, order=ORDER, heads=heads),
            [((cols, feats), F32)] * 2
            + [((8, 128), F32), ((1, cols), F32), ((heads, buckets), F32), ((experts, cols), F32)],
            [chunk_scratch],
            meta, *second_chunks, small,
            weight=1.6, after=(input_grad, block_out, gain1_grad, spread_token),
        )
    else:
        query_grad, key_grad, gain2_grad, table_grad, router_grad = lax.psum(
            (*second_grads, gain2_grad, table_grad[:heads, :buckets], router_grad), "expert"
        )
        gain1_grad = lax.psum(gain1_grad, ("expert", "tensor"))
        attn_grad, value_grad = lax.psum(tuple(first_grads), "expert")
    return (
        block_out,
        input_grad,
        gain1_grad[0],
        query_grad.astype(F32).T,
        key_grad.astype(F32).T,
        value_grad.astype(F32).T,
        attn_grad.astype(F32),
        table_grad.T,
        gain2_grad[0],
        router_grad.T,
        expert_in_grad[None],
        expert_out_grad[None],
    )


def solution(mesh):
    return jax.shard_map(
        on_device,
        mesh=mesh,
        in_specs=(
            P("expert", None),
            P("expert", "tensor"),
            P(),
            P(None, "tensor"),
            P(None, "tensor"),
            P(None, "tensor"),
            P("tensor", None),
            P(None, "tensor"),
            P("tensor"),
            P("tensor", None),
            P("expert", None, "tensor"),
            P("expert", "tensor", None),
            P("expert"),
            P("expert"),
            P("expert"),
            P(),
        ),
        out_specs=(
            P("expert", "tensor"),
            P("expert", "tensor"),
            P(),
            P(None, "tensor"),
            P(None, "tensor"),
            P(None, "tensor"),
            P("tensor", None),
            P(None, "tensor"),
            P("tensor"),
            P("tensor", None),
            P("expert", None, "tensor"),
            P("expert", "tensor", None),
        ),
        check_vma=False,
    )
```
